32 devices in a mesh: grp: 2 (over x), tile: 16 (over z, y, core).
Axes of the slice: x: 2, y: 2, z: 4, core: 2. Of those that a mesh axis runs over, the one named last changes fastest.
Arguments:
- cotangent: bfloat16 [512, 48, 128], P(('grp', 'tile')), parts along dimension 0, may hold values from -6 to 6
- remap_weight: bfloat16 [2048, 128, 128], P('tile'), may hold values from -0.5 to 0.5
- target_block: int32 [16, 128], P('tile'), may hold values from 0 to 17, as said below
- dest_device: int32 [16, 128], P('tile'), may hold values from 0 to 15, as said below
- source_block: int32 [16, 128], P('tile'), may hold values from 0 to 15
- send_count: int32 [16], P('tile'), may hold values from 32 to 128, as said below
- lev_index: int32 [8], replicated, may hold values from 0 to 18
- lev_frac: float32 [8], replicated, may hold values from 0 to 1
Outputs:
- source_grad: float32 [512, 120, 128], P(('grp', 'tile')), parts along dimension 0
The draws below stay inside these ranges and needn't reach their ends.
There are 2 independent parts, one for each index of `grp`. The reference program is written for one: setup_inputs(seed, part) draws one part's arguments, and reference() takes and returns one part's arrays. A program takes and returns all parts, laid end to end along the dimension named above; an argument that names none is the same for every part. Nothing has to cross between parts.
Inputs may be any that keep to these rules, and one draw needn't show every extreme that they name: `target_block`: 0 names the previous device's last block (cyclic), 1 to 16 the device's own blocks, 17 the next device's first block; entry 0 of every device names 0 and entry 1 names 17. `dest_device`: among the first send_count entries of a device each destination appears at most 16 times, and some device names some destination exactly 16 times; later entries are ignored. `send_count`: some device has 128 live entries.
All inputs are finite; a program needn't handle non-finite values.
Results may differ from the reference program's by a relative error of at most 0.0003.
Values may be sent and summed in bfloat16 or wider, within the bound.
No kernel may reach another device: no remote copies, remote signals or barrier semaphores. Data moves between devices by JAX's collectives and lax.ppermute only.
A program may use at most 128 MiB of HBM per device.

```python
import jax
import jax.numpy as jnp
from jax import lax

VARS = 6
LEV = 20
LEVT = 8
CELLS = 128
TB = 16
SB = 16
O_DEV = 128
CAP = 16
TGT_BLOCKS = 256
N_TILE = 16


def intersection_tables(key):
    keys = jax.random.split(key, 5)
    position = jnp.arange(N_TILE).astype(jnp.int32)
    distance = jnp.minimum(position, N_TILE - 1 - position)
    polar = distance < max(1, N_TILE // 16)
    drawn = jax.random.randint(keys[0], (N_TILE,), O_DEV // 4, O_DEV // 2 + 1)
    counts = jnp.where(polar, O_DEV, drawn).astype(jnp.int32)
    scores = jax.random.randint(keys[1], (N_TILE, N_TILE), 0, N_TILE) * N_TILE + position[None, :]
    destinations = jnp.argsort(scores, axis=1).astype(jnp.int32)
    entries = jnp.arange(O_DEV).astype(jnp.int32)
    grouped = destinations[:, entries // CAP]
    shuffle = jax.random.randint(keys[2], (N_TILE, O_DEV), 0, O_DEV) * O_DEV + entries[None, :]
    shuffle = jnp.where(entries[None, :] < counts[:, None], shuffle, O_DEV * O_DEV + entries[None, :])
    ordering = jnp.argsort(shuffle, axis=1)
    dest = jnp.take_along_axis(grouped, ordering, axis=1).astype(jnp.int32)
    target = jax.random.randint(keys[3], (N_TILE, O_DEV), 0, TB + 2).astype(jnp.int32)
    target = target.at[:, 0].set(0).at[:, 1].set(TB + 1).astype(jnp.int32)
    source = jax.random.randint(keys[4], (N_TILE, O_DEV), 0, SB).astype(jnp.int32)
    return (counts, dest, target, source)


def draw_target_block(key, part):
    return intersection_tables(key)[2]


def draw_dest_device(key, part):
    return intersection_tables(key)[1]


def draw_source_block(key, part):
    return intersection_tables(key)[3]


def draw_send_count(key, part):
    return intersection_tables(key)[0]


def set_ends(array, stream_key, least, high):
    shape = array.shape
    index_at = [jax.random.randint(jax.random.fold_in(stream_key, axis), (), 0, shape[axis]) for axis in range(len(shape))]
    array = array.at[tuple(index_at)].set(least)
    longest = shape.index(max(shape))
    index_at[longest] = (index_at[longest] + 1) % shape[longest]
    return array.at[tuple(index_at)].set(high)


def steps_of(rng, dims, cuts, low, high):
    def one(dim, shards_of):
        heights = jax.random.uniform(jax.random.fold_in(jax.random.fold_in(rng, 6), dim), (shards_of,), jnp.float32, low / len(cuts), high / len(cuts))
        return jnp.repeat(jnp.exp(heights), dims[dim] // shards_of).reshape((-1,) + (1,) * (len(dims) - dim - 1))

    factor_of = one(*cuts[0])
    for cut in cuts[1:]:
        factor_of = factor_of * one(*cut)
    return factor_of


def normal_values(own_key, extent, spread, most, pieces=(), held_as=jnp.bfloat16):
    loudness = steps_of(own_key, extent, pieces, -0.22, 0.18) if pieces else 1.0
    array = jax.random.normal(own_key, extent, jnp.float32) * spread * loudness
    return jnp.minimum(jnp.maximum(array, -most), most).astype(held_as)


def setup_inputs(seed: int = 0, part: int = 0) -> dict:
    streams_of = jax.random.split(jax.random.key(seed), 9)
    part_keys = jax.random.split(jax.random.fold_in(streams_of[8], part), 9)
    cotangent = normal_values(part_keys[0], (TGT_BLOCKS, VARS * LEVT, CELLS), 1.0, 6.0, ((0, 16),))
    remap_weight = normal_values(streams_of[1], (N_TILE * O_DEV, CELLS, CELLS), CELLS ** -0.5, 0.5, ((0, 16),))
    target_block = draw_target_block(jax.random.fold_in(streams_of[8], 71), part)
    dest_device = draw_dest_device(jax.random.fold_in(streams_of[8], 71), part)
    source_block = draw_source_block(jax.random.fold_in(streams_of[8], 71), part)
    send_count = draw_send_count(jax.random.fold_in(streams_of[8], 71), part)
    lev_index = set_ends(jax.random.randint(streams_of[6], (LEVT,), 0, LEV - 1), jax.random.fold_in(streams_of[6], 1), 0, (LEV - 1) - 1).astype(jnp.int32)
    lev_frac = jnp.clip(jax.random.uniform(streams_of[7], (LEVT,), jnp.float32, 0.0, 1.0), 0.0, 1.0)
    return dict(cotangent=cotangent, remap_weight=remap_weight, target_block=target_block, dest_device=dest_device, source_block=source_block, send_count=send_count, lev_index=lev_index, lev_frac=lev_frac)


def vertical_matrix(lev_index, lev_frac, levels):
    columns = jnp.arange(levels).astype(jnp.int32)[None, :]
    lower = (columns == lev_index[:, None]).astype(jnp.float32)
    upper = (columns == lev_index[:, None] + 1).astype(jnp.float32)
    return (1.0 - lev_frac)[:, None] * lower + lev_frac[:, None] * upper


def reference(cotangent, remap_weight, target_block, dest_device, source_block, send_count, lev_index, lev_frac):
    tile_count = target_block.shape[0]
    intersection_count = target_block.shape[1]
    tgt_total = cotangent.shape[0]
    per_device = tgt_total // tile_count
    lift_matrix = vertical_matrix(lev_index, lev_frac, LEV).astype(jnp.float32)
    weights = remap_weight.reshape(tile_count, intersection_count, CELLS, CELLS)
    totals_init = jnp.zeros((SB * tile_count, VARS * LEV, CELLS), jnp.float32)

    def add_sender(totals, sender):
        window_rows = (sender * per_device + target_block[sender] - 1) % tgt_total
        picked = cotangent[window_rows.astype(jnp.int32)].astype(jnp.float32)
        contrib = jnp.einsum("ofp,ops->ofs", picked, weights[sender].astype(jnp.float32), precision=lax.Precision.HIGHEST)
        shaped = contrib.reshape(intersection_count, VARS, LEVT, CELLS)
        lifted = jnp.einsum("jl,ovjs->ovls", lift_matrix, shaped, precision=lax.Precision.HIGHEST)
        lifted = lifted.reshape(intersection_count, VARS * LEV, CELLS)
        usable = (jnp.arange(intersection_count).astype(jnp.int32) < send_count[sender]).astype(jnp.float32)
        lifted = lifted * usable[:, None, None]
        placement = (dest_device[sender] * SB + source_block[sender]).astype(jnp.int32)
        return totals.at[placement].add(lifted), None

    totals, unused = lax.scan(add_sender, totals_init, jnp.arange(tile_count).astype(jnp.int32))
    return totals
```

```python
import functools

import jax
import jax.numpy as jnp
from jax import lax
from jax.experimental import pallas as pl
from jax.experimental.pallas import tpu as pltpu
from jax.sharding import PartitionSpec as P

VARS = 6
LEV = 20
LEVT = 8
SB = 16
ROWS = VARS * LEVT
BODY = SB * ROWS
CODED = BODY + SB
GROUP = 16
MIB = 1 << 20


def encode(read, write, exps):
    for b in range(SB):
        x = read(b)
        top = jnp.max(jnp.abs(x), axis=0, keepdims=True)
        e = jnp.ceil(jnp.log2(jnp.maximum(top, 1e-30)) + 0.001) - 15.0
        exps[b : b + 1, :] = e
        q = jnp.round(x * jnp.exp2(-e))
        write(b * ROWS, ROWS, q.astype(jnp.int32).astype(jnp.int16))
    write(BODY, SB, exps[...].astype(jnp.int32).astype(jnp.int16))


def scales(ref):
    return jnp.exp2(ref[0, BODY:CODED, :].astype(jnp.int32).astype(jnp.float32))


def decode(ref, scale, b):
    q = ref[0, b * ROWS : (b + 1) * ROWS, :].astype(jnp.int32).astype(jnp.float32)
    return q * scale[b : b + 1, :]


def products_kernel(
    tb_ref,
    dest_ref,
    src_ref,
    count_ref,
    me_ref,
    cot_ref,
    before_ref,
    after_ref,
    w_hbm,
    far_hbm,
    near_hbm,
    keep_hbm,
    window,
    w,
    acc,
    coded,
    exps,
    bins,
    w_sems,
    keep_sem,
    out_sems,
):
    entries = w.shape[0]
    groups = entries // GROUP
    count = count_ref[0]
    me = me_ref[0]
    used = (count + GROUP - 1) // GROUP

    def w_copy(g):
        return pltpu.make_async_copy(
            w_hbm.at[pl.ds(g * GROUP, GROUP)], w.at[pl.ds(g * GROUP, GROUP)], w_sems.at[g]
        )

    for g in range(groups):

        @pl.when(g < used)
        def _():
            w_copy(g).start()

    window[0] = before_ref[0]
    window[1:-1] = cot_ref[...]
    window[window.shape[0] - 1] = after_ref[0]

    trash = 2 * 8 * SB

    @pl.loop(0, entries, unroll=4)
    def _(k):
        rel = dest_ref[0, k] ^ me
        slot = (rel & 1) * 8 + ((rel >> 1) & 1) * 4 + (rel >> 2)
        bins[k] = jnp.where(k < count, slot * SB + src_ref[0, k], trash)

    @pl.loop(0, 2 * 8 * SB, unroll=8)
    def _(b):
        acc[b] = jnp.zeros((ROWS, acc.shape[2]), jnp.float32)

    for g in range(groups):

        @pl.when(g < used)
        def _():
            w_copy(g).wait()

            @pl.loop(0, GROUP // 4)
            def _(part):
                first = g * GROUP + part * 4
                found = [
                    jnp.dot(
                        window[tb_ref[0, first + i]],
                        w[first + i],
                        preferred_element_type=jnp.float32,
                    )
                    for i in range(4)
                ]
                for i in range(4):
                    at = bins[first + i]
                    acc[at] = acc[at] + found[i]

    keep = pltpu.make_async_copy(acc.at[pl.ds(0, 8 * SB)], keep_hbm, keep_sem)
    keep.start()

    @pl.loop(0, 8)
    def _(i):
        slot = (i + 4) & 7

        def read(b):
            return acc[(8 + slot) * SB + b]

        def write(row, rows, value):
            coded[slot, row : row + rows, :] = value

        encode(read, write, exps)

        @pl.when(i < 4)
        def _():
            pltpu.make_async_copy(coded.at[slot], far_hbm.at[slot - 4], out_sems.at[i]).start()

        @pl.when(i >= 4)
        def _():
            pltpu.make_async_copy(coded.at[slot], near_hbm.at[slot], out_sems.at[i]).start()

    keep.wait()
    for i in range(8):
        slot = (i + 4) & 7
        target = far_hbm.at[slot - 4] if i < 4 else near_hbm.at[slot]
        pltpu.make_async_copy(coded.at[slot], target, out_sems.at[i]).wait()


def products(tables, me, cotangent, before, after, weight):
    entries, cells_in, cells = weight.shape
    smem = pl.BlockSpec(memory_space=pltpu.SMEM)
    vmem = pl.BlockSpec(memory_space=pltpu.VMEM)
    hbm = pl.BlockSpec(memory_space=pl.ANY)
    coded = jax.ShapeDtypeStruct((4, CODED, cells), jnp.int16)
    return pl.pallas_call(
        products_kernel,
        out_shape=(coded, coded, jax.ShapeDtypeStruct((8 * SB, ROWS, cells), jnp.float32)),
        in_specs=[smem] * 5 + [vmem] * 3 + [hbm],
        out_specs=(hbm, hbm, hbm),
        scratch_shapes=[
            pltpu.VMEM((cotangent.shape[0] + 2, ROWS, cells_in), jnp.bfloat16),
            pltpu.VMEM(weight.shape, jnp.bfloat16),
            pltpu.VMEM((16 * SB + 1, ROWS, cells), jnp.float32),
            pltpu.VMEM((8, CODED, cells), jnp.int16),
            pltpu.VMEM((SB, cells), jnp.float32),
            pltpu.SMEM((entries,), jnp.int32),
            pltpu.SemaphoreType.DMA((entries // GROUP,)),
            pltpu.SemaphoreType.DMA,
            pltpu.SemaphoreType.DMA((8,)),
        ],
        compiler_params=pltpu.CompilerParams(vmem_limit_bytes=32 * MIB),
        cost_estimate=pl.CostEstimate(
            flops=2 * entries * ROWS * cells_in * cells,
            bytes_accessed=12 * MIB,
            transcendentals=0,
        ),
    )(*tables, me, cotangent, before, after, weight)


def sum_and_code_kernel(n_coded, *refs):
    coded_refs, keep_ref, out_ref, exps = refs[:n_coded], refs[n_coded], refs[-2], refs[-1]
    each = [scales(r) for r in coded_refs]

    def read(b):
        total = keep_ref[b]
        for r, s in zip(coded_refs, each):
            total = total + decode(r, s, b)
        return total

    def write(row, rows, value):
        out_ref[0, row : row + rows, :] = value

    encode(read, write, exps)


def sum_and_code(coded, keep, keep_slot):
    cells = keep.shape[2]
    return pl.pallas_call(
        functools.partial(sum_and_code_kernel, len(coded)),
        grid=(1,),
        out_shape=jax.ShapeDtypeStruct((1, CODED, cells), jnp.int16),
        in_specs=[
            pl.BlockSpec((1, CODED, cells), functools.partial(lambda i, g: (i, 0, 0), i))
            for _, i in coded
        ]
        + [pl.BlockSpec((SB, ROWS, cells), lambda g: (keep_slot, 0, 0))],
        out_specs=pl.BlockSpec((1, CODED, cells), lambda g: (0, 0, 0)),
        scratch_shapes=[pltpu.VMEM((SB, cells), jnp.float32)],
        cost_estimate=pl.CostEstimate(
            flops=10 * BODY * cells, bytes_accessed=8 * BODY * cells, transcendentals=0
        ),
    )(*[a for a, _ in coded], keep)


def finish_kernel(n_coded, index_ref, frac_ref, *refs):
    coded_refs, keep_ref, out_ref = refs[:n_coded], refs[n_coded], refs[n_coded + 1]
    high = VARS * LEV
    row = lax.broadcasted_iota(jnp.int32, (high, ROWS), 0)
    col = lax.broadcasted_iota(jnp.int32, (high, ROWS), 1)
    level = row % LEV
    lift = jnp.zeros((high, ROWS), jnp.float32)
    for j in range(LEVT):
        at, frac = index_ref[j], frac_ref[j]
        here = jnp.where(level == at, 1.0 - frac, jnp.where(level == at + 1, frac, 0.0))
        lift = jnp.where(col % LEVT == j, here, lift)
    lift = jnp.where(row // LEV == col // LEVT, lift, 0.0)
    each = [scales(r) for r in coded_refs]
    for b in range(SB):
        total = keep_ref[b]
        for r, s in zip(coded_refs, each):
            total = total + decode(r, s, b)
        out_ref[b] = jnp.dot(
            lift, total, preferred_element_type=jnp.float32, precision=lax.Precision.HIGHEST
        )


def finish(lev_index, lev_frac, coded, keep):
    cells = keep.shape[2]
    smem = pl.BlockSpec(memory_space=pltpu.SMEM)
    return pl.pallas_call(
        functools.partial(finish_kernel, len(coded)),
        grid=(1,),
        out_shape=jax.ShapeDtypeStruct((SB, VARS * LEV, cells), jnp.float32),
        in_specs=[smem, smem]
        + [pl.BlockSpec((1, CODED, cells), lambda g: (0, 0, 0)) for _ in coded]
        + [pl.BlockSpec((SB, ROWS, cells), lambda g: (0, 0, 0))],
        out_specs=pl.BlockSpec((SB, VARS * LEV, cells), lambda g: (0, 0, 0)),
        cost_estimate=pl.CostEstimate(
            flops=10 * BODY * cells, bytes_accessed=16 * BODY * cells, transcendentals=0
        ),
    )(lev_index, lev_frac, *coded, keep)


def ring_ends(cotangent, peers):
    up = [(i, (i + 1) % peers) for i in range(peers)]
    down = [(j, i) for i, j in up]
    return (
        lax.ppermute(cotangent[-1:], "tile", up),
        lax.ppermute(cotangent[:1], "tile", down),
    )


def swap(value, bits, peers):
    return lax.ppermute(value, "tile", [(i, i ^ bits) for i in range(peers)])


def staged(cotangent, weight, target_block, dest, source, count, lev_index, lev_frac):
    peers = 16
    me = lax.axis_index("tile").astype(jnp.int32).reshape(1)
    before, after = ring_ends(cotangent, peers)
    far, near, keep = products(
        (target_block, dest, source, count), me, cotangent, before, after, weight
    )
    far = swap(far, 1, peers)
    near = swap(near, 1, peers)
    over_y = {r: swap(sum_and_code([(far, r)], keep, 4 + r), 2, peers) for r in (3, 2, 1, 0)}
    over_z = [
        swap(sum_and_code([(near, r), (over_y[r], 0)], keep, r), 4 * r, peers) for r in (3, 2, 1)
    ]
    return finish(lev_index, lev_frac, [near, over_y[0]] + over_z, keep)


def vertical_matrix(lev_index, lev_frac, levels):
    columns = jnp.arange(levels)[None, :]
    lower = (columns == lev_index[:, None]).astype(jnp.float32)
    upper = (columns == lev_index[:, None] + 1).astype(jnp.float32)
    return (1.0 - lev_frac)[:, None] * lower + lev_frac[:, None] * upper


def slotted(cotangent, weight, target_block, dest, source, count, lev_index, lev_frac):
    peers = lax.axis_size("tile")
    entries, _, cells = weight.shape
    capacity = max(2, 2 * entries // peers)
    slots = peers * capacity
    before, after = ring_ends(cotangent, peers)
    window = jnp.concatenate([before, cotangent, after], axis=0)
    contrib = jnp.einsum(
        "ofp,ops->ofs", window[target_block[0]], weight, preferred_element_type=jnp.float32
    )
    live = jnp.arange(entries) < count[0]
    matches = ((dest[0][:, None] == jnp.arange(peers)[None, :]) & live[:, None]).astype(jnp.int32)
    rank = jnp.sum(matches * jnp.cumsum(matches, axis=0), axis=1) - 1
    slot = jnp.where(live, dest[0] * capacity + rank, slots)
    labels = jnp.full((slots,), SB, jnp.int32).at[slot].set(source[0], mode="drop")
    outgoing = jnp.zeros((slots, ROWS, cells), jnp.float32).at[slot].set(contrib, mode="drop")
    arrived = lax.all_to_all(outgoing, "tile", split_axis=0, concat_axis=0, tiled=True)
    arrived_labels = lax.all_to_all(labels, "tile", split_axis=0, concat_axis=0, tiled=True)
    chooser = (jnp.arange(SB)[:, None] == arrived_labels[None, :]).astype(jnp.float32)
    summed = jnp.einsum("br,rfs->bfs", chooser, arrived, precision=lax.Precision.HIGHEST)
    lifted = jnp.einsum(
        "jl,bvjs->bvls",
        vertical_matrix(lev_index, lev_frac, LEV),
        summed.reshape(SB, VARS, LEVT, cells),
        precision=lax.Precision.HIGHEST,
    )
    return lifted.reshape(SB, VARS * LEV, cells)


def solution(mesh):
    placed = (
        P(("grp", "tile"), None, None),
        P("tile", None, None),
        P("tile", None),
        P("tile", None),
        P("tile", None),
        P("tile"),
        P(),
        P(),
    )
    return jax.shard_map(
        staged if mesh.shape["tile"] == 16 else slotted,
        mesh=mesh,
        in_specs=placed,
        out_specs=P(("grp", "tile"), None, None),
        check_vma=False,
    )
```

```python
import functools

import jax
import jax.numpy as jnp
from jax import lax
from jax.experimental import pallas as pl
from jax.experimental.pallas import tpu as pltpu
from jax.sharding import PartitionSpec as P

VARS = 6
LEV = 20
LEVT = 8
SB = 16
ROWS = VARS * LEVT
BODY = SB * ROWS
CODED = BODY + SB
GROUP = 16
MIB = 1 << 20


def encode(read, write, exps):
    for b in range(SB):
        x = read(b)
        top = jnp.max(jnp.abs(x), axis=0, keepdims=True)
        e = jnp.ceil(jnp.log2(jnp.maximum(top, 1e-30)) + 0.001) - 15.0
        exps[b : b + 1, :] = e
        q = jnp.round(x * jnp.exp2(-e))
        write(b * ROWS, ROWS, q.astype(jnp.int32).astype(jnp.int16))
    write(BODY, SB, exps[...].astype(jnp.int32).astype(jnp.int16))


def scales(ref, i):
    return jnp.exp2(ref[i, BODY:CODED, :].astype(jnp.int32).astype(jnp.float32))


def decode(ref, i, scale, b):
    q = ref[i, b * ROWS : (b + 1) * ROWS, :].astype(jnp.int32).astype(jnp.float32)
    return q * scale[b : b + 1, :]


TRASH = 16 * SB


def add_products(first, entry_of, bin_of, left_of, w, acc, wide):
    found = []
    for i in range(wide):
        e = entry_of(first + i)
        found.append(jnp.dot(left_of(first + i), w[e], preferred_element_type=jnp.float32))
    for i in range(wide):
        at = bin_of(first + i)
        acc[at] = acc[at] + found[i]


def products_kernel(
    count_ref,
    me_ref,
    tb_hbm,
    dest_hbm,
    src_hbm,
    cot_hbm,
    w_hbm,
    acc,
    w,
    ends,
    cot,
    tb,
    dest,
    src,
    bins,
    sems,
    w_sems,
):
    entries, blocks = w.shape[0], cot.shape[0]
    groups = entries // GROUP
    count = count_ref[0]
    me = me_ref[0]
    used = (count + GROUP - 1) // GROUP

    def w_copy(g):
        return pltpu.make_async_copy(
            w_hbm.at[pl.ds(g * GROUP, GROUP)], w.at[pl.ds(g * GROUP, GROUP)], w_sems.at[g]
        )

    small = [
        pltpu.make_async_copy(a, b, sems.at[i])
        for i, (a, b) in enumerate(
            ((tb_hbm, tb), (dest_hbm, dest), (src_hbm, src), (cot_hbm, cot))
        )
    ]
    for copy in small:
        copy.start()
    for g in range(groups):

        @pl.when(g < used)
        def _():
            w_copy(g).start()

    @pl.loop(0, TRASH, unroll=8)
    def _(b):
        acc[b] = jnp.zeros(acc.shape[1:], jnp.float32)

    acc[TRASH] = jnp.zeros(acc.shape[1:], jnp.float32)

    for copy in small:
        copy.wait()

    @pl.loop(0, entries, init_carry=jnp.int32(0), unroll=4)
    def listed(k, n):
        rel = dest[0, k] ^ me
        slot = (rel & 1) * 8 + ((rel >> 1) & 1) * 4 + (rel >> 2)
        live = k < count
        at = jnp.where(live, slot * SB + src[0, k], TRASH)
        block = tb[0, k]
        outer = (block == 0) | (block == blocks + 1)
        bins[k] = jnp.where(outer, TRASH, at)
        tb[0, k] = jnp.clip(block - 1, 0, blocks - 1)
        ends[0, n] = k
        ends[1, n] = at
        ends[2, n] = jnp.where(block == 0, 0, 1)
        return n + (outer & live).astype(jnp.int32)

    for i in range(4):
        ends[0, listed + i] = 0
        ends[1, listed + i] = TRASH
        ends[2, listed + i] = 0
    ends[3, 0] = listed

    for g in range(groups):

        @pl.when(g < used)
        def _():
            w_copy(g).wait()

            @pl.loop(0, GROUP // 8)
            def _(part):
                add_products(
                    g * GROUP + part * 8,
                    lambda k: k,
                    lambda k: bins[k],
                    lambda k: cot[tb[0, k]],
                    w,
                    acc,
                    8,
                )


def products(tables, count, me, cotangent, weight):
    entries, cells_in, cells = weight.shape
    smem = pl.BlockSpec(memory_space=pltpu.SMEM)
    vmem = pl.BlockSpec(memory_space=pltpu.VMEM)
    hbm = pl.BlockSpec(memory_space=pltpu.HBM)
    return pl.pallas_call(
        products_kernel,
        out_shape=(
            jax.ShapeDtypeStruct((TRASH + 1, ROWS, cells), jnp.float32),
            jax.ShapeDtypeStruct(weight.shape, jnp.bfloat16),
            jax.ShapeDtypeStruct((4, entries + 4), jnp.int32),
        ),
        in_specs=[smem, smem] + [hbm] * 5,
        out_specs=(vmem, vmem, smem),
        scratch_shapes=[
            pltpu.VMEM(cotangent.shape, jnp.bfloat16),
            pltpu.SMEM((1, entries), jnp.int32),
            pltpu.SMEM((1, entries), jnp.int32),
            pltpu.SMEM((1, entries), jnp.int32),
            pltpu.SMEM((entries,), jnp.int32),
            pltpu.SemaphoreType.DMA((4,)),
            pltpu.SemaphoreType.DMA((entries // GROUP,)),
        ],
        compiler_params=pltpu.CompilerParams(vmem_limit_bytes=24 * MIB),
        cost_estimate=pl.CostEstimate(
            flops=2 * entries * ROWS * cells_in * cells,
            bytes_accessed=12 * MIB,
            transcendentals=0,
        ),
    )(count, me, *tables, cotangent, weight)


def code_slot(acc, slot, coded, exps, out_ref, out_slot):
    def read(b):
        total = acc[slot * SB + b]
        for r, i, s in coded:
            total = total + decode(r, i, s, b)
        return total

    def write(row, rows, value):
        out_ref[out_slot, row : row + rows, :] = value

    encode(read, write, exps)


def ends_kernel(ends, before, after, w, acc_in, acc, far_ref, sides, exps):
    sides[0] = before[0]
    sides[1] = after[0]

    @pl.loop(0, (ends[3, 0] + 3) // 4)
    def _(part):
        add_products(
            part * 4,
            lambda k: ends[0, k],
            lambda k: ends[1, k],
            lambda k: sides[ends[2, k]],
            w,
            acc,
            4,
        )

    @pl.loop(0, 4)
    def _(i):
        code_slot(acc, 12 + i, [], exps, far_ref, i)


def add_ends(ends, before, after, w, acc):
    cells = acc.shape[2]
    smem = pl.BlockSpec(memory_space=pltpu.SMEM)
    vmem = pl.BlockSpec(memory_space=pltpu.VMEM)
    return pl.pallas_call(
        ends_kernel,
        out_shape=(
            jax.ShapeDtypeStruct(acc.shape, jnp.float32),
            jax.ShapeDtypeStruct((4, CODED, cells), jnp.int16),
        ),
        in_specs=[smem] + [vmem] * 4,
        out_specs=(vmem, vmem),
        scratch_shapes=[
            pltpu.VMEM((2,) + before.shape[1:], jnp.bfloat16),
            pltpu.VMEM((SB, cells), jnp.float32),
        ],
        input_output_aliases={4: 0},
        compiler_params=pltpu.CompilerParams(vmem_limit_bytes=32 * MIB),
        cost_estimate=pl.CostEstimate(
            flops=10 * BODY * cells, bytes_accessed=8 * BODY * cells, transcendentals=0
        ),
    )(ends, before, after, w, acc)


def code_kernel(slots, takes, acc, *refs):
    arrays = refs[: len(refs) - len(slots) - 1]
    outs, exps = refs[len(arrays) : -1], refs[-1]
    for slot, pairs, out in zip(slots, takes, outs):
        coded = [(arrays[a], i, scales(arrays[a], i)) for a, i in pairs]
        code_slot(acc, slot, coded, exps, out, 0)


def code(acc, slots, takes, arrays):
    cells = acc.shape[2]
    vmem = pl.BlockSpec(memory_space=pltpu.VMEM)
    return pl.pallas_call(
        functools.partial(code_kernel, slots, takes),
        out_shape=tuple(jax.ShapeDtypeStruct((1, CODED, cells), jnp.int16) for _ in slots),
        in_specs=[vmem] * (1 + len(arrays)),
        out_specs=(vmem,) * len(slots),
        scratch_shapes=[pltpu.VMEM((SB, cells), jnp.float32)],
        compiler_params=pltpu.CompilerParams(vmem_limit_bytes=32 * MIB),
        cost_estimate=pl.CostEstimate(
            flops=10 * BODY * cells, bytes_accessed=8 * BODY * cells, transcendentals=0
        ),
    )(acc, *arrays)


def code_near_kernel(acc, near_ref, exps):
    @pl.loop(0, 4)
    def _(i):
        code_slot(acc, 8 + i, [], exps, near_ref, i)


def code_near(acc):
    cells = acc.shape[2]
    vmem = pl.BlockSpec(memory_space=pltpu.VMEM)
    return pl.pallas_call(
        code_near_kernel,
        out_shape=jax.ShapeDtypeStruct((4, CODED, cells), jnp.int16),
        in_specs=[vmem],
        out_specs=vmem,
        scratch_shapes=[pltpu.VMEM((SB, cells), jnp.float32)],
        compiler_params=pltpu.CompilerParams(vmem_limit_bytes=32 * MIB),
        cost_estimate=pl.CostEstimate(
            flops=10 * BODY * cells, bytes_accessed=8 * BODY * cells, transcendentals=0
        ),
    )(acc)


def finish_kernel(takes, index_ref, frac_ref, acc, *refs):
    arrays, out_hbm, out, sems = refs[:-3], refs[-3], refs[-2], refs[-1]
    high = VARS * LEV
    row = lax.broadcasted_iota(jnp.int32, (high, ROWS), 0)
    col = lax.broadcasted_iota(jnp.int32, (high, ROWS), 1)
    level = row % LEV
    lift = jnp.zeros((high, ROWS), jnp.float32)
    for j in range(LEVT):
        at, frac = index_ref[j], frac_ref[j]
        here = jnp.where(level == at, 1.0 - frac, jnp.where(level == at + 1, frac, 0.0))
        lift = jnp.where(col % LEVT == j, here, lift)
    lift = jnp.where(row // LEV == col // LEVT, lift, 0.0)
    high_part = lift.astype(jnp.bfloat16)
    low_part = (lift - high_part.astype(jnp.float32)).astype(jnp.bfloat16)
    left = jnp.concatenate([high_part, high_part, low_part, low_part], axis=1)
    coded = [(arrays[a], i, scales(arrays[a], i)) for a, i in takes]
    copies = []
    for b in range(SB):
        total = acc[b]
        for r, i, s in coded:
            total = total + decode(r, i, s, b)
        first = total.astype(jnp.bfloat16)
        second = (total - first.astype(jnp.float32)).astype(jnp.bfloat16)
        right = jnp.concatenate([first, second, first, second], axis=0)
        out[b] = jnp.dot(left, right, preferred_element_type=jnp.float32)
        if b % 4 == 3:
            part = pl.ds(b - 3, 4)
            copy = pltpu.make_async_copy(out.at[part], out_hbm.at[part], sems.at[b // 4])
            copy.start()
            copies.append(copy)
    for copy in copies:
        copy.wait()


def finish(lev_index, lev_frac, acc, takes, arrays):
    cells = acc.shape[2]
    smem = pl.BlockSpec(memory_space=pltpu.SMEM)
    vmem = pl.BlockSpec(memory_space=pltpu.VMEM)
    result = jax.ShapeDtypeStruct((SB, VARS * LEV, cells), jnp.float32)
    return pl.pallas_call(
        functools.partial(finish_kernel, takes),
        out_shape=result,
        in_specs=[smem, smem] + [vmem] * (1 + len(arrays)),
        out_specs=pl.BlockSpec(memory_space=pltpu.HBM),
        scratch_shapes=[
            pltpu.VMEM(result.shape, jnp.float32),
            pltpu.SemaphoreType.DMA((SB // 4,)),
        ],
        compiler_params=pltpu.CompilerParams(vmem_limit_bytes=32 * MIB),
        cost_estimate=pl.CostEstimate(
            flops=10 * BODY * cells, bytes_accessed=16 * BODY * cells, transcendentals=0
        ),
    )(lev_index, lev_frac, acc, *arrays)


def ring_ends(cotangent, peers):
    up = [(i, (i + 1) % peers) for i in range(peers)]
    down = [(j, i) for i, j in up]
    return (
        lax.ppermute(cotangent[-1:], "tile", up),
        lax.ppermute(cotangent[:1], "tile", down),
    )


def swap(value, bits, peers):
    return lax.ppermute(value, "tile", [(i, i ^ bits) for i in range(peers)])


def staged(cotangent, weight, target_block, dest, source, count, lev_index, lev_frac):
    peers = 16
    me = lax.axis_index("tile").astype(jnp.int32).reshape(1)
    before, after = ring_ends(cotangent, peers)
    acc, w, ends = products((target_block, dest, source), count, me, cotangent, weight)
    acc, far = add_ends(ends, before, after, w, acc)
    far = swap(far, 1, peers)
    near = swap(code_near(acc), 1, peers)
    (y3,) = code(acc, (7,), (((0, 3),),), (far,))
    y3 = swap(y3, 2, peers)
    y2, y1, y0 = code(acc, (6, 5, 4), (((0, 2),), ((0, 1),), ((0, 0),)), (far,))
    y2, y1, y0 = (swap(v, 2, peers) for v in (y2, y1, y0))
    (a3,) = code(acc, (3,), (((0, 3), (1, 0)),), (near, y3))
    a3 = swap(a3, 4, peers)
    (b2,) = code(acc, (2,), (((0, 2), (1, 0), (2, 0)),), (near, y2, a3))
    b2 = swap(b2, 8, peers)
    (a1,) = code(acc, (1,), (((0, 1), (1, 0)),), (near, y1))
    a1 = swap(a1, 4, peers)
    return finish(
        lev_index, lev_frac, acc, ((0, 0), (1, 0), (2, 0), (3, 0)), (near, y0, a1, b2)
    )


def vertical_matrix(lev_index, lev_frac, levels):
    columns = jnp.arange(levels)[None, :]
    lower = (columns == lev_index[:, None]).astype(jnp.float32)
    upper = (columns == lev_index[:, None] + 1).astype(jnp.float32)
    return (1.0 - lev_frac)[:, None] * lower + lev_frac[:, None] * upper


def slotted(cotangent, weight, target_block, dest, source, count, lev_index, lev_frac):
    peers = lax.axis_size("tile")
    entries, _, cells = weight.shape
    capacity = max(2, 2 * entries // peers)
    slots = peers * capacity
    before, after = ring_ends(cotangent, peers)
    window = jnp.concatenate([before, cotangent, after], axis=0)
    contrib = jnp.einsum(
        "ofp,ops->ofs", window[target_block[0]], weight, preferred_element_type=jnp.float32
    )
    live = jnp.arange(entries) < count[0]
    matches = ((dest[0][:, None] == jnp.arange(peers)[None, :]) & live[:, None]).astype(jnp.int32)
    rank = jnp.sum(matches * jnp.cumsum(matches, axis=0), axis=1) - 1
    slot = jnp.where(live, dest[0] * capacity + rank, slots)
    labels = jnp.full((slots,), SB, jnp.int32).at[slot].set(source[0], mode="drop")
    outgoing = jnp.zeros((slots, ROWS, cells), jnp.float32).at[slot].set(contrib, mode="drop")
    arrived = lax.all_to_all(outgoing, "tile", split_axis=0, concat_axis=0, tiled=True)
    arrived_labels = lax.all_to_all(labels, "tile", split_axis=0, concat_axis=0, tiled=True)
    chooser = (jnp.arange(SB)[:, None] == arrived_labels[None, :]).astype(jnp.float32)
    summed = jnp.einsum("br,rfs->bfs", chooser, arrived, precision=lax.Precision.HIGHEST)
    lifted = jnp.einsum(
        "jl,bvjs->bvls",
        vertical_matrix(lev_index, lev_frac, LEV),
        summed.reshape(SB, VARS, LEVT, cells),
        precision=lax.Precision.HIGHEST,
    )
    return lifted.reshape(SB, VARS * LEV, cells)


def solution(mesh):
    placed = (
        P(("grp", "tile"), None, None),
        P("tile", None, None),
        P("tile", None),
        P("tile", None),
        P("tile", None),
        P("tile"),
        P(),
        P(),
    )
    return jax.shard_map(
        staged if mesh.shape["tile"] == 16 else slotted,
        mesh=mesh,
        in_specs=placed,
        out_specs=P(("grp", "tile"), None, None),
        check_vma=False,
    )
```

```python
import functools

import jax
import jax.numpy as jnp
from jax import lax
from jax.experimental import pallas as pl
from jax.experimental.pallas import tpu as pltpu
from jax.sharding import PartitionSpec as P

VARS = 6
LEV = 20
LEVT = 8
SB = 16
ROWS = VARS * LEVT
BODY = SB * ROWS
CODED = BODY + SB
GROUP = 16
MIB = 1 << 20


def encode(read, write, exps):
    for b in range(SB):
        x = read(b)
        top = jnp.max(jnp.abs(x), axis=0, keepdims=True)
        e = jnp.ceil(jnp.log2(jnp.maximum(top, 1e-30)) + 0.001) - 15.0
        exps[b : b + 1, :] = e
        q = jnp.round(x * jnp.exp2(-e))
        write(b * ROWS, ROWS, q.astype(jnp.int32).astype(jnp.int16))
    write(BODY, SB, exps[...].astype(jnp.int32).astype(jnp.int16))


def scales(ref, i):
    return jnp.exp2(ref[i, BODY:CODED, :].astype(jnp.int32).astype(jnp.float32))


def decode(ref, i, scale, b):
    q = ref[i, b * ROWS : (b + 1) * ROWS, :].astype(jnp.int32).astype(jnp.float32)
    return q * scale[b : b + 1, :]


TRASH = 16 * SB


def add_products(entries, w, acc):
    found = [jnp.dot(left, w[e], preferred_element_type=jnp.float32) for e, left, _ in entries]
    for (_, _, at), value in zip(entries, found):
        acc[at] = acc[at] + value


def add_group(g, count, me, tables, cot, w, acc, ends):
    blocks = cot.shape[0]

    @pl.loop(0, GROUP // 8)
    def _(part):
        n = ends[3, 0]
        entries = []
        for i in range(8):
            k = g * GROUP + part * 8 + i
            block = tables[0, k]
            rel = tables[1, k] ^ me
            slot = (rel & 1) * 8 + ((rel >> 1) & 1) * 4 + (rel >> 2)
            live = k < count
            at = jnp.where(live, slot * SB + tables[2, k], TRASH)
            outer = (block == 0) | (block == blocks + 1)
            ends[0, n] = k
            ends[1, n] = at
            ends[2, n] = jnp.where(block == 0, 0, 1)
            n = n + (outer & live).astype(jnp.int32)
            left = cot[jnp.clip(block - 1, 0, blocks - 1)]
            entries.append((k, left, jnp.where(outer, TRASH, at)))
        ends[3, 0] = n
        add_products(entries, w, acc)


def first_half(count):
    used = (count + GROUP - 1) // GROUP
    return used, (used + 1) // 2


def first_kernel(
    count_ref,
    me_ref,
    tb_hbm,
    dest_hbm,
    src_hbm,
    cot_hbm,
    w_hbm,
    acc,
    w,
    cot,
    low,
    high,
    tables,
    ends,
    sems,
    w_sems,
):
    groups = w.shape[0] // GROUP
    count = count_ref[0]
    used, half = first_half(count)

    def w_copy(g):
        part = pl.ds(g * GROUP, GROUP)
        return pltpu.make_async_copy(w_hbm.at[part], w.at[part], w_sems.at[g])

    pairs = [(cot_hbm, cot)]
    pairs += [(t, tables.at[pl.ds(i, 1)]) for i, t in enumerate((tb_hbm, dest_hbm, src_hbm))]
    small = [pltpu.make_async_copy(a, b, sems.at[i]) for i, (a, b) in enumerate(pairs)]
    for copy in small:
        copy.start()
    for g in range(groups):

        @pl.when(g < used)
        def _():
            w_copy(g).start()

    @pl.loop(0, TRASH, unroll=8)
    def _(b):
        acc[b] = jnp.zeros(acc.shape[1:], jnp.float32)

    acc[TRASH] = jnp.zeros(acc.shape[1:], jnp.float32)
    ends[3, 0] = 0

    for copy in small:
        copy.wait()
    low[0] = cot[0]
    high[0] = cot[cot.shape[0] - 1]

    for g in range(groups):

        @pl.when(g < used)
        def _():
            w_copy(g).wait()

        @pl.when(g < half)
        def _():
            add_group(g, count, me_ref[0], tables, cot, w, acc, ends)


def in_hbm(x):
    return pltpu.with_memory_space_constraint(x, pltpu.HBM)


def products_first(tables, count, me, cotangent, weight):
    entries, cells_in, cells = weight.shape
    smem = pl.BlockSpec(memory_space=pltpu.SMEM)
    vmem = pl.BlockSpec(memory_space=pltpu.VMEM)
    hbm = pl.BlockSpec(memory_space=pltpu.HBM)
    end = jax.ShapeDtypeStruct((1,) + cotangent.shape[1:], cotangent.dtype)
    return pl.pallas_call(
        first_kernel,
        out_shape=(
            jax.ShapeDtypeStruct((TRASH + 1, ROWS, cells), jnp.float32),
            jax.ShapeDtypeStruct(weight.shape, weight.dtype),
            jax.ShapeDtypeStruct(cotangent.shape, cotangent.dtype),
            end,
            end,
            jax.ShapeDtypeStruct((3, entries), jnp.int32),
            jax.ShapeDtypeStruct((4, entries + 4), jnp.int32),
        ),
        in_specs=[smem, smem] + [hbm] * 5,
        out_specs=(vmem,) * 5 + (smem, smem),
        scratch_shapes=[
            pltpu.SemaphoreType.DMA((4,)),
            pltpu.SemaphoreType.DMA((entries // GROUP,)),
        ],
        compiler_params=pltpu.CompilerParams(vmem_limit_bytes=24 * MIB),
        cost_estimate=pl.CostEstimate(
            flops=entries * ROWS * cells_in * cells, bytes_accessed=12 * MIB, transcendentals=0
        ),
    )(count, me, *[in_hbm(t) for t in tables], in_hbm(cotangent), in_hbm(weight))


def second_kernel(count_ref, me_ref, tables, begun, cot, w, acc_in, acc, ends):
    count = count_ref[0]
    used, half = first_half(count)
    listed = begun[3, 0]

    @pl.loop(0, listed)
    def _(n):
        for i in range(3):
            ends[i, n] = begun[i, n]

    ends[3, 0] = listed

    @pl.loop(half, used)
    def _(g):
        add_group(g, count, me_ref[0], tables, cot, w, acc, ends)

    listed = ends[3, 0]
    for i in range(4):
        ends[0, listed + i] = 0
        ends[1, listed + i] = TRASH
        ends[2, listed + i] = 0


def products_second(tables, count, me, begun, cot, w, acc):
    entries, cells_in, cells = w.shape
    smem = pl.BlockSpec(memory_space=pltpu.SMEM)
    vmem = pl.BlockSpec(memory_space=pltpu.VMEM)
    return pl.pallas_call(
        second_kernel,
        out_shape=(
            jax.ShapeDtypeStruct(acc.shape, acc.dtype),
            jax.ShapeDtypeStruct(begun.shape, begun.dtype),
        ),
        in_specs=[smem] * 4 + [vmem] * 3,
        out_specs=(vmem, smem),
        input_output_aliases={6: 0},
        compiler_params=pltpu.CompilerParams(vmem_limit_bytes=32 * MIB),
        cost_estimate=pl.CostEstimate(
            flops=entries * ROWS * cells_in * cells, bytes_accessed=12 * MIB, transcendentals=0
        ),
    )(count, me, tables, begun, cot, w, acc)


def code_slot(acc, slot, coded, exps, out_ref, out_slot):
    def read(b):
        total = acc[slot * SB + b]
        for r, i, s in coded:
            total = total + decode(r, i, s, b)
        return total

    def write(row, rows, value):
        out_ref[out_slot, row : row + rows, :] = value

    encode(read, write, exps)


def ends_kernel(ends, before, after, w, acc_in, acc, far_ref, sides, exps):
    sides[0] = before[0]
    sides[1] = after[0]

    @pl.loop(0, (ends[3, 0] + 3) // 4)
    def _(part):
        at = [part * 4 + i for i in range(4)]
        add_products([(ends[0, k], sides[ends[2, k]], ends[1, k]) for k in at], w, acc)

    @pl.loop(0, 4)
    def _(i):
        code_slot(acc, 12 + i, [], exps, far_ref, i)


def add_ends(ends, before, after, w, acc):
    cells = acc.shape[2]
    smem = pl.BlockSpec(memory_space=pltpu.SMEM)
    vmem = pl.BlockSpec(memory_space=pltpu.VMEM)
    return pl.pallas_call(
        ends_kernel,
        out_shape=(
            jax.ShapeDtypeStruct(acc.shape, jnp.float32),
            jax.ShapeDtypeStruct((4, CODED, cells), jnp.int16),
        ),
        in_specs=[smem] + [vmem] * 4,
        out_specs=(vmem, vmem),
        scratch_shapes=[
            pltpu.VMEM((2,) + before.shape[1:], jnp.bfloat16),
            pltpu.VMEM((SB, cells), jnp.float32),
        ],
        input_output_aliases={4: 0},
        compiler_params=pltpu.CompilerParams(vmem_limit_bytes=32 * MIB),
        cost_estimate=pl.CostEstimate(
            flops=10 * BODY * cells, bytes_accessed=8 * BODY * cells, transcendentals=0
        ),
    )(ends, before, after, w, acc)


def code_kernel(slot, takes, acc, *refs):
    arrays, out, exps = refs[:-2], refs[-2], refs[-1]
    coded = [(arrays[a], i, scales(arrays[a], i)) for a, i in takes]
    code_slot(acc, slot, coded, exps, out, 0)


def code(acc, slot, takes, arrays):
    cells = acc.shape[2]
    vmem = pl.BlockSpec(memory_space=pltpu.VMEM)
    return pl.pallas_call(
        functools.partial(code_kernel, slot, takes),
        out_shape=jax.ShapeDtypeStruct((1, CODED, cells), jnp.int16),
        in_specs=[vmem] * (1 + len(arrays)),
        out_specs=vmem,
        scratch_shapes=[pltpu.VMEM((SB, cells), jnp.float32)],
        compiler_params=pltpu.CompilerParams(vmem_limit_bytes=32 * MIB),
        cost_estimate=pl.CostEstimate(
            flops=10 * BODY * cells, bytes_accessed=8 * BODY * cells, transcendentals=0
        ),
    )(acc, *arrays)


def code_near_kernel(acc, near_ref, exps):
    @pl.loop(0, 4)
    def _(i):
        code_slot(acc, 8 + i, [], exps, near_ref, i)


def code_near(acc):
    cells = acc.shape[2]
    vmem = pl.BlockSpec(memory_space=pltpu.VMEM)
    return pl.pallas_call(
        code_near_kernel,
        out_shape=jax.ShapeDtypeStruct((4, CODED, cells), jnp.int16),
        in_specs=[vmem],
        out_specs=vmem,
        scratch_shapes=[pltpu.VMEM((SB, cells), jnp.float32)],
        compiler_params=pltpu.CompilerParams(vmem_limit_bytes=32 * MIB),
        cost_estimate=pl.CostEstimate(
            flops=10 * BODY * cells, bytes_accessed=8 * BODY * cells, transcendentals=0
        ),
    )(acc)


def finish_kernel(takes, index_ref, frac_ref, acc, *refs):
    arrays, out_hbm, out, sems = refs[:-3], refs[-3], refs[-2], refs[-1]
    high = VARS * LEV
    row = lax.broadcasted_iota(jnp.int32, (high, ROWS), 0)
    col = lax.broadcasted_iota(jnp.int32, (high, ROWS), 1)
    level = row % LEV
    lift = jnp.zeros((high, ROWS), jnp.float32)
    for j in range(LEVT):
        at, frac = index_ref[j], frac_ref[j]
        here = jnp.where(level == at, 1.0 - frac, jnp.where(level == at + 1, frac, 0.0))
        lift = jnp.where(col % LEVT == j, here, lift)
    lift = jnp.where(row // LEV == col // LEVT, lift, 0.0)
    high_part = lift.astype(jnp.bfloat16)
    low_part = (lift - high_part.astype(jnp.float32)).astype(jnp.bfloat16)
    left = jnp.concatenate([high_part, high_part, low_part, low_part], axis=1)
    coded = [(arrays[a], i, scales(arrays[a], i)) for a, i in takes]
    copies = []
    for b in range(SB):
        total = acc[b]
        for r, i, s in coded:
            total = total + decode(r, i, s, b)
        first = total.astype(jnp.bfloat16)
        second = (total - first.astype(jnp.float32)).astype(jnp.bfloat16)
        right = jnp.concatenate([first, second, first, second], axis=0)
        out[b] = jnp.dot(left, right, preferred_element_type=jnp.float32)
        if b % 4 == 3:
            part = pl.ds(b - 3, 4)
            copy = pltpu.make_async_copy(out.at[part], out_hbm.at[part], sems.at[b // 4])
            copy.start()
            copies.append(copy)
    for copy in copies:
        copy.wait()


def finish(lev_index, lev_frac, acc, takes, arrays):
    cells = acc.shape[2]
    smem = pl.BlockSpec(memory_space=pltpu.SMEM)
    vmem = pl.BlockSpec(memory_space=pltpu.VMEM)
    result = jax.ShapeDtypeStruct((SB, VARS * LEV, cells), jnp.float32)
    return pl.pallas_call(
        functools.partial(finish_kernel, takes),
        out_shape=result,
        in_specs=[smem, smem] + [vmem] * (1 + len(arrays)),
        out_specs=pl.BlockSpec(memory_space=pltpu.HBM),
        scratch_shapes=[
            pltpu.VMEM(result.shape, jnp.float32),
            pltpu.SemaphoreType.DMA((SB // 4,)),
        ],
        compiler_params=pltpu.CompilerParams(vmem_limit_bytes=32 * MIB),
        cost_estimate=pl.CostEstimate(
            flops=10 * BODY * cells, bytes_accessed=16 * BODY * cells, transcendentals=0
        ),
    )(lev_index, lev_frac, acc, *arrays)


def ring_ends(low, high, peers):
    up = [(i, (i + 1) % peers) for i in range(peers)]
    down = [(j, i) for i, j in up]
    return lax.ppermute(high, "tile", up), lax.ppermute(low, "tile", down)


def swap(value, bits, peers):
    return lax.ppermute(value, "tile", [(i, i ^ bits) for i in range(peers)])


def staged(cotangent, weight, target_block, dest, source, count, lev_index, lev_frac):
    peers = 16
    me = lax.axis_index("tile").astype(jnp.int32).reshape(1)
    acc, w, cot, low, high, tables, ends = products_first(
        (target_block, dest, source), count, me, cotangent, weight
    )
    before, after = ring_ends(low, high, peers)
    acc, ends = products_second(tables, count, me, ends, cot, w, acc)
    acc, far = add_ends(ends, before, after, w, acc)
    far = swap(far, 1, peers)
    near = swap(code_near(acc), 1, peers)
    y3 = swap(code(acc, 7, ((0, 3),), (far,)), 2, peers)
    o1 = swap(code(acc, 5, ((0, 1),), (far,)), 4, peers)
    y2 = swap(code(acc, 6, ((0, 2),), (far, y3)), 2, peers)
    a3 = swap(code(acc, 3, ((0, 3), (1, 0)), (near, y3)), 4, peers)
    b2_own = code(acc, 2, ((0, 2), (1, 0), (2, 0)), (near, y2, a3))
    b2 = swap(b2_own, 8, peers)
    y0 = swap(code(acc, 4, ((0, 0), (1, 0)), (far, o1, y2)), 2, peers)
    a1 = swap(code(acc, 1, ((0, 1),), (near, b2_own)), 4, peers)
    return finish(
        lev_index, lev_frac, acc, ((0, 0), (1, 0), (2, 0), (3, 0)), (near, y0, a1, b2)
    )


def vertical_matrix(lev_index, lev_frac, levels):
    columns = jnp.arange(levels)[None, :]
    lower = (columns == lev_index[:, None]).astype(jnp.float32)
    upper = (columns == lev_index[:, None] + 1).astype(jnp.float32)
    return (1.0 - lev_frac)[:, None] * lower + lev_frac[:, None] * upper


def slotted(cotangent, weight, target_block, dest, source, count, lev_index, lev_frac):
    peers = lax.axis_size("tile")
    entries, _, cells = weight.shape
    capacity = max(2, 2 * entries // peers)
    slots = peers * capacity
    before, after = ring_ends(cotangent[:1], cotangent[-1:], peers)
    window = jnp.concatenate([before, cotangent, after], axis=0)
    contrib = jnp.einsum(
        "ofp,ops->ofs", window[target_block[0]], weight, preferred_element_type=jnp.float32
    )
    live = jnp.arange(entries) < count[0]
    matches = ((dest[0][:, None] == jnp.arange(peers)[None, :]) & live[:, None]).astype(jnp.int32)
    rank = jnp.sum(matches * jnp.cumsum(matches, axis=0), axis=1) - 1
    slot = jnp.where(live, dest[0] * capacity + rank, slots)
    labels = jnp.full((slots,), SB, jnp.int32).at[slot].set(source[0], mode="drop")
    outgoing = jnp.zeros((slots, ROWS, cells), jnp.float32).at[slot].set(contrib, mode="drop")
    arrived = lax.all_to_all(outgoing, "tile", split_axis=0, concat_axis=0, tiled=True)
    arrived_labels = lax.all_to_all(labels, "tile", split_axis=0, concat_axis=0, tiled=True)
    chooser = (jnp.arange(SB)[:, None] == arrived_labels[None, :]).astype(jnp.float32)
    summed = jnp.einsum("br,rfs->bfs", chooser, arrived, precision=lax.Precision.HIGHEST)
    lifted = jnp.einsum(
        "jl,bvjs->bvls",
        vertical_matrix(lev_index, lev_frac, LEV),
        summed.reshape(SB, VARS, LEVT, cells),
        precision=lax.Precision.HIGHEST,
    )
    return lifted.reshape(SB, VARS * LEV, cells)


def solution(mesh):
    placed = (
        P(("grp", "tile"), None, None),
        P("tile", None, None),
        P("tile", None),
        P("tile", None),
        P("tile", None),
        P("tile"),
        P(),
        P(),
    )
    return jax.shard_map(
        staged if mesh.shape["tile"] == 16 else slotted,
        mesh=mesh,
        in_specs=placed,
        out_specs=P(("grp", "tile"), None, None),
        check_vma=False,
    )
```

```python
import functools

import jax
import jax.numpy as jnp
from jax import lax
from jax.experimental import pallas as pl
from jax.experimental.pallas import tpu as pltpu
from jax.sharding import PartitionSpec as P

VARS = 6
LEV = 20
LEVT = 8
SB = 16
ROWS = VARS * LEVT
HALF = SB // 2
BODY = HALF * ROWS
CODED = BODY + 16
GROUP = 16
MIB = 1 << 20


def encode(read, write, exps):
    exps[HALF:, :] = jnp.zeros((16 - HALF, exps.shape[1]), jnp.float32)
    for b in range(HALF):
        x = read(b)
        top = jnp.max(jnp.abs(x), axis=0, keepdims=True)
        e = jnp.ceil(jnp.log2(jnp.maximum(top, 1e-30)) + 0.001) - 15.0
        exps[b : b + 1, :] = e
        q = jnp.round(x * jnp.exp2(-e))
        write(b * ROWS, ROWS, q.astype(jnp.int32).astype(jnp.int16))
    write(BODY, 16, exps[...].astype(jnp.int32).astype(jnp.int16))


def scales(ref, i):
    return jnp.exp2(ref[i, BODY:CODED, :].astype(jnp.int32).astype(jnp.float32))


def decode(ref, i, scale, b):
    q = ref[i, b * ROWS : (b + 1) * ROWS, :].astype(jnp.int32).astype(jnp.float32)
    return q * scale[b : b + 1, :]


TRASH = 16 * SB


def add_products(entries, w, acc):
    found = [jnp.dot(left, w[e], preferred_element_type=jnp.float32) for e, left, _ in entries]
    for (_, _, at), value in zip(entries, found):
        acc[at] = acc[at] + value


def add_group(g, count, me, tables, cot, w, acc, ends):
    blocks = cot.shape[0]

    @pl.loop(0, GROUP // 8)
    def _(part):
        n = ends[3, 0]
        entries = []
        for i in range(8):
            k = g * GROUP + part * 8 + i
            block = tables[0, k]
            rel = tables[1, k] ^ me
            slot = (rel & 1) * 8 + ((rel >> 1) & 1) * 4 + (rel >> 2)
            live = k < count
            at = jnp.where(live, slot * SB + tables[2, k], TRASH)
            outer = (block == 0) | (block == blocks + 1)
            ends[0, n] = k
            ends[1, n] = at
            ends[2, n] = jnp.where(block == 0, 0, 1)
            n = n + (outer & live).astype(jnp.int32)
            left = cot[jnp.clip(block - 1, 0, blocks - 1)]
            entries.append((k, left, jnp.where(outer, TRASH, at)))
        ends[3, 0] = n
        add_products(entries, w, acc)


def first_half(count):
    used = (count + GROUP - 1) // GROUP
    return used, (used + 1) // 2


def first_kernel(
    count_ref,
    me_ref,
    tb_hbm,
    dest_hbm,
    src_hbm,
    cot_hbm,
    w_hbm,
    acc,
    w,
    cot,
    low,
    high,
    tables,
    ends,
    sems,
    w_sems,
):
    groups = w.shape[0] // GROUP
    count = count_ref[0]
    used, half = first_half(count)

    def w_copy(g):
        part = pl.ds(g * GROUP, GROUP)
        return pltpu.make_async_copy(w_hbm.at[part], w.at[part], w_sems.at[g])

    pairs = [(cot_hbm, cot)]
    pairs += [(t, tables.at[pl.ds(i, 1)]) for i, t in enumerate((tb_hbm, dest_hbm, src_hbm))]
    small = [pltpu.make_async_copy(a, b, sems.at[i]) for i, (a, b) in enumerate(pairs)]
    for copy in small:
        copy.start()
    for g in range(groups):

        @pl.when(g < used)
        def _():
            w_copy(g).start()

    @pl.loop(0, TRASH, unroll=8)
    def _(b):
        acc[b] = jnp.zeros(acc.shape[1:], jnp.float32)

    acc[TRASH] = jnp.zeros(acc.shape[1:], jnp.float32)
    ends[3, 0] = 0

    for copy in small:
        copy.wait()
    low[0] = cot[0]
    high[0] = cot[cot.shape[0] - 1]

    for g in range(groups):

        @pl.when(g < used)
        def _():
            w_copy(g).wait()

        @pl.when(g < half)
        def _():
            add_group(g, count, me_ref[0], tables, cot, w, acc, ends)


def in_hbm(x):
    return pltpu.with_memory_space_constraint(x, pltpu.HBM)


def products_first(tables, count, me, cotangent, weight):
    entries, cells_in, cells = weight.shape
    smem = pl.BlockSpec(memory_space=pltpu.SMEM)
    vmem = pl.BlockSpec(memory_space=pltpu.VMEM)
    hbm = pl.BlockSpec(memory_space=pltpu.HBM)
    end = jax.ShapeDtypeStruct((1,) + cotangent.shape[1:], cotangent.dtype)
    return pl.pallas_call(
        first_kernel,
        out_shape=(
            jax.ShapeDtypeStruct((TRASH + 1, ROWS, cells), jnp.float32),
            jax.ShapeDtypeStruct(weight.shape, weight.dtype),
            jax.ShapeDtypeStruct(cotangent.shape, cotangent.dtype),
            end,
            end,
            jax.ShapeDtypeStruct((3, entries), jnp.int32),
            jax.ShapeDtypeStruct((4, entries + 4), jnp.int32),
        ),
        in_specs=[smem, smem] + [hbm] * 5,
        out_specs=(vmem,) * 5 + (smem, smem),
        scratch_shapes=[
            pltpu.SemaphoreType.DMA((4,)),
            pltpu.SemaphoreType.DMA((entries // GROUP,)),
        ],
        compiler_params=pltpu.CompilerParams(vmem_limit_bytes=24 * MIB),
        cost_estimate=pl.CostEstimate(
            flops=entries * ROWS * cells_in * cells, bytes_accessed=12 * MIB, transcendentals=0
        ),
    )(count, me, *[in_hbm(t) for t in tables], in_hbm(cotangent), in_hbm(weight))


def second_kernel(count_ref, me_ref, tables, begun, cot, w, acc_in, acc, ends):
    count = count_ref[0]
    used, half = first_half(count)
    listed = begun[3, 0]

    @pl.loop(0, listed)
    def _(n):
        for i in range(3):
            ends[i, n] = begun[i, n]

    ends[3, 0] = listed

    @pl.loop(half, used)
    def _(g):
        add_group(g, count, me_ref[0], tables, cot, w, acc, ends)

    listed = ends[3, 0]
    for i in range(4):
        ends[0, listed + i] = 0
        ends[1, listed + i] = TRASH
        ends[2, listed + i] = 0


def products_second(tables, count, me, begun, cot, w, acc):
    entries, cells_in, cells = w.shape
    smem = pl.BlockSpec(memory_space=pltpu.SMEM)
    vmem = pl.BlockSpec(memory_space=pltpu.VMEM)
    return pl.pallas_call(
        second_kernel,
        out_shape=(
            jax.ShapeDtypeStruct(acc.shape, acc.dtype),
            jax.ShapeDtypeStruct(begun.shape, begun.dtype),
        ),
        in_specs=[smem] * 4 + [vmem] * 3,
        out_specs=(vmem, smem),
        input_output_aliases={6: 0},
        compiler_params=pltpu.CompilerParams(vmem_limit_bytes=32 * MIB),
        cost_estimate=pl.CostEstimate(
            flops=entries * ROWS * cells_in * cells, bytes_accessed=12 * MIB, transcendentals=0
        ),
    )(count, me, tables, begun, cot, w, acc)


def code_half(acc, unit, coded, exps, out_ref, at):
    def read(b):
        total = acc[unit * HALF + b]
        for r, i, s in coded:
            total = total + decode(r, i, s, b)
        return total

    def write(row, rows, value):
        out_ref[at, row : row + rows, :] = value

    encode(read, write, exps)


def ends_kernel(ends, before, after, w, acc_in, acc, far_ref, sides, exps):
    sides[0] = before[0]
    sides[1] = after[0]

    @pl.loop(0, (ends[3, 0] + 3) // 4)
    def _(part):
        at = [part * 4 + i for i in range(4)]
        add_products([(ends[0, k], sides[ends[2, k]], ends[1, k]) for k in at], w, acc)

    @pl.loop(0, 8)
    def _(i):
        code_half(acc, 24 + i, [], exps, far_ref, i)


def add_ends(ends, before, after, w, acc):
    cells = acc.shape[2]
    smem = pl.BlockSpec(memory_space=pltpu.SMEM)
    vmem = pl.BlockSpec(memory_space=pltpu.VMEM)
    return pl.pallas_call(
        ends_kernel,
        out_shape=(
            jax.ShapeDtypeStruct(acc.shape, jnp.float32),
            jax.ShapeDtypeStruct((8, CODED, cells), jnp.int16),
        ),
        in_specs=[smem] + [vmem] * 4,
        out_specs=(vmem, vmem),
        scratch_shapes=[
            pltpu.VMEM((2,) + before.shape[1:], jnp.bfloat16),
            pltpu.VMEM((16, cells), jnp.float32),
        ],
        input_output_aliases={4: 0},
        compiler_params=pltpu.CompilerParams(vmem_limit_bytes=32 * MIB),
        cost_estimate=pl.CostEstimate(
            flops=10 * BODY * cells, bytes_accessed=8 * BODY * cells, transcendentals=0
        ),
    )(ends, before, after, w, acc)


def code_kernel(jobs, acc, *refs):
    arrays, outs, exps = refs[: -1 - len(jobs)], refs[-1 - len(jobs) : -1], refs[-1]
    for parts, out in zip(jobs, outs):
        for at, (unit, takes) in enumerate(parts):
            coded = [(arrays[a], i, scales(arrays[a], i)) for a, i in takes]
            code_half(acc, unit, coded, exps, out, at)


def code(acc, jobs, arrays):
    cells = acc.shape[2]
    vmem = pl.BlockSpec(memory_space=pltpu.VMEM)
    return pl.pallas_call(
        functools.partial(code_kernel, jobs),
        out_shape=tuple(
            jax.ShapeDtypeStruct((len(parts), CODED, cells), jnp.int16) for parts in jobs
        ),
        in_specs=[vmem] * (1 + len(arrays)),
        out_specs=(vmem,) * len(jobs),
        scratch_shapes=[pltpu.VMEM((16, cells), jnp.float32)],
        compiler_params=pltpu.CompilerParams(vmem_limit_bytes=32 * MIB),
        cost_estimate=pl.CostEstimate(
            flops=10 * BODY * cells, bytes_accessed=8 * BODY * cells, transcendentals=0
        ),
    )(acc, *arrays)


def code_near_kernel(acc, after, near_ref, exps):
    @pl.loop(0, 8)
    def _(i):
        code_half(acc, 16 + i, [], exps, near_ref, i)


def code_near(acc, after):
    cells = acc.shape[2]
    vmem = pl.BlockSpec(memory_space=pltpu.VMEM)
    return pl.pallas_call(
        code_near_kernel,
        out_shape=jax.ShapeDtypeStruct((8, CODED, cells), jnp.int16),
        in_specs=[vmem, vmem],
        out_specs=vmem,
        scratch_shapes=[pltpu.VMEM((16, cells), jnp.float32)],
        compiler_params=pltpu.CompilerParams(vmem_limit_bytes=32 * MIB),
        cost_estimate=pl.CostEstimate(
            flops=10 * BODY * cells, bytes_accessed=8 * BODY * cells, transcendentals=0
        ),
    )(acc, after)


def lift_kernel(index_ref, frac_ref, after, left):
    high = VARS * LEV
    row = lax.broadcasted_iota(jnp.int32, (high, ROWS), 0)
    col = lax.broadcasted_iota(jnp.int32, (high, ROWS), 1)
    level = row % LEV
    lift = jnp.zeros((high, ROWS), jnp.float32)
    for j in range(LEVT):
        at, frac = index_ref[j], frac_ref[j]
        here = jnp.where(level == at, 1.0 - frac, jnp.where(level == at + 1, frac, 0.0))
        lift = jnp.where(col % LEVT == j, here, lift)
    lift = jnp.where(row // LEV == col // LEVT, lift, 0.0)
    high_part = lift.astype(jnp.bfloat16)
    low_part = (lift - high_part.astype(jnp.float32)).astype(jnp.bfloat16)
    left[...] = jnp.concatenate([high_part, high_part, low_part, low_part], axis=1)


def lift_matrix(lev_index, lev_frac, after):
    smem = pl.BlockSpec(memory_space=pltpu.SMEM)
    vmem = pl.BlockSpec(memory_space=pltpu.VMEM)
    return pl.pallas_call(
        lift_kernel,
        out_shape=jax.ShapeDtypeStruct((VARS * LEV, 4 * ROWS), jnp.bfloat16),
        in_specs=[smem, smem, vmem],
        out_specs=vmem,
    )(lev_index, lev_frac, after)


def finish_kernel(half, takes, left, acc, *refs):
    arrays, out_hbm, out, sems = refs[:-3], refs[-3], refs[-2], refs[-1]
    coded = [(arrays[a], i, scales(arrays[a], i)) for a, i in takes]
    copies = []
    for b in range(HALF):
        total = acc[half * HALF + b]
        for r, i, s in coded:
            total = total + decode(r, i, s, b)
        first = total.astype(jnp.bfloat16)
        second = (total - first.astype(jnp.float32)).astype(jnp.bfloat16)
        right = jnp.concatenate([first, second, first, second], axis=0)
        out[b] = jnp.dot(left[...], right, preferred_element_type=jnp.float32)
        if b % 4 == 3:
            copy = pltpu.make_async_copy(
                out.at[pl.ds(b - 3, 4)],
                out_hbm.at[pl.ds(half * HALF + b - 3, 4)],
                sems.at[b // 4],
            )
            copy.start()
            copies.append(copy)
    for copy in copies:
        copy.wait()


def finish(half, left, acc, takes, arrays, begun=None):
    cells = acc.shape[2]
    vmem = pl.BlockSpec(memory_space=pltpu.VMEM)
    hbm = pl.BlockSpec(memory_space=pltpu.HBM)
    extra = () if begun is None else (begun,)
    return pl.pallas_call(
        functools.partial(finish_kernel, half, takes),
        out_shape=jax.ShapeDtypeStruct((SB, VARS * LEV, cells), jnp.float32),
        in_specs=[vmem] * (2 + len(arrays)) + [hbm] * len(extra),
        out_specs=hbm,
        scratch_shapes=[
            pltpu.VMEM((HALF, VARS * LEV, cells), jnp.float32),
            pltpu.SemaphoreType.DMA((HALF // 4,)),
        ],
        input_output_aliases={2 + len(arrays): 0} if extra else {},
        compiler_params=pltpu.CompilerParams(vmem_limit_bytes=32 * MIB),
        cost_estimate=pl.CostEstimate(
            flops=10 * BODY * cells, bytes_accessed=16 * BODY * cells, transcendentals=0
        ),
    )(left, acc, *arrays, *extra)


def ring_ends(low, high, peers):
    up = [(i, (i + 1) % peers) for i in range(peers)]
    down = [(j, i) for i, j in up]
    return lax.ppermute(high, "tile", up), lax.ppermute(low, "tile", down)


def swap(value, bits, peers):
    return lax.ppermute(value, "tile", [(i, i ^ bits) for i in range(peers)])


def staged(cotangent, weight, target_block, dest, source, count, lev_index, lev_frac):
    peers = 16
    me = lax.axis_index("tile").astype(jnp.int32).reshape(1)
    acc, w, cot, low, high, tables, ends = products_first(
        (target_block, dest, source), count, me, cotangent, weight
    )
    before, after = ring_ends(low, high, peers)
    acc, ends = products_second(tables, count, me, ends, cot, w, acc)
    acc, far = add_ends(ends, before, after, w, acc)
    far = swap(far, 1, peers)
    y3 = code(acc, (((14, ((0, 6),)),), ((15, ((0, 7),)),)), (far,))
    (o1_own,) = code(acc, (((10, ((0, 2),)), (11, ((0, 3),))),), (far, y3[0]))
    y2 = code(acc, (((12, ((0, 4),)),), ((13, ((0, 5),)),)), (far, o1_own))
    near = code_near(acc, y2[0])
    y3 = [swap(v, 2, peers) for v in y3]
    o1 = swap(o1_own, 4, peers)
    y2 = [swap(v, 2, peers) for v in y2]
    near = swap(near, 1, peers)
    (a3_low,) = code(acc, (((6, ((0, 6), (1, 0))),),), (near, y3[0]))
    (a3_high,) = code(acc, (((7, ((0, 7), (1, 0))),),), (near, y3[1], a3_low))
    a3 = [swap(a3_low, 4, peers), swap(a3_high, 4, peers)]
    (a1_own,) = code(acc, (((2, ((0, 2),)), (3, ((0, 3),))),), (near, a3_high))
    a1 = swap(a1_own, 4, peers)
    (y0_own,) = code(acc, (((8, ((0, 0), (1, 0))), (9, ((0, 1), (1, 1)))),), (far, o1, a1_own))
    y0 = swap(y0_own, 2, peers)
    (b2_low,) = code(acc, (((4, ((0, 4), (1, 0), (2, 0))),),), (near, y2[0], a3[0], y0_own))
    (b2_high,) = code(acc, (((5, ((0, 5), (1, 0), (2, 0))),),), (near, y2[1], a3[1], b2_low))
    b2 = [swap(b2_low, 8, peers), swap(b2_high, 8, peers)]
    left = lift_matrix(lev_index, lev_frac, b2_high)
    out = finish(0, left, acc, ((0, 0), (1, 0), (2, 0), (3, 0)), (near, y0, a1, b2[0]))
    return finish(1, left, acc, ((0, 1), (1, 1), (2, 1), (3, 0)), (near, y0, a1, b2[1]), out)


def vertical_matrix(lev_index, lev_frac, levels):
    columns = jnp.arange(levels)[None, :]
    lower = (columns == lev_index[:, None]).astype(jnp.float32)
    upper = (columns == lev_index[:, None] + 1).astype(jnp.float32)
    return (1.0 - lev_frac)[:, None] * lower + lev_frac[:, None] * upper


def slotted(cotangent, weight, target_block, dest, source, count, lev_index, lev_frac):
    peers = lax.axis_size("tile")
    entries, _, cells = weight.shape
    capacity = max(2, 2 * entries // peers)
    slots = peers * capacity
    before, after = ring_ends(cotangent[:1], cotangent[-1:], peers)
    window = jnp.concatenate([before, cotangent, after], axis=0)
    contrib = jnp.einsum(
        "ofp,ops->ofs", window[target_block[0]], weight, preferred_element_type=jnp.float32
    )
    live = jnp.arange(entries) < count[0]
    matches = ((dest[0][:, None] == jnp.arange(peers)[None, :]) & live[:, None]).astype(jnp.int32)
    rank = jnp.sum(matches * jnp.cumsum(matches, axis=0), axis=1) - 1
    slot = jnp.where(live, dest[0] * capacity + rank, slots)
    labels = jnp.full((slots,), SB, jnp.int32).at[slot].set(source[0], mode="drop")
    outgoing = jnp.zeros((slots, ROWS, cells), jnp.float32).at[slot].set(contrib, mode="drop")
    arrived = lax.all_to_all(outgoing, "tile", split_axis=0, concat_axis=0, tiled=True)
    arrived_labels = lax.all_to_all(labels, "tile", split_axis=0, concat_axis=0, tiled=True)
    chooser = (jnp.arange(SB)[:, None] == arrived_labels[None, :]).astype(jnp.float32)
    summed = jnp.einsum("br,rfs->bfs", chooser, arrived, precision=lax.Precision.HIGHEST)
    lifted = jnp.einsum(
        "jl,bvjs->bvls",
        vertical_matrix(lev_index, lev_frac, LEV),
        summed.reshape(SB, VARS, LEVT, cells),
        precision=lax.Precision.HIGHEST,
    )
    return lifted.reshape(SB, VARS * LEV, cells)


def solution(mesh):
    placed = (
        P(("grp", "tile"), None, None),
        P("tile", None, None),
        P("tile", None),
        P("tile", None),
        P("tile", None),
        P("tile"),
        P(),
        P(),
    )
    return jax.shard_map(
        staged if mesh.shape["tile"] == 16 else slotted,
        mesh=mesh,
        in_specs=placed,
        out_specs=P(("grp", "tile"), None, None),
        check_vma=False,
    )
```

```python
import functools

import jax
import jax.numpy as jnp
from jax import lax
from jax.experimental import pallas as pl
from jax.experimental.pallas import tpu as pltpu
from jax.sharding import PartitionSpec as P

VARS = 6
LEV = 20
LEVT = 8
SB = 16
ROWS = VARS * LEVT
HALF = SB // 2
BODY = HALF * ROWS
CODED = BODY + 16
GROUP = 16
MIB = 1 << 20


def encode(read, write, exps):
    exps[HALF:, :] = jnp.zeros((16 - HALF, exps.shape[1]), jnp.float32)
    for b in range(HALF):
        x = read(b)
        top = jnp.max(jnp.abs(x), axis=0, keepdims=True)
        e = jnp.ceil(jnp.log2(jnp.maximum(top, 1e-30)) + 0.001) - 15.0
        exps[b : b + 1, :] = e
        q = jnp.round(x * jnp.exp2(-e))
        write(b * ROWS, ROWS, q.astype(jnp.int32).astype(jnp.int16))
    write(BODY, 16, exps[...].astype(jnp.int32).astype(jnp.int16))


def scales(ref, i):
    return jnp.exp2(ref[i, BODY:CODED, :].astype(jnp.int32).astype(jnp.float32))


def decode(ref, i, scale, b):
    q = ref[i, b * ROWS : (b + 1) * ROWS, :].astype(jnp.int32).astype(jnp.float32)
    return q * scale[b : b + 1, :]


TRASH = 16 * SB


def add_products(entries, w, acc):
    found = [jnp.dot(left, w[e], preferred_element_type=jnp.float32) for e, left, _ in entries]
    for (_, _, at), value in zip(entries, found):
        acc[at] = acc[at] + value


def add_group(g, count, me, tables, cot, w, acc, ends):
    blocks = cot.shape[0]

    @pl.loop(0, GROUP // 8)
    def _(part):
        n = ends[3, 0]
        entries = []
        for i in range(8):
            k = g * GROUP + part * 8 + i
            block = tables[0, k]
            rel = tables[1, k] ^ me
            slot = (rel & 1) * 8 + ((rel >> 1) & 1) * 4 + (rel >> 2)
            live = k < count
            at = jnp.where(live, slot * SB + tables[2, k], TRASH)
            outer = (block == 0) | (block == blocks + 1)
            ends[0, n] = k
            ends[1, n] = at
            ends[2, n] = jnp.where(block == 0, 0, 1)
            n = n + (outer & live).astype(jnp.int32)
            left = cot[jnp.clip(block - 1, 0, blocks - 1)]
            entries.append((k, left, jnp.where(outer, TRASH, at)))
        ends[3, 0] = n
        add_products(entries, w, acc)


def first_half(count):
    used = (count + GROUP - 1) // GROUP
    return used, (used + 1) // 2


def first_kernel(
    count_ref,
    me_ref,
    tb_hbm,
    dest_hbm,
    src_hbm,
    cot_hbm,
    w_hbm,
    acc,
    w,
    cot,
    low,
    high,
    tables,
    ends,
    sems,
    w_sems,
):
    groups = w.shape[0] // GROUP
    count = count_ref[0]
    used, half = first_half(count)

    def w_copy(g):
        part = pl.ds(g * GROUP, GROUP)
        return pltpu.make_async_copy(w_hbm.at[part], w.at[part], w_sems.at[g])

    pairs = [(cot_hbm, cot)]
    pairs += [(t, tables.at[pl.ds(i, 1)]) for i, t in enumerate((tb_hbm, dest_hbm, src_hbm))]
    small = [pltpu.make_async_copy(a, b, sems.at[i]) for i, (a, b) in enumerate(pairs)]
    for copy in small:
        copy.start()
    for g in range(groups):

        @pl.when(g < used)
        def _():
            w_copy(g).start()

    @pl.loop(0, TRASH, unroll=8)
    def _(b):
        acc[b] = jnp.zeros(acc.shape[1:], jnp.float32)

    acc[TRASH] = jnp.zeros(acc.shape[1:], jnp.float32)
    ends[3, 0] = 0

    for copy in small:
        copy.wait()
    low[0] = cot[0]
    high[0] = cot[cot.shape[0] - 1]

    for g in range(groups):

        @pl.when(g < used)
        def _():
            w_copy(g).wait()

        @pl.when(g < half)
        def _():
            add_group(g, count, me_ref[0], tables, cot, w, acc, ends)


def in_hbm(x):
    return pltpu.with_memory_space_constraint(x, pltpu.HBM)


def products_first(tables, count, me, cotangent, weight):
    entries, cells_in, cells = weight.shape
    smem = pl.BlockSpec(memory_space=pltpu.SMEM)
    vmem = pl.BlockSpec(memory_space=pltpu.VMEM)
    hbm = pl.BlockSpec(memory_space=pltpu.HBM)
    end = jax.ShapeDtypeStruct((1,) + cotangent.shape[1:], cotangent.dtype)
    return pl.pallas_call(
        first_kernel,
        out_shape=(
            jax.ShapeDtypeStruct((TRASH + 1, ROWS, cells), jnp.float32),
            jax.ShapeDtypeStruct(weight.shape, weight.dtype),
            jax.ShapeDtypeStruct(cotangent.shape, cotangent.dtype),
            end,
            end,
            jax.ShapeDtypeStruct((3, entries), jnp.int32),
            jax.ShapeDtypeStruct((4, entries + 4), jnp.int32),
        ),
        in_specs=[smem, smem] + [hbm] * 5,
        out_specs=(vmem,) * 5 + (smem, smem),
        scratch_shapes=[
            pltpu.SemaphoreType.DMA((4,)),
            pltpu.SemaphoreType.DMA((entries // GROUP,)),
        ],
        compiler_params=pltpu.CompilerParams(vmem_limit_bytes=24 * MIB),
        cost_estimate=pl.CostEstimate(
            flops=entries * ROWS * cells_in * cells, bytes_accessed=12 * MIB, transcendentals=0
        ),
    )(count, me, *[in_hbm(t) for t in tables], in_hbm(cotangent), in_hbm(weight))


def second_kernel(count_ref, me_ref, tables, begun, cot, w, acc_in, acc, ends):
    count = count_ref[0]
    used, half = first_half(count)
    listed = begun[3, 0]

    @pl.loop(0, listed)
    def _(n):
        for i in range(3):
            ends[i, n] = begun[i, n]

    ends[3, 0] = listed

    @pl.loop(half, used)
    def _(g):
        add_group(g, count, me_ref[0], tables, cot, w, acc, ends)

    listed = ends[3, 0]
    for i in range(4):
        ends[0, listed + i] = 0
        ends[1, listed + i] = TRASH
        ends[2, listed + i] = 0


def products_second(tables, count, me, begun, cot, w, acc):
    entries, cells_in, cells = w.shape
    smem = pl.BlockSpec(memory_space=pltpu.SMEM)
    vmem = pl.BlockSpec(memory_space=pltpu.VMEM)
    return pl.pallas_call(
        second_kernel,
        out_shape=(
            jax.ShapeDtypeStruct(acc.shape, acc.dtype),
            jax.ShapeDtypeStruct(begun.shape, begun.dtype),
        ),
        in_specs=[smem] * 4 + [vmem] * 3,
        out_specs=(vmem, smem),
        input_output_aliases={6: 0},
        compiler_params=pltpu.CompilerParams(vmem_limit_bytes=32 * MIB),
        cost_estimate=pl.CostEstimate(
            flops=entries * ROWS * cells_in * cells, bytes_accessed=12 * MIB, transcendentals=0
        ),
    )(count, me, tables, begun, cot, w, acc)


def code_half(acc, unit, coded, exps, out_ref, at):
    def read(b):
        total = acc[unit * HALF + b]
        for r, i, s in coded:
            total = total + decode(r, i, s, b)
        return total

    def write(row, rows, value):
        out_ref[at, row : row + rows, :] = value

    encode(read, write, exps)


def ends_kernel(ends, before, after, w, acc_in, acc, far_ref, sides, exps):
    sides[0] = before[0]
    sides[1] = after[0]

    @pl.loop(0, (ends[3, 0] + 3) // 4)
    def _(part):
        at = [part * 4 + i for i in range(4)]
        add_products([(ends[0, k], sides[ends[2, k]], ends[1, k]) for k in at], w, acc)

    @pl.loop(0, 8)
    def _(i):
        code_half(acc, 24 + i, [], exps, far_ref, i)


def add_ends(ends, before, after, w, acc):
    cells = acc.shape[2]
    smem = pl.BlockSpec(memory_space=pltpu.SMEM)
    vmem = pl.BlockSpec(memory_space=pltpu.VMEM)
    return pl.pallas_call(
        ends_kernel,
        out_shape=(
            jax.ShapeDtypeStruct(acc.shape, jnp.float32),
            jax.ShapeDtypeStruct((8, CODED, cells), jnp.int16),
        ),
        in_specs=[smem] + [vmem] * 4,
        out_specs=(vmem, vmem),
        scratch_shapes=[
            pltpu.VMEM((2,) + before.shape[1:], jnp.bfloat16),
            pltpu.VMEM((16, cells), jnp.float32),
        ],
        input_output_aliases={4: 0},
        compiler_params=pltpu.CompilerParams(vmem_limit_bytes=32 * MIB),
        cost_estimate=pl.CostEstimate(
            flops=10 * BODY * cells, bytes_accessed=8 * BODY * cells, transcendentals=0
        ),
    )(ends, before, after, w, acc)


def code_kernel(jobs, acc, *refs):
    arrays, outs, exps = refs[: -1 - len(jobs)], refs[-1 - len(jobs) : -1], refs[-1]
    for parts, out in zip(jobs, outs):
        for at, (unit, takes) in enumerate(parts):
            coded = [(arrays[a], i, scales(arrays[a], i)) for a, i in takes]
            code_half(acc, unit, coded, exps, out, at)


def code(acc, jobs, arrays):
    cells = acc.shape[2]
    vmem = pl.BlockSpec(memory_space=pltpu.VMEM)
    return pl.pallas_call(
        functools.partial(code_kernel, jobs),
        out_shape=tuple(
            jax.ShapeDtypeStruct((len(parts), CODED, cells), jnp.int16) for parts in jobs
        ),
        in_specs=[vmem] * (1 + len(arrays)),
        out_specs=(vmem,) * len(jobs),
        scratch_shapes=[pltpu.VMEM((16, cells), jnp.float32)],
        compiler_params=pltpu.CompilerParams(vmem_limit_bytes=32 * MIB),
        cost_estimate=pl.CostEstimate(
            flops=10 * BODY * cells, bytes_accessed=8 * BODY * cells, transcendentals=0
        ),
    )(acc, *arrays)


def code_near_kernel(acc, near_ref, exps):
    @pl.loop(0, 8)
    def _(i):
        code_half(acc, 16 + i, [], exps, near_ref, i)


def code_near(acc):
    cells = acc.shape[2]
    vmem = pl.BlockSpec(memory_space=pltpu.VMEM)
    return pl.pallas_call(
        code_near_kernel,
        out_shape=jax.ShapeDtypeStruct((8, CODED, cells), jnp.int16),
        in_specs=[vmem],
        out_specs=vmem,
        scratch_shapes=[pltpu.VMEM((16, cells), jnp.float32)],
        compiler_params=pltpu.CompilerParams(vmem_limit_bytes=32 * MIB),
        cost_estimate=pl.CostEstimate(
            flops=10 * BODY * cells, bytes_accessed=8 * BODY * cells, transcendentals=0
        ),
    )(acc)


def lift_kernel(index_ref, frac_ref, after, left):
    high = VARS * LEV
    row = lax.broadcasted_iota(jnp.int32, (high, ROWS), 0)
    col = lax.broadcasted_iota(jnp.int32, (high, ROWS), 1)
    level = row % LEV
    lift = jnp.zeros((high, ROWS), jnp.float32)
    for j in range(LEVT):
        at, frac = index_ref[j], frac_ref[j]
        here = jnp.where(level == at, 1.0 - frac, jnp.where(level == at + 1, frac, 0.0))
        lift = jnp.where(col % LEVT == j, here, lift)
    lift = jnp.where(row // LEV == col // LEVT, lift, 0.0)
    high_part = lift.astype(jnp.bfloat16)
    low_part = (lift - high_part.astype(jnp.float32)).astype(jnp.bfloat16)
    left[...] = jnp.concatenate([high_part, high_part, low_part, low_part], axis=1)


def lift_matrix(lev_index, lev_frac, after):
    smem = pl.BlockSpec(memory_space=pltpu.SMEM)
    vmem = pl.BlockSpec(memory_space=pltpu.VMEM)
    return pl.pallas_call(
        lift_kernel,
        out_shape=jax.ShapeDtypeStruct((VARS * LEV, 4 * ROWS), jnp.bfloat16),
        in_specs=[smem, smem, vmem],
        out_specs=vmem,
        compiler_params=pltpu.CompilerParams(vmem_limit_bytes=4 * MIB),
    )(lev_index, lev_frac, after)


def finish_kernel(half, takes, left, acc, *refs):
    arrays, out_hbm, out, sems = refs[:-3], refs[-3], refs[-2], refs[-1]
    coded = [(arrays[a], i, scales(arrays[a], i)) for a, i in takes]
    copies = []
    for b in range(HALF):
        total = acc[half * HALF + b]
        for r, i, s in coded:
            total = total + decode(r, i, s, b)
        first = total.astype(jnp.bfloat16)
        second = (total - first.astype(jnp.float32)).astype(jnp.bfloat16)
        right = jnp.concatenate([first, second, first, second], axis=0)
        out[b] = jnp.dot(left[...], right, preferred_element_type=jnp.float32)
        if b % 4 == 3:
            copy = pltpu.make_async_copy(
                out.at[pl.ds(b - 3, 4)],
                out_hbm.at[pl.ds(half * HALF + b - 3, 4)],
                sems.at[b // 4],
            )
            copy.start()
            copies.append(copy)
    for copy in copies:
        copy.wait()


def finish(half, left, acc, takes, arrays, begun=None):
    cells = acc.shape[2]
    vmem = pl.BlockSpec(memory_space=pltpu.VMEM)
    hbm = pl.BlockSpec(memory_space=pltpu.HBM)
    extra = () if begun is None else (begun,)
    return pl.pallas_call(
        functools.partial(finish_kernel, half, takes),
        out_shape=jax.ShapeDtypeStruct((SB, VARS * LEV, cells), jnp.float32),
        in_specs=[vmem] * (2 + len(arrays)) + [hbm] * len(extra),
        out_specs=hbm,
        scratch_shapes=[
            pltpu.VMEM((HALF, VARS * LEV, cells), jnp.float32),
            pltpu.SemaphoreType.DMA((HALF // 4,)),
        ],
        input_output_aliases={2 + len(arrays): 0} if extra else {},
        compiler_params=pltpu.CompilerParams(vmem_limit_bytes=32 * MIB),
        cost_estimate=pl.CostEstimate(
            flops=10 * BODY * cells, bytes_accessed=16 * BODY * cells, transcendentals=0
        ),
    )(left, acc, *arrays, *extra)


def ring_ends(low, high, peers):
    up = [(i, (i + 1) % peers) for i in range(peers)]
    down = [(j, i) for i, j in up]
    return lax.ppermute(high, "tile", up), lax.ppermute(low, "tile", down)


def swap(value, bits, peers):
    return lax.ppermute(value, "tile", [(i, i ^ bits) for i in range(peers)])


def staged(cotangent, weight, target_block, dest, source, count, lev_index, lev_frac):
    peers = 16
    me = lax.axis_index("tile").astype(jnp.int32).reshape(1)
    acc, w, cot, low, high, tables, ends = products_first(
        (target_block, dest, source), count, me, cotangent, weight
    )
    before, after = ring_ends(low, high, peers)
    acc, ends = products_second(tables, count, me, ends, cot, w, acc)
    acc, far = add_ends(ends, before, after, w, acc)
    far = swap(far, 1, peers)
    near = swap(code_near(acc), 1, peers)
    y3 = code(acc, (((14, ((0, 6),)),), ((15, ((0, 7),)),)), (far,))
    y3 = [swap(v, 2, peers) for v in y3]
    (y2_own,) = code(acc, (((12, ((0, 4),)), (13, ((0, 5),))),), (far, y3[0]))
    y2 = swap(y2_own, 2, peers)
    (a3_low,) = code(acc, (((6, ((0, 6), (1, 0))),),), (near, y3[0], y2_own))
    (a3_high,) = code(acc, (((7, ((0, 7), (1, 0))),),), (near, y3[1], a3_low))
    a3 = [swap(a3_low, 4, peers), swap(a3_high, 4, peers)]
    (y1_own,) = code(acc, (((10, ((0, 2),)), (11, ((0, 3),))),), (far, a3_high))
    y1 = swap(y1_own, 2, peers)
    (b2_low,) = code(acc, (((4, ((0, 4), (1, 0), (2, 0))),),), (near, y2, a3[0], y1_own))
    (b2_high,) = code(acc, (((5, ((0, 5), (1, 1), (2, 0))),),), (near, y2, a3[1], b2_low))
    b2 = [swap(b2_low, 8, peers), swap(b2_high, 8, peers)]
    (y0_own,) = code(acc, (((8, ((0, 0),)), (9, ((0, 1),))),), (far, b2_high))
    y0 = swap(y0_own, 2, peers)
    (a1_own,) = code(acc, (((2, ((0, 2), (1, 0))), (3, ((0, 3), (1, 1)))),), (near, y1, y0_own))
    a1 = swap(a1_own, 4, peers)
    left = lift_matrix(lev_index, lev_frac, a1_own)
    out = finish(0, left, acc, ((0, 0), (1, 0), (2, 0), (3, 0)), (near, y0, a1, b2[0]))
    return finish(1, left, acc, ((0, 1), (1, 1), (2, 1), (3, 0)), (near, y0, a1, b2[1]), out)


def vertical_matrix(lev_index, lev_frac, levels):
    columns = jnp.arange(levels)[None, :]
    lower = (columns == lev_index[:, None]).astype(jnp.float32)
    upper = (columns == lev_index[:, None] + 1).astype(jnp.float32)
    return (1.0 - lev_frac)[:, None] * lower + lev_frac[:, None] * upper


def slotted(cotangent, weight, target_block, dest, source, count, lev_index, lev_frac):
    peers = lax.axis_size("tile")
    entries, _, cells = weight.shape
    capacity = max(2, 2 * entries // peers)
    slots = peers * capacity
    before, after = ring_ends(cotangent[:1], cotangent[-1:], peers)
    window = jnp.concatenate([before, cotangent, after], axis=0)
    contrib = jnp.einsum(
        "ofp,ops->ofs", window[target_block[0]], weight, preferred_element_type=jnp.float32
    )
    live = jnp.arange(entries) < count[0]
    matches = ((dest[0][:, None] == jnp.arange(peers)[None, :]) & live[:, None]).astype(jnp.int32)
    rank = jnp.sum(matches * jnp.cumsum(matches, axis=0), axis=1) - 1
    slot = jnp.where(live, dest[0] * capacity + rank, slots)
    labels = jnp.full((slots,), SB, jnp.int32).at[slot].set(source[0], mode="drop")
    outgoing = jnp.zeros((slots, ROWS, cells), jnp.float32).at[slot].set(contrib, mode="drop")
    arrived = lax.all_to_all(outgoing, "tile", split_axis=0, concat_axis=0, tiled=True)
    arrived_labels = lax.all_to_all(labels, "tile", split_axis=0, concat_axis=0, tiled=True)
    chooser = (jnp.arange(SB)[:, None] == arrived_labels[None, :]).astype(jnp.float32)
    summed = jnp.einsum("br,rfs->bfs", chooser, arrived, precision=lax.Precision.HIGHEST)
    lifted = jnp.einsum(
        "jl,bvjs->bvls",
        vertical_matrix(lev_index, lev_frac, LEV),
        summed.reshape(SB, VARS, LEVT, cells),
        precision=lax.Precision.HIGHEST,
    )
    return lifted.reshape(SB, VARS * LEV, cells)


def solution(mesh):
    placed = (
        P(("grp", "tile"), None, None),
        P("tile", None, None),
        P("tile", None),
        P("tile", None),
        P("tile", None),
        P("tile"),
        P(),
        P(),
    )
    return jax.shard_map(
        staged if mesh.shape["tile"] == 16 else slotted,
        mesh=mesh,
        in_specs=placed,
        out_specs=P(("grp", "tile"), None, None),
        check_vma=False,
    )
```

```python
import functools

import jax
import jax.numpy as jnp
from jax import lax
from jax.experimental import pallas as pl
from jax.experimental.pallas import tpu as pltpu
from jax.sharding import PartitionSpec as P

VARS = 6
LEV = 20
LEVT = 8
SB = 16
ROWS = VARS * LEVT
HALF = SB // 2
BODY = HALF * ROWS
CODED = BODY + 16
GROUP = 16
MIB = 1 << 20
LITTLE = pl.CostEstimate(flops=1, bytes_accessed=1, transcendentals=0)
MUCH = pl.CostEstimate(flops=1 << 28, bytes_accessed=12 * MIB, transcendentals=0)


def encode(read, write, exps):
    exps[HALF:, :] = jnp.zeros((16 - HALF, exps.shape[1]), jnp.float32)
    for b in range(HALF):
        x = read(b)
        top = jnp.max(jnp.abs(x), axis=0, keepdims=True)
        e = jnp.ceil(jnp.log2(jnp.maximum(top, 1e-30)) + 0.001) - 15.0
        exps[b : b + 1, :] = e
        q = jnp.round(x * jnp.exp2(-e))
        write(b * ROWS, ROWS, q.astype(jnp.int32).astype(jnp.int16))
    write(BODY, 16, exps[...].astype(jnp.int32).astype(jnp.int16))


def scales(ref, i):
    return jnp.exp2(ref[i, BODY:CODED, :].astype(jnp.int32).astype(jnp.float32))


def decode(ref, i, scale, b):
    q = ref[i, b * ROWS : (b + 1) * ROWS, :].astype(jnp.int32).astype(jnp.float32)
    return q * scale[b : b + 1, :]


TRASH = 16 * SB


def add_products(entries, w, acc):
    found = [jnp.dot(left, w[e], preferred_element_type=jnp.float32) for e, left, _ in entries]
    for (_, _, at), value in zip(entries, found):
        acc[at] = acc[at] + value


def add_group(g, count, me, tables, cot, w, acc, ends):
    blocks = cot.shape[0]

    @pl.loop(0, GROUP // 8)
    def _(part):
        n = ends[3, 0]
        entries = []
        for i in range(8):
            k = g * GROUP + part * 8 + i
            block = tables[0, k]
            rel = tables[1, k] ^ me
            slot = (rel & 1) * 8 + ((rel >> 1) & 1) * 4 + (rel >> 2)
            live = k < count
            at = jnp.where(live, slot * SB + tables[2, k], TRASH)
            outer = (block == 0) | (block == blocks + 1)
            ends[0, n] = k
            ends[1, n] = at
            ends[2, n] = jnp.where(block == 0, 0, 1)
            n = n + (outer & live).astype(jnp.int32)
            left = cot[jnp.clip(block - 1, 0, blocks - 1)]
            entries.append((k, left, jnp.where(outer, TRASH, at)))
        ends[3, 0] = n
        add_products(entries, w, acc)


def groups_of(count):
    used = (count + GROUP - 1) // GROUP
    return used, (used + 1) // 2


def load(used, pairs, w_hbm, w, acc, sems, w_sems):
    def w_copy(g):
        part = pl.ds(g * GROUP, GROUP)
        return pltpu.make_async_copy(w_hbm.at[part], w.at[part], w_sems.at[g])

    small = [pltpu.make_async_copy(a, b, sems.at[i]) for i, (a, b) in enumerate(pairs)]
    for copy in small:
        copy.start()
    for g in range(w.shape[0] // GROUP):

        @pl.when(g < used)
        def _():
            w_copy(g).start()

    @pl.loop(0, TRASH, unroll=8)
    def _(b):
        acc[b] = jnp.zeros(acc.shape[1:], jnp.float32)

    acc[TRASH] = jnp.zeros(acc.shape[1:], jnp.float32)
    for copy in small:
        copy.wait()
    return w_copy


def ahead_kernel(
    count_ref, me_ref, tb, dest, src, cot_hbm, w_hbm, low_in, acc, w, cot, low, ends, *scratch
):
    tables, sems, w_sems = scratch
    used, half = groups_of(count_ref[0])
    low[...] = low_in[...]

    @pl.when(me_ref[0] == 0)
    def _():
        pairs = [(cot_hbm, cot)]
        pairs += [(t, tables.at[pl.ds(i, 1)]) for i, t in enumerate((tb, dest, src))]
        w_copy = load(used, pairs, w_hbm, w, acc, sems, w_sems)
        ends[3, 0] = 0
        for g in range(w.shape[0] // GROUP):

            @pl.when(g < used)
            def _():
                w_copy(g).wait()

            @pl.when(g < half)
            def _():
                add_group(g, count_ref[0], me_ref[0], tables, cot, w, acc, ends)


def rest_kernel(
    count_ref, me_ref, tb, dest, src, cot_hbm, w_hbm, begun, acc_in, w_in, cot_in, *refs
):
    acc, w, cot, ends, tables, sems, w_sems = refs
    used, half = groups_of(count_ref[0])
    early = me_ref[0] == 0
    done = jnp.where(early, half, 0)
    listed = jnp.where(early, begun[3, 0], 0)
    three = [(t, tables.at[pl.ds(i, 1)]) for i, t in enumerate((tb, dest, src))]

    @pl.when(early)
    def _():
        small = [pltpu.make_async_copy(a, b, sems.at[i]) for i, (a, b) in enumerate(three)]
        for copy in small:
            copy.start()
        for copy in small:
            copy.wait()

    @pl.when(jnp.logical_not(early))
    def _():
        load(used, three + [(cot_hbm, cot)], w_hbm, w, acc, sems, w_sems)

    @pl.loop(0, listed)
    def _(n):
        for i in range(3):
            ends[i, n] = begun[i, n]

    ends[3, 0] = listed

    for g in range(w.shape[0] // GROUP):

        @pl.when(jnp.logical_not(early) & (g < used))
        def _():
            part = pl.ds(g * GROUP, GROUP)
            pltpu.make_async_copy(w_hbm.at[part], w.at[part], w_sems.at[g]).wait()

        @pl.when((g >= done) & (g < used))
        def _():
            add_group(g, count_ref[0], me_ref[0], tables, cot, w, acc, ends)

    listed = ends[3, 0]
    for i in range(4):
        ends[0, listed + i] = 0
        ends[1, listed + i] = TRASH
        ends[2, listed + i] = 0


def in_hbm(x):
    return pltpu.with_memory_space_constraint(x, pltpu.HBM)


def products_call(kernel, operands, given, low, cost):
    cotangent, weight = operands[5], operands[6]
    entries, _, cells = weight.shape
    smem = pl.BlockSpec(memory_space=pltpu.SMEM)
    vmem = pl.BlockSpec(memory_space=pltpu.VMEM)
    hbm = pl.BlockSpec(memory_space=pltpu.HBM)
    results = [
        jax.ShapeDtypeStruct((TRASH + 1, ROWS, cells), jnp.float32),
        jax.ShapeDtypeStruct(weight.shape, weight.dtype),
        jax.ShapeDtypeStruct(cotangent.shape, cotangent.dtype),
    ]
    listed = jax.ShapeDtypeStruct((4, entries + 4), jnp.int32)
    first = not given
    if first:
        results.append(jax.ShapeDtypeStruct(low.shape, low.dtype))
    return pl.pallas_call(
        kernel,
        out_shape=tuple(results + [listed]),
        in_specs=[smem, smem] + [hbm] * 5 + ([vmem] if first else [smem] + [vmem] * 3),
        out_specs=(vmem,) * len(results) + (smem,),
        scratch_shapes=[
            pltpu.SMEM((3, entries), jnp.int32),
            pltpu.SemaphoreType.DMA((4,)),
            pltpu.SemaphoreType.DMA((entries // GROUP,)),
        ],
        input_output_aliases={} if first else {8: 0, 9: 1, 10: 2},
        compiler_params=pltpu.CompilerParams(vmem_limit_bytes=24 * MIB),
        cost_estimate=cost,
    )(*operands[:2], *[in_hbm(x) for x in operands[2:]], *([low] if first else given))


def code_half(acc, unit, coded, exps, out_ref, at):
    def read(b):
        total = acc[unit * HALF + b]
        for r, i, s in coded:
            total = total + decode(r, i, s, b)
        return total

    def write(row, rows, value):
        out_ref[at, row : row + rows, :] = value

    encode(read, write, exps)


def ends_kernel(ends, before, after, w, acc_in, acc, far_ref, sides, exps):
    sides[0] = before[0]
    sides[1] = after[0]

    @pl.loop(0, (ends[3, 0] + 3) // 4)
    def _(part):
        at = [part * 4 + i for i in range(4)]
        add_products([(ends[0, k], sides[ends[2, k]], ends[1, k]) for k in at], w, acc)

    @pl.loop(0, 8)
    def _(i):
        code_half(acc, 24 + i, [], exps, far_ref, i)


def add_ends(ends, before, after, w, acc):
    cells = acc.shape[2]
    smem = pl.BlockSpec(memory_space=pltpu.SMEM)
    vmem = pl.BlockSpec(memory_space=pltpu.VMEM)
    return pl.pallas_call(
        ends_kernel,
        out_shape=(
            jax.ShapeDtypeStruct(acc.shape, jnp.float32),
            jax.ShapeDtypeStruct((8, CODED, cells), jnp.int16),
        ),
        in_specs=[smem] + [vmem] * 4,
        out_specs=(vmem, vmem),
        scratch_shapes=[
            pltpu.VMEM((2,) + before.shape[1:], jnp.bfloat16),
            pltpu.VMEM((16, cells), jnp.float32),
        ],
        input_output_aliases={4: 0},
        compiler_params=pltpu.CompilerParams(vmem_limit_bytes=32 * MIB),
        cost_estimate=LITTLE,
    )(ends, before, after, w, acc)


def code_kernel(jobs, acc, *refs):
    arrays, outs, exps = refs[: -1 - len(jobs)], refs[-1 - len(jobs) : -1], refs[-1]
    for parts, out in zip(jobs, outs):
        for at, (unit, takes) in enumerate(parts):
            coded = [(arrays[a], i, scales(arrays[a], i)) for a, i in takes]
            code_half(acc, unit, coded, exps, out, at)


def code(acc, jobs, arrays):
    cells = acc.shape[2]
    vmem = pl.BlockSpec(memory_space=pltpu.VMEM)
    return pl.pallas_call(
        functools.partial(code_kernel, jobs),
        out_shape=tuple(
            jax.ShapeDtypeStruct((len(parts), CODED, cells), jnp.int16) for parts in jobs
        ),
        in_specs=[vmem] * (1 + len(arrays)),
        out_specs=(vmem,) * len(jobs),
        scratch_shapes=[pltpu.VMEM((16, cells), jnp.float32)],
        compiler_params=pltpu.CompilerParams(vmem_limit_bytes=32 * MIB),
        cost_estimate=LITTLE,
    )(acc, *arrays)


def code_near_kernel(acc, near_ref, exps):
    @pl.loop(0, 8)
    def _(i):
        code_half(acc, 16 + i, [], exps, near_ref, i)


def code_near(acc):
    cells = acc.shape[2]
    vmem = pl.BlockSpec(memory_space=pltpu.VMEM)
    return pl.pallas_call(
        code_near_kernel,
        out_shape=jax.ShapeDtypeStruct((8, CODED, cells), jnp.int16),
        in_specs=[vmem],
        out_specs=vmem,
        scratch_shapes=[pltpu.VMEM((16, cells), jnp.float32)],
        compiler_params=pltpu.CompilerParams(vmem_limit_bytes=32 * MIB),
        cost_estimate=LITTLE,
    )(acc)


def lift_kernel(index_ref, frac_ref, after, left):
    high = VARS * LEV
    row = lax.broadcasted_iota(jnp.int32, (high, ROWS), 0)
    col = lax.broadcasted_iota(jnp.int32, (high, ROWS), 1)
    level = row % LEV
    lift = jnp.zeros((high, ROWS), jnp.float32)
    for j in range(LEVT):
        at, frac = index_ref[j], frac_ref[j]
        here = jnp.where(level == at, 1.0 - frac, jnp.where(level == at + 1, frac, 0.0))
        lift = jnp.where(col % LEVT == j, here, lift)
    lift = jnp.where(row // LEV == col // LEVT, lift, 0.0)
    high_part = lift.astype(jnp.bfloat16)
    low_part = (lift - high_part.astype(jnp.float32)).astype(jnp.bfloat16)
    left[...] = jnp.concatenate([high_part, high_part, low_part, low_part], axis=1)


def lift_matrix(lev_index, lev_frac, after):
    smem = pl.BlockSpec(memory_space=pltpu.SMEM)
    vmem = pl.BlockSpec(memory_space=pltpu.VMEM)
    return pl.pallas_call(
        lift_kernel,
        out_shape=jax.ShapeDtypeStruct((VARS * LEV, 4 * ROWS), jnp.bfloat16),
        in_specs=[smem, smem, vmem],
        out_specs=vmem,
        compiler_params=pltpu.CompilerParams(vmem_limit_bytes=4 * MIB),
        cost_estimate=LITTLE,
    )(lev_index, lev_frac, after)


def finish_kernel(half, takes, left, acc, *refs):
    arrays, out_hbm, out, sems = refs[:-3], refs[-3], refs[-2], refs[-1]
    coded = [(arrays[a], i, scales(arrays[a], i)) for a, i in takes]
    copies = []
    for b in range(HALF):
        total = acc[half * HALF + b]
        for r, i, s in coded:
            total = total + decode(r, i, s, b)
        first = total.astype(jnp.bfloat16)
        second = (total - first.astype(jnp.float32)).astype(jnp.bfloat16)
        right = jnp.concatenate([first, second, first, second], axis=0)
        out[b] = jnp.dot(left[...], right, preferred_element_type=jnp.float32)
        if b % 4 == 3:
            copy = pltpu.make_async_copy(
                out.at[pl.ds(b - 3, 4)],
                out_hbm.at[pl.ds(half * HALF + b - 3, 4)],
                sems.at[b // 4],
            )
            copy.start()
            copies.append(copy)
    for copy in copies:
        copy.wait()


def finish(half, left, acc, takes, arrays, begun=None):
    cells = acc.shape[2]
    vmem = pl.BlockSpec(memory_space=pltpu.VMEM)
    hbm = pl.BlockSpec(memory_space=pltpu.HBM)
    extra = () if begun is None else (begun,)
    return pl.pallas_call(
        functools.partial(finish_kernel, half, takes),
        out_shape=jax.ShapeDtypeStruct((SB, VARS * LEV, cells), jnp.float32),
        in_specs=[vmem] * (2 + len(arrays)) + [hbm] * len(extra),
        out_specs=hbm,
        scratch_shapes=[
            pltpu.VMEM((HALF, VARS * LEV, cells), jnp.float32),
            pltpu.SemaphoreType.DMA((HALF // 4,)),
        ],
        input_output_aliases={2 + len(arrays): 0} if extra else {},
        compiler_params=pltpu.CompilerParams(vmem_limit_bytes=32 * MIB),
        cost_estimate=LITTLE,
    )(left, acc, *arrays, *extra)


def ring(peers):
    up = [(i, (i + 1) % peers) for i in range(peers)]
    return up, [(j, i) for i, j in up]


def swap(value, bits, peers):
    return lax.ppermute(value, "tile", [(i, i ^ bits) for i in range(peers)])


def staged(cotangent, weight, target_block, dest, source, count, lev_index, lev_frac):
    peers = 16
    me = lax.axis_index("tile").astype(jnp.int32).reshape(1)
    operands = (count, me, target_block, dest, source, cotangent, weight)
    up, down = ring(peers)
    before = lax.ppermute(cotangent[-1:], "tile", up)
    acc, w, cot, low, ends = products_call(ahead_kernel, operands, (), cotangent[:1], MUCH)
    after = lax.ppermute(low, "tile", down)
    acc, w, cot, ends = products_call(rest_kernel, operands, (ends, acc, w, cot), None, LITTLE)
    acc, far = add_ends(ends, before, after, w, acc)
    far = swap(far, 1, peers)
    near = swap(code_near(acc), 1, peers)
    y3 = code(acc, (((14, ((0, 6),)),), ((15, ((0, 7),)),)), (far,))
    y3_own = y3[0]
    y3 = [swap(v, 2, peers) for v in y3]
    y2 = code(acc, (((12, ((0, 4),)),), ((13, ((0, 5),)),)), (far, y3_own))
    y2_own = y2[0]
    y2 = [swap(v, 2, peers) for v in y2]
    (a3_low,) = code(acc, (((6, ((0, 6), (1, 0))),),), (near, y3[0], far))
    (a3_high,) = code(acc, (((7, ((0, 7), (1, 0))),),), (near, y3[1], a3_low))
    a3 = [swap(a3_low, 4, peers), swap(a3_high, 4, peers)]
    (y1_own,) = code(acc, (((10, ((0, 2),)), (11, ((0, 3),))),), (far, y2_own))
    o1 = swap(y1_own, 4, peers)
    (b2_low,) = code(acc, (((4, ((0, 4), (1, 0), (2, 0))),),), (near, y2[0], a3[0], y1_own))
    (b2_high,) = code(acc, (((5, ((0, 5), (1, 0), (2, 0))),),), (near, y2[1], a3[1], b2_low))
    b2 = [swap(b2_low, 8, peers), swap(b2_high, 8, peers)]
    (y0_own,) = code(acc, (((8, ((0, 0), (1, 0))), (9, ((0, 1), (1, 1)))),), (far, o1, a3[0]))
    y0 = swap(y0_own, 2, peers)
    (a1_own,) = code(acc, (((2, ((0, 2),)), (3, ((0, 3),))),), (near, y1_own))
    a1 = swap(a1_own, 4, peers)
    left = lift_matrix(lev_index, lev_frac, b2_low)
    out = finish(0, left, acc, ((0, 0), (1, 0), (2, 0), (3, 0)), (near, y0, a1, b2[0]))
    return finish(1, left, acc, ((0, 1), (1, 1), (2, 1), (3, 0)), (near, y0, a1, b2[1]), out)


def vertical_matrix(lev_index, lev_frac, levels):
    columns = jnp.arange(levels)[None, :]
    lower = (columns == lev_index[:, None]).astype(jnp.float32)
    upper = (columns == lev_index[:, None] + 1).astype(jnp.float32)
    return (1.0 - lev_frac)[:, None] * lower + lev_frac[:, None] * upper


def slotted(cotangent, weight, target_block, dest, source, count, lev_index, lev_frac):
    peers = lax.axis_size("tile")
    entries, _, cells = weight.shape
    capacity = max(2, 2 * entries // peers)
    slots = peers * capacity
    up, down = ring(peers)
    before = lax.ppermute(cotangent[-1:], "tile", up)
    after = lax.ppermute(cotangent[:1], "tile", down)
    window = jnp.concatenate([before, cotangent, after], axis=0)
    contrib = jnp.einsum(
        "ofp,ops->ofs", window[target_block[0]], weight, preferred_element_type=jnp.float32
    )
    live = jnp.arange(entries) < count[0]
    matches = ((dest[0][:, None] == jnp.arange(peers)[None, :]) & live[:, None]).astype(jnp.int32)
    rank = jnp.sum(matches * jnp.cumsum(matches, axis=0), axis=1) - 1
    slot = jnp.where(live, dest[0] * capacity + rank, slots)
    labels = jnp.full((slots,), SB, jnp.int32).at[slot].set(source[0], mode="drop")
    outgoing = jnp.zeros((slots, ROWS, cells), jnp.float32).at[slot].set(contrib, mode="drop")
    arrived = lax.all_to_all(outgoing, "tile", split_axis=0, concat_axis=0, tiled=True)
    arrived_labels = lax.all_to_all(labels, "tile", split_axis=0, concat_axis=0, tiled=True)
    chooser = (jnp.arange(SB)[:, None] == arrived_labels[None, :]).astype(jnp.float32)
    summed = jnp.einsum("br,rfs->bfs", chooser, arrived, precision=lax.Precision.HIGHEST)
    lifted = jnp.einsum(
        "jl,bvjs->bvls",
        vertical_matrix(lev_index, lev_frac, LEV),
        summed.reshape(SB, VARS, LEVT, cells),
        precision=lax.Precision.HIGHEST,
    )
    return lifted.reshape(SB, VARS * LEV, cells)


def solution(mesh):
    placed = (
        P(("grp", "tile"), None, None),
        P("tile", None, None),
        P("tile", None),
        P("tile", None),
        P("tile", None),
        P("tile"),
        P(),
        P(),
    )
    return jax.shard_map(
        staged if mesh.shape["tile"] == 16 else slotted,
        mesh=mesh,
        in_specs=placed,
        out_specs=P(("grp", "tile"), None, None),
        check_vma=False,
    )
```

```python
import functools

import jax
import jax.numpy as jnp
from jax import lax
from jax.experimental import pallas as pl
from jax.experimental.pallas import tpu as pltpu
from jax.sharding import PartitionSpec as P

VARS = 6
LEV = 20
LEVT = 8
SB = 16
ROWS = VARS * LEVT
HALF = SB // 2
BODY = HALF * ROWS
CODED = BODY + 16
GROUP = 16
MIB = 1 << 20
LITTLE = pl.CostEstimate(flops=1, bytes_accessed=1, transcendentals=0)
MUCH = pl.CostEstimate(flops=1 << 28, bytes_accessed=12 * MIB, transcendentals=0)


def encode(read, write, exps):
    exps[HALF:, :] = jnp.zeros((16 - HALF, exps.shape[1]), jnp.float32)
    for b in range(HALF):
        x = read(b)
        top = jnp.max(jnp.abs(x), axis=0, keepdims=True)
        e = jnp.ceil(jnp.log2(jnp.maximum(top, 1e-30)) + 0.001) - 15.0
        exps[b : b + 1, :] = e
        q = jnp.round(x * jnp.exp2(-e))
        write(b * ROWS, ROWS, q.astype(jnp.int32).astype(jnp.int16))
    write(BODY, 16, exps[...].astype(jnp.int32).astype(jnp.int16))


def scales(ref, i):
    return jnp.exp2(ref[i, BODY:CODED, :].astype(jnp.int32).astype(jnp.float32))


def decode(ref, i, scale, b):
    q = ref[i, b * ROWS : (b + 1) * ROWS, :].astype(jnp.int32).astype(jnp.float32)
    return q * scale[b : b + 1, :]


TRASH = 16 * SB


def add_group(g, count, me, tables, cot, w, acc, ends, add, listing):
    blocks = cot.shape[0]
    n = ends[3, 0] if listing else None
    for i in range(GROUP):
        k = g * GROUP + i
        block = tables[0, k]
        rel = tables[1, k] ^ me
        slot = (rel & 1) * 8 + ((rel >> 1) & 1) * 4 + (rel >> 2)
        live = k < count
        at = jnp.where(live, slot * SB + tables[2, k], TRASH)
        outer = (block == 0) | (block == blocks + 1)
        if listing:
            ends[0, n] = k
            ends[1, n] = at
            ends[2, n] = jnp.where(block == 0, 0, 1)
            n = n + (outer & live).astype(jnp.int32)
        if add:
            at = jnp.where(outer, TRASH, at)
            left = cot[jnp.clip(block - 1, 0, blocks - 1)]
            acc[at] = acc[at] + jnp.dot(left, w[k], preferred_element_type=jnp.float32)
    if listing:
        ends[3, 0] = n


def groups_of(count):
    used = (count + GROUP - 1) // GROUP
    return used, (used + 1) // 2


def load(used, pairs, w_hbm, w, acc, sems, w_sems):
    def w_copy(g):
        part = pl.ds(g * GROUP, GROUP)
        return pltpu.make_async_copy(w_hbm.at[part], w.at[part], w_sems.at[g])

    small = [pltpu.make_async_copy(a, b, sems.at[i]) for i, (a, b) in enumerate(pairs)]
    for copy in small:
        copy.start()
    for g in range(w.shape[0] // GROUP):

        @pl.when(g < used)
        def _():
            w_copy(g).start()

    @pl.loop(0, TRASH, unroll=8)
    def _(b):
        acc[b] = jnp.zeros(acc.shape[1:], jnp.float32)

    acc[TRASH] = jnp.zeros(acc.shape[1:], jnp.float32)
    for copy in small:
        copy.wait()
    return w_copy


def ahead_kernel(
    count_ref, me_ref, tb, dest, src, cot_hbm, w_hbm, low_in, acc, w, cot, low, *scratch
):
    tables, sems, w_sems = scratch
    used, half = groups_of(count_ref[0])
    low[...] = low_in[...]

    @pl.when(me_ref[0] == 0)
    def _():
        pairs = [(cot_hbm, cot)]
        pairs += [(t, tables.at[pl.ds(i, 1)]) for i, t in enumerate((tb, dest, src))]
        w_copy = load(used, pairs, w_hbm, w, acc, sems, w_sems)
        for g in range(w.shape[0] // GROUP):

            @pl.when(g < used)
            def _():
                w_copy(g).wait()

            @pl.when(g < half)
            def _():
                add_group(g, count_ref[0], me_ref[0], tables, cot, w, acc, None, True, False)


def rest_kernel(count_ref, me_ref, tb, dest, src, cot_hbm, w_hbm, acc_in, w_in, cot_in, *refs):
    acc, w, cot, ends, tables, sems, w_sems = refs
    used, half = groups_of(count_ref[0])
    early = me_ref[0] == 0
    done = jnp.where(early, half, 0)
    ends[3, 0] = 0
    three = [(t, tables.at[pl.ds(i, 1)]) for i, t in enumerate((tb, dest, src))]

    @pl.when(early)
    def _():
        small = [pltpu.make_async_copy(a, b, sems.at[i]) for i, (a, b) in enumerate(three)]
        for copy in small:
            copy.start()
        for copy in small:
            copy.wait()

    @pl.when(jnp.logical_not(early))
    def _():
        load(used, three + [(cot_hbm, cot)], w_hbm, w, acc, sems, w_sems)

    @pl.loop(0, done)
    def _(g):
        add_group(g, count_ref[0], me_ref[0], tables, cot, w, acc, ends, False, True)

    for g in range(w.shape[0] // GROUP):

        @pl.when(jnp.logical_not(early) & (g < used))
        def _():
            part = pl.ds(g * GROUP, GROUP)
            pltpu.make_async_copy(w_hbm.at[part], w.at[part], w_sems.at[g]).wait()

        @pl.when((g >= done) & (g < used))
        def _():
            add_group(g, count_ref[0], me_ref[0], tables, cot, w, acc, ends, True, True)

    listed = ends[3, 0]
    for i in range(8):
        ends[0, listed + i] = 0
        ends[1, listed + i] = TRASH
        ends[2, listed + i] = 0


def in_hbm(x):
    return pltpu.with_memory_space_constraint(x, pltpu.HBM)


def products_call(kernel, operands, given, low, cost):
    cotangent, weight = operands[5], operands[6]
    entries, _, cells = weight.shape
    smem = pl.BlockSpec(memory_space=pltpu.SMEM)
    vmem = pl.BlockSpec(memory_space=pltpu.VMEM)
    hbm = pl.BlockSpec(memory_space=pltpu.HBM)
    results = [
        jax.ShapeDtypeStruct((TRASH + 1, ROWS, cells), jnp.float32),
        jax.ShapeDtypeStruct(weight.shape, weight.dtype),
        jax.ShapeDtypeStruct(cotangent.shape, cotangent.dtype),
    ]
    first = not given
    last = low if first else jax.ShapeDtypeStruct((4, entries + 8), jnp.int32)
    results.append(jax.ShapeDtypeStruct(last.shape, last.dtype))
    return pl.pallas_call(
        kernel,
        out_shape=tuple(results),
        in_specs=[smem, smem] + [hbm] * 5 + [vmem] * (1 if first else 3),
        out_specs=(vmem,) * 3 + (vmem if first else smem,),
        scratch_shapes=[
            pltpu.SMEM((3, entries), jnp.int32),
            pltpu.SemaphoreType.DMA((4,)),
            pltpu.SemaphoreType.DMA((entries // GROUP,)),
        ],
        input_output_aliases={} if first else {7: 0, 8: 1, 9: 2},
        compiler_params=pltpu.CompilerParams(vmem_limit_bytes=24 * MIB),
        cost_estimate=cost,
    )(*operands[:2], *[in_hbm(x) for x in operands[2:]], *([low] if first else given))


def code_half(acc, unit, coded, exps, out_ref, at):
    def read(b):
        total = acc[unit * HALF + b]
        for r, i, s in coded:
            total = total + decode(r, i, s, b)
        return total

    def write(row, rows, value):
        out_ref[at, row : row + rows, :] = value

    encode(read, write, exps)


def ends_kernel(ends, before, after, w, acc_in, acc, far_ref, sides, exps):
    sides[0] = before[0]
    sides[1] = after[0]

    @pl.loop(0, (ends[3, 0] + 7) // 8)
    def _(part):
        for i in range(8):
            k = part * 8 + i
            at = ends[1, k]
            left = sides[ends[2, k]]
            acc[at] = acc[at] + jnp.dot(left, w[ends[0, k]], preferred_element_type=jnp.float32)

    @pl.loop(0, 8)
    def _(i):
        code_half(acc, 24 + i, [], exps, far_ref, i)


def add_ends(ends, before, after, w, acc):
    cells = acc.shape[2]
    smem = pl.BlockSpec(memory_space=pltpu.SMEM)
    vmem = pl.BlockSpec(memory_space=pltpu.VMEM)
    return pl.pallas_call(
        ends_kernel,
        out_shape=(
            jax.ShapeDtypeStruct(acc.shape, jnp.float32),
            jax.ShapeDtypeStruct((8, CODED, cells), jnp.int16),
        ),
        in_specs=[smem] + [vmem] * 4,
        out_specs=(vmem, vmem),
        scratch_shapes=[
            pltpu.VMEM((2,) + before.shape[1:], jnp.bfloat16),
            pltpu.VMEM((16, cells), jnp.float32),
        ],
        input_output_aliases={4: 0},
        compiler_params=pltpu.CompilerParams(vmem_limit_bytes=32 * MIB),
        cost_estimate=LITTLE,
    )(ends, before, after, w, acc)


def code_kernel(jobs, acc, *refs):
    arrays, outs, exps = refs[: -1 - len(jobs)], refs[-1 - len(jobs) : -1], refs[-1]
    for parts, out in zip(jobs, outs):
        for at, (unit, takes) in enumerate(parts):
            coded = [(arrays[a], i, scales(arrays[a], i)) for a, i in takes]
            code_half(acc, unit, coded, exps, out, at)


def code(acc, jobs, arrays):
    cells = acc.shape[2]
    vmem = pl.BlockSpec(memory_space=pltpu.VMEM)
    return pl.pallas_call(
        functools.partial(code_kernel, jobs),
        out_shape=tuple(
            jax.ShapeDtypeStruct((len(parts), CODED, cells), jnp.int16) for parts in jobs
        ),
        in_specs=[vmem] * (1 + len(arrays)),
        out_specs=(vmem,) * len(jobs),
        scratch_shapes=[pltpu.VMEM((16, cells), jnp.float32)],
        compiler_params=pltpu.CompilerParams(vmem_limit_bytes=32 * MIB),
        cost_estimate=LITTLE,
    )(acc, *arrays)


def code_near_kernel(acc, near_ref, exps):
    @pl.loop(0, 8)
    def _(i):
        code_half(acc, 16 + i, [], exps, near_ref, i)


def code_near(acc):
    cells = acc.shape[2]
    vmem = pl.BlockSpec(memory_space=pltpu.VMEM)
    return pl.pallas_call(
        code_near_kernel,
        out_shape=jax.ShapeDtypeStruct((8, CODED, cells), jnp.int16),
        in_specs=[vmem],
        out_specs=vmem,
        scratch_shapes=[pltpu.VMEM((16, cells), jnp.float32)],
        compiler_params=pltpu.CompilerParams(vmem_limit_bytes=32 * MIB),
        cost_estimate=LITTLE,
    )(acc)


def lift_kernel(index_ref, frac_ref, after, left):
    high = VARS * LEV
    row = lax.broadcasted_iota(jnp.int32, (high, ROWS), 0)
    col = lax.broadcasted_iota(jnp.int32, (high, ROWS), 1)
    level = row % LEV
    lift = jnp.zeros((high, ROWS), jnp.float32)
    for j in range(LEVT):
        at, frac = index_ref[j], frac_ref[j]
        here = jnp.where(level == at, 1.0 - frac, jnp.where(level == at + 1, frac, 0.0))
        lift = jnp.where(col % LEVT == j, here, lift)
    lift = jnp.where(row // LEV == col // LEVT, lift, 0.0)
    high_part = lift.astype(jnp.bfloat16)
    low_part = (lift - high_part.astype(jnp.float32)).astype(jnp.bfloat16)
    left[...] = jnp.concatenate([high_part, high_part, low_part, low_part], axis=1)


def lift_matrix(lev_index, lev_frac, after):
    smem = pl.BlockSpec(memory_space=pltpu.SMEM)
    vmem = pl.BlockSpec(memory_space=pltpu.VMEM)
    return pl.pallas_call(
        lift_kernel,
        out_shape=jax.ShapeDtypeStruct((VARS * LEV, 4 * ROWS), jnp.bfloat16),
        in_specs=[smem, smem, vmem],
        out_specs=vmem,
        compiler_params=pltpu.CompilerParams(vmem_limit_bytes=4 * MIB),
        cost_estimate=LITTLE,
    )(lev_index, lev_frac, after)


def finish_kernel(half, takes, left, acc, *refs):
    arrays, out_hbm, out, sems = refs[:-3], refs[-3], refs[-2], refs[-1]
    coded = [(arrays[a], i, scales(arrays[a], i)) for a, i in takes]
    copies = []
    for b in range(HALF):
        total = acc[half * HALF + b]
        for r, i, s in coded:
            total = total + decode(r, i, s, b)
        first = total.astype(jnp.bfloat16)
        second = (total - first.astype(jnp.float32)).astype(jnp.bfloat16)
        right = jnp.concatenate([first, second, first, second], axis=0)
        out[b] = jnp.dot(left[...], right, preferred_element_type=jnp.float32)
        if b % 4 == 3:
            copy = pltpu.make_async_copy(
                out.at[pl.ds(b - 3, 4)],
                out_hbm.at[pl.ds(half * HALF + b - 3, 4)],
                sems.at[b // 4],
            )
            copy.start()
            copies.append(copy)
    for copy in copies:
        copy.wait()


def finish(half, left, acc, takes, arrays, begun=None):
    cells = acc.shape[2]
    vmem = pl.BlockSpec(memory_space=pltpu.VMEM)
    hbm = pl.BlockSpec(memory_space=pltpu.HBM)
    extra = () if begun is None else (begun,)
    return pl.pallas_call(
        functools.partial(finish_kernel, half, takes),
        out_shape=jax.ShapeDtypeStruct((SB, VARS * LEV, cells), jnp.float32),
        in_specs=[vmem] * (2 + len(arrays)) + [hbm] * len(extra),
        out_specs=hbm,
        scratch_shapes=[
            pltpu.VMEM((HALF, VARS * LEV, cells), jnp.float32),
            pltpu.SemaphoreType.DMA((HALF // 4,)),
        ],
        input_output_aliases={2 + len(arrays): 0} if extra else {},
        compiler_params=pltpu.CompilerParams(vmem_limit_bytes=32 * MIB),
        cost_estimate=pl.CostEstimate(flops=1, bytes_accessed=4194304, transcendentals=0),
    )(left, acc, *arrays, *extra)


def ring(peers):
    up = [(i, (i + 1) % peers) for i in range(peers)]
    return up, [(j, i) for i, j in up]


def swap(value, bits, peers):
    return lax.ppermute(value, "tile", [(i, i ^ bits) for i in range(peers)])


def staged(cotangent, weight, target_block, dest, source, count, lev_index, lev_frac):
    peers = 16
    me = lax.axis_index("tile").astype(jnp.int32).reshape(1)
    operands = (count, me, target_block, dest, source, cotangent, weight)
    up, down = ring(peers)
    before = lax.ppermute(cotangent[-1:], "tile", up)
    acc, w, cot, low = products_call(ahead_kernel, operands, (), cotangent[:1], MUCH)
    after = lax.ppermute(low, "tile", down)
    acc, w, cot, ends = products_call(rest_kernel, operands, (acc, w, cot), None, LITTLE)
    acc, far = add_ends(ends, before, after, w, acc)
    far = swap(far, 1, peers)
    near = swap(code_near(acc), 1, peers)
    y3 = code(acc, (((14, ((0, 6),)),), ((15, ((0, 7),)),)), (far,))
    y3_own = y3[0]
    y3 = [swap(v, 2, peers) for v in y3]
    y2 = code(acc, (((12, ((0, 4),)),), ((13, ((0, 5),)),)), (far, y3_own))
    y2_own = y2[0]
    y2 = [swap(v, 2, peers) for v in y2]
    (a3_low,) = code(acc, (((6, ((0, 6), (1, 0))),),), (near, y3[0], far))
    (a3_high,) = code(acc, (((7, ((0, 7), (1, 0))),),), (near, y3[1], a3_low))
    a3 = [swap(a3_low, 4, peers), swap(a3_high, 4, peers)]
    (y1_own,) = code(acc, (((10, ((0, 2),)), (11, ((0, 3),))),), (far, y2_own))
    o1 = swap(y1_own, 4, peers)
    (b2_low,) = code(acc, (((4, ((0, 4), (1, 0), (2, 0))),),), (near, y2[0], a3[0], far))
    (b2_high,) = code(acc, (((5, ((0, 5), (1, 0), (2, 0))),),), (near, y2[1], a3[1], b2_low))
    b2 = [swap(b2_low, 8, peers), swap(b2_high, 8, peers)]
    y0_own = code(acc, (((8, ((0, 0), (1, 0))),), ((9, ((0, 1), (1, 1))),)), (far, o1, b2_low))
    y0 = [swap(v, 2, peers) for v in y0_own]
    y0_own = y0_own[0]
    (a1_own,) = code(acc, (((2, ((0, 2),)), (3, ((0, 3),))),), (near, a3_high))
    a1 = swap(a1_own, 4, peers)
    left = lift_matrix(lev_index, lev_frac, b2_high)
    out = finish(0, left, acc, ((0, 0), (1, 0), (2, 0), (3, 0)), (near, y0[0], a1, b2[0]))
    return finish(1, left, acc, ((0, 1), (1, 0), (2, 1), (3, 0)), (near, y0[1], a1, b2[1]), out)


def vertical_matrix(lev_index, lev_frac, levels):
    columns = jnp.arange(levels)[None, :]
    lower = (columns == lev_index[:, None]).astype(jnp.float32)
    upper = (columns == lev_index[:, None] + 1).astype(jnp.float32)
    return (1.0 - lev_frac)[:, None] * lower + lev_frac[:, None] * upper


def slotted(cotangent, weight, target_block, dest, source, count, lev_index, lev_frac):
    peers = lax.axis_size("tile")
    entries, _, cells = weight.shape
    capacity = max(2, 2 * entries // peers)
    slots = peers * capacity
    up, down = ring(peers)
    before = lax.ppermute(cotangent[-1:], "tile", up)
    after = lax.ppermute(cotangent[:1], "tile", down)
    window = jnp.concatenate([before, cotangent, after], axis=0)
    contrib = jnp.einsum(
        "ofp,ops->ofs", window[target_block[0]], weight, preferred_element_type=jnp.float32
    )
    live = jnp.arange(entries) < count[0]
    matches = ((dest[0][:, None] == jnp.arange(peers)[None, :]) & live[:, None]).astype(jnp.int32)
    rank = jnp.sum(matches * jnp.cumsum(matches, axis=0), axis=1) - 1
    slot = jnp.where(live, dest[0] * capacity + rank, slots)
    labels = jnp.full((slots,), SB, jnp.int32).at[slot].set(source[0], mode="drop")
    outgoing = jnp.zeros((slots, ROWS, cells), jnp.float32).at[slot].set(contrib, mode="drop")
    arrived = lax.all_to_all(outgoing, "tile", split_axis=0, concat_axis=0, tiled=True)
    arrived_labels = lax.all_to_all(labels, "tile", split_axis=0, concat_axis=0, tiled=True)
    chooser = (jnp.arange(SB)[:, None] == arrived_labels[None, :]).astype(jnp.float32)
    summed = jnp.einsum("br,rfs->bfs", chooser, arrived, precision=lax.Precision.HIGHEST)
    lifted = jnp.einsum(
        "jl,bvjs->bvls",
        vertical_matrix(lev_index, lev_frac, LEV),
        summed.reshape(SB, VARS, LEVT, cells),
        precision=lax.Precision.HIGHEST,
    )
    return lifted.reshape(SB, VARS * LEV, cells)


def solution(mesh):
    placed = (
        P(("grp", "tile"), None, None),
        P("tile", None, None),
        P("tile", None),
        P("tile", None),
        P("tile", None),
        P("tile"),
        P(),
        P(),
    )
    return jax.shard_map(
        staged if mesh.shape["tile"] == 16 else slotted,
        mesh=mesh,
        in_specs=placed,
        out_specs=P(("grp", "tile"), None, None),
        check_vma=False,
    )
```

```python
import functools

import jax
import jax.numpy as jnp
from jax import lax
from jax.experimental import pallas as pl
from jax.experimental.pallas import tpu as pltpu
from jax.sharding import PartitionSpec as P

VARS = 6
LEV = 20
LEVT = 8
SB = 16
ROWS = VARS * LEVT
HALF = SB // 2
BODY = HALF * ROWS
CODED = BODY + 16
GROUP = 16
MIB = 1 << 20
LITTLE = pl.CostEstimate(flops=1, bytes_accessed=1, transcendentals=0)
MUCH = pl.CostEstimate(flops=1 << 28, bytes_accessed=12 * MIB, transcendentals=0)


def encode(read, write, exps):
    exps[HALF:, :] = jnp.zeros((16 - HALF, exps.shape[1]), jnp.float32)
    for b in range(HALF):
        x = read(b)
        top = jnp.max(jnp.abs(x), axis=0, keepdims=True)
        e = jnp.ceil(jnp.log2(jnp.maximum(top, 1e-30)) + 0.001) - 15.0
        exps[b : b + 1, :] = e
        q = jnp.round(x * jnp.exp2(-e))
        write(b * ROWS, ROWS, q.astype(jnp.int32).astype(jnp.int16))
    write(BODY, 16, exps[...].astype(jnp.int32).astype(jnp.int16))


def scales(ref, i):
    return jnp.exp2(ref[i, BODY:CODED, :].astype(jnp.int32).astype(jnp.float32))


def decode(ref, i, scale, b):
    q = ref[i, b * ROWS : (b + 1) * ROWS, :].astype(jnp.int32).astype(jnp.float32)
    return q * scale[b : b + 1, :]


TRASH = 16 * SB


def add_group(g, count, me, tables, cot, w, acc, ends, add, listing):
    blocks = cot.shape[0]
    n = ends[3, 0] if listing else None
    for i in range(GROUP):
        k = g * GROUP + i
        block = tables[0, k]
        rel = tables[1, k] ^ me
        slot = (rel & 1) * 8 + ((rel >> 1) & 1) * 4 + (rel >> 2)
        live = k < count
        at = jnp.where(live, slot * SB + tables[2, k], TRASH)
        outer = (block == 0) | (block == blocks + 1)
        if listing:
            ends[0, n] = k
            ends[1, n] = at
            ends[2, n] = jnp.where(block == 0, 0, 1)
            n = n + (outer & live).astype(jnp.int32)
        if add:
            at = jnp.where(outer, TRASH, at)
            left = cot[jnp.clip(block - 1, 0, blocks - 1)]
            acc[at] = acc[at] + jnp.dot(left, w[k], preferred_element_type=jnp.float32)
    if listing:
        ends[3, 0] = n


def groups_of(count):
    used = (count + GROUP - 1) // GROUP
    return used, (used + 1) // 2


def load(used, pairs, w_hbm, w, acc, sems, w_sems):
    def w_copy(g):
        part = pl.ds(g * GROUP, GROUP)
        return pltpu.make_async_copy(w_hbm.at[part], w.at[part], w_sems.at[g])

    small = [pltpu.make_async_copy(a, b, sems.at[i]) for i, (a, b) in enumerate(pairs)]
    for copy in small:
        copy.start()
    for g in range(w.shape[0] // GROUP):

        @pl.when(g < used)
        def _():
            w_copy(g).start()

    @pl.loop(0, TRASH, unroll=8)
    def _(b):
        acc[b] = jnp.zeros(acc.shape[1:], jnp.float32)

    acc[TRASH] = jnp.zeros(acc.shape[1:], jnp.float32)
    for copy in small:
        copy.wait()
    return w_copy


def ahead_kernel(
    count_ref, me_ref, tb, dest, src, cot_hbm, w_hbm, low_in, acc, w, cot, low, *scratch
):
    tables, sems, w_sems = scratch
    used, half = groups_of(count_ref[0])
    low[...] = low_in[...]

    @pl.when(me_ref[0] == 0)
    def _():
        pairs = [(cot_hbm, cot)]
        pairs += [(t, tables.at[pl.ds(i, 1)]) for i, t in enumerate((tb, dest, src))]
        w_copy = load(used, pairs, w_hbm, w, acc, sems, w_sems)
        for g in range(w.shape[0] // GROUP):

            @pl.when(g < used)
            def _():
                w_copy(g).wait()

            @pl.when(g < half)
            def _():
                add_group(g, count_ref[0], me_ref[0], tables, cot, w, acc, None, True, False)


def rest_kernel(count_ref, me_ref, tb, dest, src, cot_hbm, w_hbm, acc_in, w_in, cot_in, *refs):
    acc, w, cot, ends, tables, sems, w_sems = refs
    used, half = groups_of(count_ref[0])
    early = me_ref[0] == 0
    done = jnp.where(early, half, 0)
    ends[3, 0] = 0
    three = [(t, tables.at[pl.ds(i, 1)]) for i, t in enumerate((tb, dest, src))]

    @pl.when(early)
    def _():
        small = [pltpu.make_async_copy(a, b, sems.at[i]) for i, (a, b) in enumerate(three)]
        for copy in small:
            copy.start()
        for copy in small:
            copy.wait()

    @pl.when(jnp.logical_not(early))
    def _():
        load(used, three + [(cot_hbm, cot)], w_hbm, w, acc, sems, w_sems)

    @pl.loop(0, done)
    def _(g):
        add_group(g, count_ref[0], me_ref[0], tables, cot, w, acc, ends, False, True)

    for g in range(w.shape[0] // GROUP):

        @pl.when(jnp.logical_not(early) & (g < used))
        def _():
            part = pl.ds(g * GROUP, GROUP)
            pltpu.make_async_copy(w_hbm.at[part], w.at[part], w_sems.at[g]).wait()

        @pl.when((g >= done) & (g < used))
        def _():
            add_group(g, count_ref[0], me_ref[0], tables, cot, w, acc, ends, True, True)

    listed = ends[3, 0]
    for i in range(8):
        ends[0, listed + i] = 0
        ends[1, listed + i] = TRASH
        ends[2, listed + i] = 0


def in_hbm(x):
    return pltpu.with_memory_space_constraint(x, pltpu.HBM)


def products_call(kernel, operands, given, low, cost):
    cotangent, weight = operands[5], operands[6]
    entries, _, cells = weight.shape
    smem = pl.BlockSpec(memory_space=pltpu.SMEM)
    vmem = pl.BlockSpec(memory_space=pltpu.VMEM)
    hbm = pl.BlockSpec(memory_space=pltpu.HBM)
    results = [
        jax.ShapeDtypeStruct((TRASH + 1, ROWS, cells), jnp.float32),
        jax.ShapeDtypeStruct(weight.shape, weight.dtype),
        jax.ShapeDtypeStruct(cotangent.shape, cotangent.dtype),
    ]
    first = not given
    last = low if first else jax.ShapeDtypeStruct((4, entries + 8), jnp.int32)
    results.append(jax.ShapeDtypeStruct(last.shape, last.dtype))
    return pl.pallas_call(
        kernel,
        out_shape=tuple(results),
        in_specs=[smem, smem] + [hbm] * 5 + [vmem] * (1 if first else 3),
        out_specs=(vmem,) * 3 + (vmem if first else smem,),
        scratch_shapes=[
            pltpu.SMEM((3, entries), jnp.int32),
            pltpu.SemaphoreType.DMA((4,)),
            pltpu.SemaphoreType.DMA((entries // GROUP,)),
        ],
        input_output_aliases={} if first else {7: 0, 8: 1, 9: 2},
        compiler_params=pltpu.CompilerParams(vmem_limit_bytes=24 * MIB),
        cost_estimate=cost,
    )(*operands[:2], *[in_hbm(x) for x in operands[2:]], *([low] if first else given))


def code_half(acc, unit, coded, exps, out_ref, at):
    def read(b):
        total = acc[unit * HALF + b]
        for r, i, s in coded:
            total = total + decode(r, i, s, b)
        return total

    def write(row, rows, value):
        out_ref[at, row : row + rows, :] = value

    encode(read, write, exps)


def ends_kernel(ends, before, after, w, acc_in, acc, far_ref, sides, exps):
    sides[0] = before[0]
    sides[1] = after[0]

    @pl.loop(0, (ends[3, 0] + 7) // 8)
    def _(part):
        for i in range(8):
            k = part * 8 + i
            at = ends[1, k]
            left = sides[ends[2, k]]
            acc[at] = acc[at] + jnp.dot(left, w[ends[0, k]], preferred_element_type=jnp.float32)

    @pl.loop(0, 8)
    def _(i):
        code_half(acc, 24 + i, [], exps, far_ref, i)


def add_ends(ends, before, after, w, acc):
    cells = acc.shape[2]
    smem = pl.BlockSpec(memory_space=pltpu.SMEM)
    vmem = pl.BlockSpec(memory_space=pltpu.VMEM)
    return pl.pallas_call(
        ends_kernel,
        out_shape=(
            jax.ShapeDtypeStruct(acc.shape, jnp.float32),
            jax.ShapeDtypeStruct((8, CODED, cells), jnp.int16),
        ),
        in_specs=[smem] + [vmem] * 4,
        out_specs=(vmem, vmem),
        scratch_shapes=[
            pltpu.VMEM((2,) + before.shape[1:], jnp.bfloat16),
            pltpu.VMEM((16, cells), jnp.float32),
        ],
        input_output_aliases={4: 0},
        compiler_params=pltpu.CompilerParams(vmem_limit_bytes=32 * MIB),
        cost_estimate=LITTLE,
    )(ends, before, after, w, acc)


def taken(takes, arrays, me):
    for a, i, *pair in takes:
        if pair:
            i = i + pair[0] * jnp.where(me & pair[1], 0, 1)
        yield arrays[a], i, scales(arrays[a], i)


def code_kernel(jobs, me, acc, *refs):
    arrays, outs, exps = refs[: -1 - len(jobs)], refs[-1 - len(jobs) : -1], refs[-1]
    for parts, out in zip(jobs, outs):
        for at, (unit, takes) in enumerate(parts):
            coded = list(taken(takes, arrays, me[0]))
            code_half(acc, unit, coded, exps, out, at)


def code(me, acc, jobs, arrays):
    cells = acc.shape[2]
    smem = pl.BlockSpec(memory_space=pltpu.SMEM)
    vmem = pl.BlockSpec(memory_space=pltpu.VMEM)
    return pl.pallas_call(
        functools.partial(code_kernel, jobs),
        out_shape=tuple(
            jax.ShapeDtypeStruct((len(parts), CODED, cells), jnp.int16) for parts in jobs
        ),
        in_specs=[smem] + [vmem] * (1 + len(arrays)),
        out_specs=(vmem,) * len(jobs),
        scratch_shapes=[pltpu.VMEM((16, cells), jnp.float32)],
        compiler_params=pltpu.CompilerParams(vmem_limit_bytes=32 * MIB),
        cost_estimate=LITTLE,
    )(me, acc, *arrays)


def code_near_kernel(acc, near_ref, exps):
    @pl.loop(0, 8)
    def _(i):
        code_half(acc, 16 + i, [], exps, near_ref, i)


def code_near(acc):
    cells = acc.shape[2]
    vmem = pl.BlockSpec(memory_space=pltpu.VMEM)
    return pl.pallas_call(
        code_near_kernel,
        out_shape=jax.ShapeDtypeStruct((8, CODED, cells), jnp.int16),
        in_specs=[vmem],
        out_specs=vmem,
        scratch_shapes=[pltpu.VMEM((16, cells), jnp.float32)],
        compiler_params=pltpu.CompilerParams(vmem_limit_bytes=32 * MIB),
        cost_estimate=LITTLE,
    )(acc)


def lift_kernel(index_ref, frac_ref, after, left):
    high = VARS * LEV
    row = lax.broadcasted_iota(jnp.int32, (high, ROWS), 0)
    col = lax.broadcasted_iota(jnp.int32, (high, ROWS), 1)
    level = row % LEV
    lift = jnp.zeros((high, ROWS), jnp.float32)
    for j in range(LEVT):
        at, frac = index_ref[j], frac_ref[j]
        here = jnp.where(level == at, 1.0 - frac, jnp.where(level == at + 1, frac, 0.0))
        lift = jnp.where(col % LEVT == j, here, lift)
    lift = jnp.where(row // LEV == col // LEVT, lift, 0.0)
    high_part = lift.astype(jnp.bfloat16)
    low_part = (lift - high_part.astype(jnp.float32)).astype(jnp.bfloat16)
    left[...] = jnp.concatenate([high_part, high_part, low_part, low_part], axis=1)


def lift_matrix(lev_index, lev_frac, after):
    smem = pl.BlockSpec(memory_space=pltpu.SMEM)
    vmem = pl.BlockSpec(memory_space=pltpu.VMEM)
    return pl.pallas_call(
        lift_kernel,
        out_shape=jax.ShapeDtypeStruct((VARS * LEV, 4 * ROWS), jnp.bfloat16),
        in_specs=[smem, smem, vmem],
        out_specs=vmem,
        compiler_params=pltpu.CompilerParams(vmem_limit_bytes=4 * MIB),
        cost_estimate=LITTLE,
    )(lev_index, lev_frac, after)


def finish_kernel(half, takes, me, left, acc, *refs):
    arrays, out_hbm, out, sems = refs[:-3], refs[-3], refs[-2], refs[-1]
    coded = list(taken(takes, arrays, me[0]))
    copies = []
    for b in range(HALF):
        total = acc[half * HALF + b]
        for r, i, s in coded:
            total = total + decode(r, i, s, b)
        first = total.astype(jnp.bfloat16)
        second = (total - first.astype(jnp.float32)).astype(jnp.bfloat16)
        right = jnp.concatenate([first, second, first, second], axis=0)
        out[b] = jnp.dot(left[...], right, preferred_element_type=jnp.float32)
        if b % 4 == 3:
            copy = pltpu.make_async_copy(
                out.at[pl.ds(b - 3, 4)],
                out_hbm.at[pl.ds(half * HALF + b - 3, 4)],
                sems.at[b // 4],
            )
            copy.start()
            copies.append(copy)
    for copy in copies:
        copy.wait()


def finish(half, me, left, acc, takes, arrays, begun=None):
    cells = acc.shape[2]
    smem = pl.BlockSpec(memory_space=pltpu.SMEM)
    vmem = pl.BlockSpec(memory_space=pltpu.VMEM)
    hbm = pl.BlockSpec(memory_space=pltpu.HBM)
    extra = () if begun is None else (begun,)
    return pl.pallas_call(
        functools.partial(finish_kernel, half, takes),
        out_shape=jax.ShapeDtypeStruct((SB, VARS * LEV, cells), jnp.float32),
        in_specs=[smem] + [vmem] * (2 + len(arrays)) + [hbm] * len(extra),
        out_specs=hbm,
        scratch_shapes=[
            pltpu.VMEM((HALF, VARS * LEV, cells), jnp.float32),
            pltpu.SemaphoreType.DMA((HALF // 4,)),
        ],
        input_output_aliases={3 + len(arrays): 0} if extra else {},
        compiler_params=pltpu.CompilerParams(vmem_limit_bytes=32 * MIB),
        cost_estimate=LITTLE,
    )(me, left, acc, *arrays, *extra)


def ring(peers):
    up = [(i, (i + 1) % peers) for i in range(peers)]
    return up, [(j, i) for i, j in up]


def both(value, bits, peers):
    pairs = [[i, i ^ bits] for i in range(peers) if not i & bits]
    return lax.all_gather(value, "tile", axis_index_groups=pairs, tiled=True)


def swap(value, bits, peers):
    return lax.ppermute(value, "tile", [(i, i ^ bits) for i in range(peers)])


def staged(cotangent, weight, target_block, dest, source, count, lev_index, lev_frac):
    peers = 16
    me = lax.axis_index("tile").astype(jnp.int32).reshape(1)
    operands = (count, me, target_block, dest, source, cotangent, weight)
    up, down = ring(peers)
    before = lax.ppermute(cotangent[-1:], "tile", up)
    acc, w, cot, low = products_call(ahead_kernel, operands, (), cotangent[:1], MUCH)
    after = lax.ppermute(low, "tile", down)
    acc, w, cot, ends = products_call(rest_kernel, operands, (acc, w, cot), None, LITTLE)
    acc, far = add_ends(ends, before, after, w, acc)
    far = swap(far, 1, peers)
    near = swap(code_near(acc), 1, peers)
    add = functools.partial(code, me, acc)
    y3 = add((((14, ((0, 6),)),), ((15, ((0, 7),)),)), (far,))
    y3_own = y3[0]
    y3 = [swap(v, 2, peers) for v in y3]
    (o1_own,) = add((((10, ((0, 2),)), (11, ((0, 3),))),), (far, y3_own))
    o1 = both(o1_own, 4, peers)
    y2 = add((((12, ((0, 4),)),), ((13, ((0, 5),)),)), (far, o1_own))
    y2_own = y2[0]
    y2 = [swap(v, 2, peers) for v in y2]
    (a3_low,) = add((((6, ((0, 6), (1, 0))),),), (near, y3[0], y2_own))
    (a3_high,) = add((((7, ((0, 7), (1, 0))),),), (near, y3[1], a3_low))
    a3 = [swap(a3_low, 4, peers), swap(a3_high, 4, peers)]
    (a1_own,) = add((((2, ((0, 2),)), (3, ((0, 3),))),), (near,))
    a1 = both(a1_own, 4, peers)
    (y0_own,) = add((((8, ((0, 0), (1, 0, 2, 4))), (9, ((0, 1), (1, 1, 2, 4)))),), (far, o1))
    y0 = both(y0_own, 2, peers)
    (b2_low,) = add((((4, ((0, 4), (1, 0), (2, 0))),),), (near, y2[0], a3[0]))
    (b2_high,) = add((((5, ((0, 5), (1, 0), (2, 0))),),), (near, y2[1], a3[1], b2_low))
    b2 = [swap(b2_low, 8, peers), swap(b2_high, 8, peers)]
    left = lift_matrix(lev_index, lev_frac, b2_low)
    sums = ((0, 0), (1, 0, 2, 2), (2, 0, 2, 4), (3, 0))
    out = finish(0, me, left, acc, sums, (near, y0, a1, b2[0]))
    sums = ((0, 1), (1, 1, 2, 2), (2, 1, 2, 4), (3, 0))
    return finish(1, me, left, acc, sums, (near, y0, a1, b2[1]), out)


def vertical_matrix(lev_index, lev_frac, levels):
    columns = jnp.arange(levels)[None, :]
    lower = (columns == lev_index[:, None]).astype(jnp.float32)
    upper = (columns == lev_index[:, None] + 1).astype(jnp.float32)
    return (1.0 - lev_frac)[:, None] * lower + lev_frac[:, None] * upper


def slotted(cotangent, weight, target_block, dest, source, count, lev_index, lev_frac):
    peers = lax.axis_size("tile")
    entries, _, cells = weight.shape
    capacity = max(2, 2 * entries // peers)
    slots = peers * capacity
    up, down = ring(peers)
    before = lax.ppermute(cotangent[-1:], "tile", up)
    after = lax.ppermute(cotangent[:1], "tile", down)
    window = jnp.concatenate([before, cotangent, after], axis=0)
    contrib = jnp.einsum(
        "ofp,ops->ofs", window[target_block[0]], weight, preferred_element_type=jnp.float32
    )
    live = jnp.arange(entries) < count[0]
    matches = ((dest[0][:, None] == jnp.arange(peers)[None, :]) & live[:, None]).astype(jnp.int32)
    rank = jnp.sum(matches * jnp.cumsum(matches, axis=0), axis=1) - 1
    slot = jnp.where(live, dest[0] * capacity + rank, slots)
    labels = jnp.full((slots,), SB, jnp.int32).at[slot].set(source[0], mode="drop")
    outgoing = jnp.zeros((slots, ROWS, cells), jnp.float32).at[slot].set(contrib, mode="drop")
    arrived = lax.all_to_all(outgoing, "tile", split_axis=0, concat_axis=0, tiled=True)
    arrived_labels = lax.all_to_all(labels, "tile", split_axis=0, concat_axis=0, tiled=True)
    chooser = (jnp.arange(SB)[:, None] == arrived_labels[None, :]).astype(jnp.float32)
    summed = jnp.einsum("br,rfs->bfs", chooser, arrived, precision=lax.Precision.HIGHEST)
    lifted = jnp.einsum(
        "jl,bvjs->bvls",
        vertical_matrix(lev_index, lev_frac, LEV),
        summed.reshape(SB, VARS, LEVT, cells),
        precision=lax.Precision.HIGHEST,
    )
    return lifted.reshape(SB, VARS * LEV, cells)


def solution(mesh):
    placed = (
        P(("grp", "tile"), None, None),
        P("tile", None, None),
        P("tile", None),
        P("tile", None),
        P("tile", None),
        P("tile"),
        P(),
        P(),
    )
    return jax.shard_map(
        staged if mesh.shape["tile"] == 16 else slotted,
        mesh=mesh,
        in_specs=placed,
        out_specs=P(("grp", "tile"), None, None),
        check_vma=False,
    )
```

```python
import functools

import jax
import jax.numpy as jnp
from jax import lax
from jax.experimental import pallas as pl
from jax.experimental.pallas import tpu as pltpu
from jax.sharding import PartitionSpec as P

VARS = 6
LEV = 20
LEVT = 8
SB = 16
ROWS = VARS * LEVT
HALF = SB // 2
BODY = HALF * ROWS
CODED = BODY + 16
GROUP = 16
MIB = 1 << 20
LITTLE = pl.CostEstimate(flops=1, bytes_accessed=1, transcendentals=0)
MUCH = pl.CostEstimate(flops=1 << 28, bytes_accessed=12 * MIB, transcendentals=0)


def encode(read, write, exps):
    exps[HALF:, :] = jnp.zeros((16 - HALF, exps.shape[1]), jnp.float32)
    for b in range(HALF):
        x = read(b)
        top = jnp.max(jnp.abs(x), axis=0, keepdims=True)
        e = jnp.ceil(jnp.log2(jnp.maximum(top, 1e-30)) + 0.001) - 15.0
        exps[b : b + 1, :] = e
        q = jnp.round(x * jnp.exp2(-e))
        write(b * ROWS, ROWS, q.astype(jnp.int32).astype(jnp.int16))
    write(BODY, 16, exps[...].astype(jnp.int32).astype(jnp.int16))


def scales(ref, i):
    return jnp.exp2(ref[i, BODY:CODED, :].astype(jnp.int32).astype(jnp.float32))


def decode(ref, i, scale, b):
    q = ref[i, b * ROWS : (b + 1) * ROWS, :].astype(jnp.int32).astype(jnp.float32)
    return q * scale[b : b + 1, :]


TRASH = 16 * SB


def add_group(g, count, me, tables, cot, w, acc, ends, add, listing):
    blocks = cot.shape[0]
    n = ends[3, 0] if listing else None
    for i in range(GROUP):
        k = g * GROUP + i
        block = tables[0, k]
        rel = tables[1, k] ^ me
        slot = (rel & 1) * 8 + ((rel >> 1) & 1) * 4 + (rel >> 2)
        live = k < count
        at = jnp.where(live, slot * SB + tables[2, k], TRASH)
        outer = (block == 0) | (block == blocks + 1)
        if listing:
            ends[0, n] = k
            ends[1, n] = at
            ends[2, n] = jnp.where(block == 0, 0, 1)
            n = n + (outer & live).astype(jnp.int32)
        if add:
            at = jnp.where(outer, TRASH, at)
            left = cot[jnp.clip(block - 1, 0, blocks - 1)]
            acc[at] = acc[at] + jnp.dot(left, w[k], preferred_element_type=jnp.float32)
    if listing:
        ends[3, 0] = n


def groups_of(count):
    used = (count + GROUP - 1) // GROUP
    return used, (used + 1) // 2


def load(used, pairs, w_hbm, w, acc, sems, w_sems):
    def w_copy(g):
        part = pl.ds(g * GROUP, GROUP)
        return pltpu.make_async_copy(w_hbm.at[part], w.at[part], w_sems.at[g])

    small = [pltpu.make_async_copy(a, b, sems.at[i]) for i, (a, b) in enumerate(pairs)]
    for copy in small:
        copy.start()
    for g in range(w.shape[0] // GROUP):

        @pl.when(g < used)
        def _():
            w_copy(g).start()

    @pl.loop(0, TRASH, unroll=8)
    def _(b):
        acc[b] = jnp.zeros(acc.shape[1:], jnp.float32)

    acc[TRASH] = jnp.zeros(acc.shape[1:], jnp.float32)
    for copy in small:
        copy.wait()
    return w_copy


def ahead_kernel(
    count_ref, me_ref, tb, dest, src, cot_hbm, w_hbm, low_in, acc, w, cot, low, *scratch
):
    tables, sems, w_sems = scratch
    used, half = groups_of(count_ref[0])
    low[...] = low_in[...]

    @pl.when(me_ref[0] == 0)
    def _():
        pairs = [(cot_hbm, cot)]
        pairs += [(t, tables.at[pl.ds(i, 1)]) for i, t in enumerate((tb, dest, src))]
        w_copy = load(used, pairs, w_hbm, w, acc, sems, w_sems)
        for g in range(w.shape[0] // GROUP):

            @pl.when(g < used)
            def _():
                w_copy(g).wait()

            @pl.when(g < half)
            def _():
                add_group(g, count_ref[0], me_ref[0], tables, cot, w, acc, None, True, False)


def rest_kernel(count_ref, me_ref, tb, dest, src, cot_hbm, w_hbm, acc_in, w_in, cot_in, *refs):
    acc, w, cot, ends, tables, sems, w_sems = refs
    used, half = groups_of(count_ref[0])
    early = me_ref[0] == 0
    done = jnp.where(early, half, 0)
    ends[3, 0] = 0
    three = [(t, tables.at[pl.ds(i, 1)]) for i, t in enumerate((tb, dest, src))]

    @pl.when(early)
    def _():
        small = [pltpu.make_async_copy(a, b, sems.at[i]) for i, (a, b) in enumerate(three)]
        for copy in small:
            copy.start()
        for copy in small:
            copy.wait()

    @pl.when(jnp.logical_not(early))
    def _():
        load(used, three + [(cot_hbm, cot)], w_hbm, w, acc, sems, w_sems)

    @pl.loop(0, done)
    def _(g):
        add_group(g, count_ref[0], me_ref[0], tables, cot, w, acc, ends, False, True)

    for g in range(w.shape[0] // GROUP):

        @pl.when(jnp.logical_not(early) & (g < used))
        def _():
            part = pl.ds(g * GROUP, GROUP)
            pltpu.make_async_copy(w_hbm.at[part], w.at[part], w_sems.at[g]).wait()

        @pl.when((g >= done) & (g < used))
        def _():
            add_group(g, count_ref[0], me_ref[0], tables, cot, w, acc, ends, True, True)

    listed = ends[3, 0]
    for i in range(8):
        ends[0, listed + i] = 0
        ends[1, listed + i] = TRASH
        ends[2, listed + i] = 0


def in_hbm(x):
    return pltpu.with_memory_space_constraint(x, pltpu.HBM)


def products_call(kernel, operands, given, low, cost):
    cotangent, weight = operands[5], operands[6]
    entries, _, cells = weight.shape
    smem = pl.BlockSpec(memory_space=pltpu.SMEM)
    vmem = pl.BlockSpec(memory_space=pltpu.VMEM)
    hbm = pl.BlockSpec(memory_space=pltpu.HBM)
    results = [
        jax.ShapeDtypeStruct((TRASH + 1, ROWS, cells), jnp.float32),
        jax.ShapeDtypeStruct(weight.shape, weight.dtype),
        jax.ShapeDtypeStruct(cotangent.shape, cotangent.dtype),
    ]
    first = not given
    last = low if first else jax.ShapeDtypeStruct((4, entries + 8), jnp.int32)
    results.append(jax.ShapeDtypeStruct(last.shape, last.dtype))
    return pl.pallas_call(
        kernel,
        out_shape=tuple(results),
        in_specs=[smem, smem] + [hbm] * 5 + [vmem] * (1 if first else 3),
        out_specs=(vmem,) * 3 + (vmem if first else smem,),
        scratch_shapes=[
            pltpu.SMEM((3, entries), jnp.int32),
            pltpu.SemaphoreType.DMA((4,)),
            pltpu.SemaphoreType.DMA((entries // GROUP,)),
        ],
        input_output_aliases={} if first else {7: 0, 8: 1, 9: 2},
        compiler_params=pltpu.CompilerParams(vmem_limit_bytes=24 * MIB),
        cost_estimate=cost,
    )(*operands[:2], *[in_hbm(x) for x in operands[2:]], *([low] if first else given))


def code_half(acc, unit, coded, exps, out_ref, at):
    def read(b):
        total = acc[unit * HALF + b]
        for r, i, s in coded:
            total = total + decode(r, i, s, b)
        return total

    def write(row, rows, value):
        out_ref[at, row : row + rows, :] = value

    encode(read, write, exps)


def ends_kernel(ends, before, after, w, acc_in, acc, far_ref, sides, exps):
    sides[0] = before[0]
    sides[1] = after[0]

    @pl.loop(0, (ends[3, 0] + 7) // 8)
    def _(part):
        for i in range(8):
            k = part * 8 + i
            at = ends[1, k]
            left = sides[ends[2, k]]
            acc[at] = acc[at] + jnp.dot(left, w[ends[0, k]], preferred_element_type=jnp.float32)

    for i in range(2):
        code_half(acc, 30 + i, [], exps, far_ref, i)


def add_ends(ends, before, after, w, acc):
    cells = acc.shape[2]
    smem = pl.BlockSpec(memory_space=pltpu.SMEM)
    vmem = pl.BlockSpec(memory_space=pltpu.VMEM)
    return pl.pallas_call(
        ends_kernel,
        out_shape=(
            jax.ShapeDtypeStruct(acc.shape, jnp.float32),
            jax.ShapeDtypeStruct((2, CODED, cells), jnp.int16),
        ),
        in_specs=[smem] + [vmem] * 4,
        out_specs=(vmem, vmem),
        scratch_shapes=[
            pltpu.VMEM((2,) + before.shape[1:], jnp.bfloat16),
            pltpu.VMEM((16, cells), jnp.float32),
        ],
        input_output_aliases={4: 0},
        compiler_params=pltpu.CompilerParams(vmem_limit_bytes=32 * MIB),
        cost_estimate=LITTLE,
    )(ends, before, after, w, acc)


def code_kernel(jobs, acc, *refs):
    arrays, outs, exps = refs[: -1 - len(jobs)], refs[-1 - len(jobs) : -1], refs[-1]
    for parts, out in zip(jobs, outs):
        for at, (unit, takes) in enumerate(parts):
            coded = [(arrays[a], i, scales(arrays[a], i)) for a, i in takes]
            code_half(acc, unit, coded, exps, out, at)


def code(acc, jobs, arrays):
    cells = acc.shape[2]
    vmem = pl.BlockSpec(memory_space=pltpu.VMEM)
    return pl.pallas_call(
        functools.partial(code_kernel, jobs),
        out_shape=tuple(
            jax.ShapeDtypeStruct((len(parts), CODED, cells), jnp.int16) for parts in jobs
        ),
        in_specs=[vmem] * (1 + len(arrays)),
        out_specs=(vmem,) * len(jobs),
        scratch_shapes=[pltpu.VMEM((16, cells), jnp.float32)],
        compiler_params=pltpu.CompilerParams(vmem_limit_bytes=32 * MIB),
        cost_estimate=LITTLE,
    )(acc, *arrays)


def code_range_kernel(first, acc, *refs):
    out, exps = refs[-2:]

    @pl.loop(0, out.shape[0])
    def _(i):
        code_half(acc, first + i, [], exps, out, i)


def code_range(acc, first, number, after=()):
    cells = acc.shape[2]
    vmem = pl.BlockSpec(memory_space=pltpu.VMEM)
    return pl.pallas_call(
        functools.partial(code_range_kernel, first),
        out_shape=jax.ShapeDtypeStruct((number, CODED, cells), jnp.int16),
        in_specs=[vmem] * (1 + len(after)),
        out_specs=vmem,
        scratch_shapes=[pltpu.VMEM((16, cells), jnp.float32)],
        compiler_params=pltpu.CompilerParams(vmem_limit_bytes=32 * MIB),
        cost_estimate=LITTLE,
    )(acc, *after)


def lift_kernel(index_ref, frac_ref, after, left):
    high = VARS * LEV
    row = lax.broadcasted_iota(jnp.int32, (high, ROWS), 0)
    col = lax.broadcasted_iota(jnp.int32, (high, ROWS), 1)
    level = row % LEV
    lift = jnp.zeros((high, ROWS), jnp.float32)
    for j in range(LEVT):
        at, frac = index_ref[j], frac_ref[j]
        here = jnp.where(level == at, 1.0 - frac, jnp.where(level == at + 1, frac, 0.0))
        lift = jnp.where(col % LEVT == j, here, lift)
    lift = jnp.where(row // LEV == col // LEVT, lift, 0.0)
    high_part = lift.astype(jnp.bfloat16)
    low_part = (lift - high_part.astype(jnp.float32)).astype(jnp.bfloat16)
    left[...] = jnp.concatenate([high_part, high_part, low_part, low_part], axis=1)


def lift_matrix(lev_index, lev_frac, after):
    smem = pl.BlockSpec(memory_space=pltpu.SMEM)
    vmem = pl.BlockSpec(memory_space=pltpu.VMEM)
    return pl.pallas_call(
        lift_kernel,
        out_shape=jax.ShapeDtypeStruct((VARS * LEV, 4 * ROWS), jnp.bfloat16),
        in_specs=[smem, smem, vmem],
        out_specs=vmem,
        compiler_params=pltpu.CompilerParams(vmem_limit_bytes=4 * MIB),
        cost_estimate=LITTLE,
    )(lev_index, lev_frac, after)


def finish_kernel(half, takes, left, acc, *refs):
    arrays, out_hbm, out, sems = refs[:-3], refs[-3], refs[-2], refs[-1]
    coded = [(arrays[a], i, scales(arrays[a], i)) for a, i in takes]
    copies = []
    for b in range(HALF):
        total = acc[half * HALF + b]
        for r, i, s in coded:
            total = total + decode(r, i, s, b)
        first = total.astype(jnp.bfloat16)
        second = (total - first.astype(jnp.float32)).astype(jnp.bfloat16)
        right = jnp.concatenate([first, second, first, second], axis=0)
        out[b] = jnp.dot(left[...], right, preferred_element_type=jnp.float32)
        if b % 4 == 3:
            copy = pltpu.make_async_copy(
                out.at[pl.ds(b - 3, 4)],
                out_hbm.at[pl.ds(half * HALF + b - 3, 4)],
                sems.at[b // 4],
            )
            copy.start()
            copies.append(copy)
    for copy in copies:
        copy.wait()


def finish(half, left, acc, takes, arrays, begun=None):
    cells = acc.shape[2]
    vmem = pl.BlockSpec(memory_space=pltpu.VMEM)
    hbm = pl.BlockSpec(memory_space=pltpu.HBM)
    extra = () if begun is None else (begun,)
    return pl.pallas_call(
        functools.partial(finish_kernel, half, takes),
        out_shape=jax.ShapeDtypeStruct((SB, VARS * LEV, cells), jnp.float32),
        in_specs=[vmem] * (2 + len(arrays)) + [hbm] * len(extra),
        out_specs=hbm,
        scratch_shapes=[
            pltpu.VMEM((HALF, VARS * LEV, cells), jnp.float32),
            pltpu.SemaphoreType.DMA((HALF // 4,)),
        ],
        input_output_aliases={2 + len(arrays): 0} if extra else {},
        compiler_params=pltpu.CompilerParams(vmem_limit_bytes=32 * MIB),
        cost_estimate=pl.CostEstimate(flops=1, bytes_accessed=4194304, transcendentals=0),
    )(left, acc, *arrays, *extra)


def ring(peers):
    up = [(i, (i + 1) % peers) for i in range(peers)]
    return up, [(j, i) for i, j in up]


def swap(value, bits, peers):
    return lax.ppermute(value, "tile", [(i, i ^ bits) for i in range(peers)])


def staged(cotangent, weight, target_block, dest, source, count, lev_index, lev_frac):
    peers = 16
    me = lax.axis_index("tile").astype(jnp.int32).reshape(1)
    operands = (count, me, target_block, dest, source, cotangent, weight)
    up, down = ring(peers)
    before = lax.ppermute(cotangent[-1:], "tile", up)
    acc, w, cot, low = products_call(ahead_kernel, operands, (), cotangent[:1], MUCH)
    after = lax.ppermute(low, "tile", down)
    acc, w, cot, ends = products_call(rest_kernel, operands, (acc, w, cot), None, LITTLE)
    acc, far3 = add_ends(ends, before, after, w, acc)
    far3 = swap(far3, 1, peers)
    near = swap(code_range(acc, 16, 8), 1, peers)
    y3 = code(acc, (((14, ((0, 0),)),), ((15, ((0, 1),)),)), (far3,))
    y3_own = y3[0]
    far = swap(code_range(acc, 24, 6, (y3_own,)), 1, peers)
    y3 = [swap(v, 2, peers) for v in y3]
    y2 = code(acc, (((12, ((0, 4),)),), ((13, ((0, 5),)),)), (far, y3_own))
    y2_own = y2[0]
    y2 = [swap(v, 2, peers) for v in y2]
    (a3_low,) = code(acc, (((6, ((0, 6), (1, 0))),),), (near, y3[0], y2_own))
    (a3_high,) = code(acc, (((7, ((0, 7), (1, 0))),),), (near, y3[1], a3_low))
    a3 = [swap(a3_low, 4, peers), swap(a3_high, 4, peers)]
    (y1_own,) = code(acc, (((10, ((0, 2),)), (11, ((0, 3),))),), (far, y3_own))
    o1 = swap(y1_own, 4, peers)
    (b2_low,) = code(acc, (((4, ((0, 4), (1, 0), (2, 0))),),), (near, y2[0], a3[0], y1_own))
    (b2_high,) = code(acc, (((5, ((0, 5), (1, 0), (2, 0))),),), (near, y2[1], a3[1], b2_low))
    b2 = [swap(b2_low, 8, peers), swap(b2_high, 8, peers)]
    y0_own = code(acc, (((8, ((0, 0), (1, 0))),), ((9, ((0, 1), (1, 1))),)), (far, o1, a3[0]))
    y0 = [swap(v, 2, peers) for v in y0_own]
    y0_own = y0_own[0]
    (a1_own,) = code(acc, (((2, ((0, 2),)), (3, ((0, 3),))),), (near, a3_high))
    a1 = swap(a1_own, 4, peers)
    left = lift_matrix(lev_index, lev_frac, b2_low)
    out = finish(0, left, acc, ((0, 0), (1, 0), (2, 0), (3, 0)), (near, y0[0], a1, b2[0]))
    return finish(1, left, acc, ((0, 1), (1, 0), (2, 1), (3, 0)), (near, y0[1], a1, b2[1]), out)


def vertical_matrix(lev_index, lev_frac, levels):
    columns = jnp.arange(levels)[None, :]
    lower = (columns == lev_index[:, None]).astype(jnp.float32)
    upper = (columns == lev_index[:, None] + 1).astype(jnp.float32)
    return (1.0 - lev_frac)[:, None] * lower + lev_frac[:, None] * upper


def slotted(cotangent, weight, target_block, dest, source, count, lev_index, lev_frac):
    peers = lax.axis_size("tile")
    entries, _, cells = weight.shape
    capacity = max(2, 2 * entries // peers)
    slots = peers * capacity
    up, down = ring(peers)
    before = lax.ppermute(cotangent[-1:], "tile", up)
    after = lax.ppermute(cotangent[:1], "tile", down)
    window = jnp.concatenate([before, cotangent, after], axis=0)
    contrib = jnp.einsum(
        "ofp,ops->ofs", window[target_block[0]], weight, preferred_element_type=jnp.float32
    )
    live = jnp.arange(entries) < count[0]
    matches = ((dest[0][:, None] == jnp.arange(peers)[None, :]) & live[:, None]).astype(jnp.int32)
    rank = jnp.sum(matches * jnp.cumsum(matches, axis=0), axis=1) - 1
    slot = jnp.where(live, dest[0] * capacity + rank, slots)
    labels = jnp.full((slots,), SB, jnp.int32).at[slot].set(source[0], mode="drop")
    outgoing = jnp.zeros((slots, ROWS, cells), jnp.float32).at[slot].set(contrib, mode="drop")
    arrived = lax.all_to_all(outgoing, "tile", split_axis=0, concat_axis=0, tiled=True)
    arrived_labels = lax.all_to_all(labels, "tile", split_axis=0, concat_axis=0, tiled=True)
    chooser = (jnp.arange(SB)[:, None] == arrived_labels[None, :]).astype(jnp.float32)
    summed = jnp.einsum("br,rfs->bfs", chooser, arrived, precision=lax.Precision.HIGHEST)
    lifted = jnp.einsum(
        "jl,bvjs->bvls",
        vertical_matrix(lev_index, lev_frac, LEV),
        summed.reshape(SB, VARS, LEVT, cells),
        precision=lax.Precision.HIGHEST,
    )
    return lifted.reshape(SB, VARS * LEV, cells)


def solution(mesh):
    placed = (
        P(("grp", "tile"), None, None),
        P("tile", None, None),
        P("tile", None),
        P("tile", None),
        P("tile", None),
        P("tile"),
        P(),
        P(),
    )
    return jax.shard_map(
        staged if mesh.shape["tile"] == 16 else slotted,
        mesh=mesh,
        in_specs=placed,
        out_specs=P(("grp", "tile"), None, None),
        check_vma=False,
    )
```

```python
import functools

import jax
import jax.numpy as jnp
from jax import lax
from jax.experimental import pallas as pl
from jax.experimental.pallas import tpu as pltpu
from jax.sharding import PartitionSpec as P

VARS = 6
LEV = 20
LEVT = 8
SB = 16
ROWS = VARS * LEVT
HALF = SB // 2
BODY = HALF * ROWS
CODED = BODY + 16
GROUP = 16
MIB = 1 << 20
LITTLE = pl.CostEstimate(flops=1, bytes_accessed=1, transcendentals=0)
MUCH = pl.CostEstimate(flops=1 << 28, bytes_accessed=12 * MIB, transcendentals=0)


def encode(read, write, exps):
    exps[HALF:, :] = jnp.zeros((16 - HALF, exps.shape[1]), jnp.float32)
    for b in range(HALF):
        x = read(b)
        top = jnp.max(jnp.abs(x), axis=0, keepdims=True)
        e = jnp.ceil(jnp.log2(jnp.maximum(top, 1e-30)) + 0.001) - 15.0
        exps[b : b + 1, :] = e
        q = jnp.round(x * jnp.exp2(-e))
        write(b * ROWS, ROWS, q.astype(jnp.int32).astype(jnp.int16))
    write(BODY, 16, exps[...].astype(jnp.int32).astype(jnp.int16))


def scales(ref, i):
    return jnp.exp2(ref[i, BODY:CODED, :].astype(jnp.int32).astype(jnp.float32))


def decode(ref, i, scale, b):
    q = ref[i, b * ROWS : (b + 1) * ROWS, :].astype(jnp.int32).astype(jnp.float32)
    return q * scale[b : b + 1, :]


TRASH = 16 * SB


def add_group(g, count, me, tables, cot, w, acc, ends, add, listing):
    blocks = cot.shape[0]
    n = ends[3, 0] if listing else None
    for i in range(GROUP):
        k = g * GROUP + i
        block = tables[0, k]
        rel = tables[1, k] ^ me
        slot = (rel & 1) * 8 + ((rel >> 1) & 1) * 4 + (rel >> 2)
        live = k < count
        at = jnp.where(live, slot * SB + tables[2, k], TRASH)
        outer = (block == 0) | (block == blocks + 1)
        if listing:
            ends[0, n] = k
            ends[1, n] = at
            ends[2, n] = jnp.where(block == 0, 0, 1)
            n = n + (outer & live).astype(jnp.int32)
        if add:
            at = jnp.where(outer, TRASH, at)
            left = cot[jnp.clip(block - 1, 0, blocks - 1)]
            acc[at] = acc[at] + jnp.dot(left, w[k], preferred_element_type=jnp.float32)
    if listing:
        ends[3, 0] = n


def groups_of(count):
    used = (count + GROUP - 1) // GROUP
    return used, (used + 1) // 2


def load(used, pairs, w_hbm, w, acc, sems, w_sems):
    def w_copy(g):
        part = pl.ds(g * GROUP, GROUP)
        return pltpu.make_async_copy(w_hbm.at[part], w.at[part], w_sems.at[g])

    small = [pltpu.make_async_copy(a, b, sems.at[i]) for i, (a, b) in enumerate(pairs)]
    for copy in small:
        copy.start()
    for g in range(w.shape[0] // GROUP):

        @pl.when(g < used)
        def _():
            w_copy(g).start()

    @pl.loop(0, TRASH, unroll=8)
    def _(b):
        acc[b] = jnp.zeros(acc.shape[1:], jnp.float32)

    acc[TRASH] = jnp.zeros(acc.shape[1:], jnp.float32)
    for copy in small:
        copy.wait()
    return w_copy


def ahead_kernel(
    count_ref, me_ref, tb, dest, src, cot_hbm, w_hbm, low_in, acc, w, cot, low, *scratch
):
    tables, sems, w_sems = scratch
    used, half = groups_of(count_ref[0])
    low[...] = low_in[...]

    @pl.when(me_ref[0] == 0)
    def _():
        pairs = [(cot_hbm, cot)]
        pairs += [(t, tables.at[pl.ds(i, 1)]) for i, t in enumerate((tb, dest, src))]
        w_copy = load(used, pairs, w_hbm, w, acc, sems, w_sems)
        for g in range(w.shape[0] // GROUP):

            @pl.when(g < used)
            def _():
                w_copy(g).wait()

            @pl.when(g < half)
            def _():
                add_group(g, count_ref[0], me_ref[0], tables, cot, w, acc, None, True, False)


def rest_kernel(count_ref, me_ref, tb, dest, src, cot_hbm, w_hbm, acc_in, w_in, cot_in, *refs):
    acc, w, cot, ends, tables, sems, w_sems = refs
    used, half = groups_of(count_ref[0])
    early = me_ref[0] == 0
    done = jnp.where(early, half, 0)
    ends[3, 0] = 0
    three = [(t, tables.at[pl.ds(i, 1)]) for i, t in enumerate((tb, dest, src))]

    @pl.when(early)
    def _():
        small = [pltpu.make_async_copy(a, b, sems.at[i]) for i, (a, b) in enumerate(three)]
        for copy in small:
            copy.start()
        for copy in small:
            copy.wait()

    @pl.when(jnp.logical_not(early))
    def _():
        load(used, three + [(cot_hbm, cot)], w_hbm, w, acc, sems, w_sems)

    @pl.loop(0, done)
    def _(g):
        add_group(g, count_ref[0], me_ref[0], tables, cot, w, acc, ends, False, True)

    for g in range(w.shape[0] // GROUP):

        @pl.when(jnp.logical_not(early) & (g < used))
        def _():
            part = pl.ds(g * GROUP, GROUP)
            pltpu.make_async_copy(w_hbm.at[part], w.at[part], w_sems.at[g]).wait()

        @pl.when((g >= done) & (g < used))
        def _():
            add_group(g, count_ref[0], me_ref[0], tables, cot, w, acc, ends, True, True)

    listed = ends[3, 0]
    for i in range(8):
        ends[0, listed + i] = 0
        ends[1, listed + i] = TRASH
        ends[2, listed + i] = 0


def in_hbm(x):
    return pltpu.with_memory_space_constraint(x, pltpu.HBM)


def products_call(kernel, operands, given, low, cost):
    cotangent, weight = operands[5], operands[6]
    entries, _, cells = weight.shape
    smem = pl.BlockSpec(memory_space=pltpu.SMEM)
    vmem = pl.BlockSpec(memory_space=pltpu.VMEM)
    hbm = pl.BlockSpec(memory_space=pltpu.HBM)
    results = [
        jax.ShapeDtypeStruct((TRASH + 1, ROWS, cells), jnp.float32),
        jax.ShapeDtypeStruct(weight.shape, weight.dtype),
        jax.ShapeDtypeStruct(cotangent.shape, cotangent.dtype),
    ]
    first = not given
    last = low if first else jax.ShapeDtypeStruct((4, entries + 8), jnp.int32)
    results.append(jax.ShapeDtypeStruct(last.shape, last.dtype))
    return pl.pallas_call(
        kernel,
        out_shape=tuple(results),
        in_specs=[smem, smem] + [hbm] * 5 + [vmem] * (1 if first else 3),
        out_specs=(vmem,) * 3 + (vmem if first else smem,),
        scratch_shapes=[
            pltpu.SMEM((3, entries), jnp.int32),
            pltpu.SemaphoreType.DMA((4,)),
            pltpu.SemaphoreType.DMA((entries // GROUP,)),
        ],
        input_output_aliases={} if first else {7: 0, 8: 1, 9: 2},
        compiler_params=pltpu.CompilerParams(vmem_limit_bytes=24 * MIB),
        cost_estimate=cost,
    )(*operands[:2], *[in_hbm(x) for x in operands[2:]], *([low] if first else given))


def code_half(acc, unit, coded, exps, out_ref, at):
    def read(b):
        total = acc[unit * HALF + b]
        for r, i, s in coded:
            total = total + decode(r, i, s, b)
        return total

    def write(row, rows, value):
        out_ref[at, row : row + rows, :] = value

    encode(read, write, exps)


def ends_kernel(ends, before, after, w, acc_in, acc, far_ref, sides, exps):
    sides[0] = before[0]
    sides[1] = after[0]

    @pl.loop(0, (ends[3, 0] + 7) // 8)
    def _(part):
        for i in range(8):
            k = part * 8 + i
            at = ends[1, k]
            left = sides[ends[2, k]]
            acc[at] = acc[at] + jnp.dot(left, w[ends[0, k]], preferred_element_type=jnp.float32)

    @pl.loop(0, 8, unroll=4)
    def _(i):
        code_half(acc, 24 + i, [], exps, far_ref, i)


def add_ends(ends, before, after, w, acc):
    cells = acc.shape[2]
    smem = pl.BlockSpec(memory_space=pltpu.SMEM)
    vmem = pl.BlockSpec(memory_space=pltpu.VMEM)
    return pl.pallas_call(
        ends_kernel,
        out_shape=(
            jax.ShapeDtypeStruct(acc.shape, jnp.float32),
            jax.ShapeDtypeStruct((8, CODED, cells), jnp.int16),
        ),
        in_specs=[smem] + [vmem] * 4,
        out_specs=(vmem, vmem),
        scratch_shapes=[
            pltpu.VMEM((2,) + before.shape[1:], jnp.bfloat16),
            pltpu.VMEM((16, cells), jnp.float32),
        ],
        input_output_aliases={4: 0},
        compiler_params=pltpu.CompilerParams(vmem_limit_bytes=32 * MIB),
        cost_estimate=LITTLE,
    )(ends, before, after, w, acc)


def code_kernel(jobs, acc, *refs):
    arrays, outs, exps = refs[: -1 - len(jobs)], refs[-1 - len(jobs) : -1], refs[-1]
    for parts, out in zip(jobs, outs):
        for at, (unit, takes) in enumerate(parts):
            coded = [(arrays[a], i, scales(arrays[a], i)) for a, i in takes]
            code_half(acc, unit, coded, exps, out, at)


def code(acc, jobs, arrays):
    cells = acc.shape[2]
    vmem = pl.BlockSpec(memory_space=pltpu.VMEM)
    return pl.pallas_call(
        functools.partial(code_kernel, jobs),
        out_shape=tuple(
            jax.ShapeDtypeStruct((len(parts), CODED, cells), jnp.int16) for parts in jobs
        ),
        in_specs=[vmem] * (1 + len(arrays)),
        out_specs=(vmem,) * len(jobs),
        scratch_shapes=[pltpu.VMEM((16, cells), jnp.float32)],
        compiler_params=pltpu.CompilerParams(vmem_limit_bytes=32 * MIB),
        cost_estimate=LITTLE,
    )(acc, *arrays)


def code_near_kernel(acc, near_ref, exps):
    @pl.loop(0, 8, unroll=4)
    def _(i):
        code_half(acc, 16 + i, [], exps, near_ref, i)


def code_near(acc):
    cells = acc.shape[2]
    vmem = pl.BlockSpec(memory_space=pltpu.VMEM)
    return pl.pallas_call(
        code_near_kernel,
        out_shape=jax.ShapeDtypeStruct((8, CODED, cells), jnp.int16),
        in_specs=[vmem],
        out_specs=vmem,
        scratch_shapes=[pltpu.VMEM((16, cells), jnp.float32)],
        compiler_params=pltpu.CompilerParams(vmem_limit_bytes=32 * MIB),
        cost_estimate=LITTLE,
    )(acc)


def lift_kernel(index_ref, frac_ref, after, left):
    high = VARS * LEV
    row = lax.broadcasted_iota(jnp.int32, (high, ROWS), 0)
    col = lax.broadcasted_iota(jnp.int32, (high, ROWS), 1)
    level = row % LEV
    lift = jnp.zeros((high, ROWS), jnp.float32)
    for j in range(LEVT):
        at, frac = index_ref[j], frac_ref[j]
        here = jnp.where(level == at, 1.0 - frac, jnp.where(level == at + 1, frac, 0.0))
        lift = jnp.where(col % LEVT == j, here, lift)
    lift = jnp.where(row // LEV == col // LEVT, lift, 0.0)
    high_part = lift.astype(jnp.bfloat16)
    low_part = (lift - high_part.astype(jnp.float32)).astype(jnp.bfloat16)
    left[...] = jnp.concatenate([high_part, high_part, low_part, low_part], axis=1)


def lift_matrix(lev_index, lev_frac, after):
    smem = pl.BlockSpec(memory_space=pltpu.SMEM)
    vmem = pl.BlockSpec(memory_space=pltpu.VMEM)
    return pl.pallas_call(
        lift_kernel,
        out_shape=jax.ShapeDtypeStruct((VARS * LEV, 4 * ROWS), jnp.bfloat16),
        in_specs=[smem, smem, vmem],
        out_specs=vmem,
        compiler_params=pltpu.CompilerParams(vmem_limit_bytes=4 * MIB),
        cost_estimate=LITTLE,
    )(lev_index, lev_frac, after)


def finish_kernel(half, takes, left, acc, *refs):
    arrays, out_hbm, out, sems = refs[:-3], refs[-3], refs[-2], refs[-1]
    coded = [(arrays[a], i, scales(arrays[a], i)) for a, i in takes]
    copies = []
    for b in range(HALF):
        total = acc[half * HALF + b]
        for r, i, s in coded:
            total = total + decode(r, i, s, b)
        first = total.astype(jnp.bfloat16)
        second = (total - first.astype(jnp.float32)).astype(jnp.bfloat16)
        right = jnp.concatenate([first, second, first, second], axis=0)
        out[b] = jnp.dot(left[...], right, preferred_element_type=jnp.float32)
        if b % 2:
            copy = pltpu.make_async_copy(
                out.at[pl.ds(b - 1, 2)],
                out_hbm.at[pl.ds(half * HALF + b - 1, 2)],
                sems.at[b // 2],
            )
            copy.start()
            copies.append(copy)
    for copy in copies:
        copy.wait()


def finish(half, left, acc, takes, arrays, begun=None):
    cells = acc.shape[2]
    vmem = pl.BlockSpec(memory_space=pltpu.VMEM)
    hbm = pl.BlockSpec(memory_space=pltpu.HBM)
    extra = () if begun is None else (begun,)
    return pl.pallas_call(
        functools.partial(finish_kernel, half, takes),
        out_shape=jax.ShapeDtypeStruct((SB, VARS * LEV, cells), jnp.float32),
        in_specs=[vmem] * (2 + len(arrays)) + [hbm] * len(extra),
        out_specs=hbm,
        scratch_shapes=[
            pltpu.VMEM((HALF, VARS * LEV, cells), jnp.float32),
            pltpu.SemaphoreType.DMA((HALF // 2,)),
        ],
        input_output_aliases={2 + len(arrays): 0} if extra else {},
        compiler_params=pltpu.CompilerParams(vmem_limit_bytes=32 * MIB),
        cost_estimate=pl.CostEstimate(flops=1, bytes_accessed=4194304, transcendentals=0),
    )(left, acc, *arrays, *extra)


def ring(peers):
    up = [(i, (i + 1) % peers) for i in range(peers)]
    return up, [(j, i) for i, j in up]


def swap(value, bits, peers):
    return lax.ppermute(value, "tile", [(i, i ^ bits) for i in range(peers)])


def staged(cotangent, weight, target_block, dest, source, count, lev_index, lev_frac):
    peers = 16
    me = lax.axis_index("tile").astype(jnp.int32).reshape(1)
    operands = (count, me, target_block, dest, source, cotangent, weight)
    up, down = ring(peers)
    before = lax.ppermute(cotangent[-1:], "tile", up)
    acc, w, cot, low = products_call(ahead_kernel, operands, (), cotangent[:1], MUCH)
    after = lax.ppermute(low, "tile", down)
    acc, w, cot, ends = products_call(rest_kernel, operands, (acc, w, cot), None, LITTLE)
    acc, far = add_ends(ends, before, after, w, acc)
    far = swap(far, 1, peers)
    near = swap(code_near(acc), 1, peers)
    y3 = code(acc, (((14, ((0, 6),)),), ((15, ((0, 7),)),)), (far,))
    y3_own = y3[0]
    y3 = [swap(v, 2, peers) for v in y3]
    y2 = code(acc, (((12, ((0, 4),)),), ((13, ((0, 5),)),)), (far, y3_own))
    y2_own = y2[0]
    y2 = [swap(v, 2, peers) for v in y2]
    (a3_low,) = code(acc, (((6, ((0, 6), (1, 0))),),), (near, y3[0], far))
    (a3_high,) = code(acc, (((7, ((0, 7), (1, 0))),),), (near, y3[1], a3_low))
    a3 = [swap(a3_low, 4, peers), swap(a3_high, 4, peers)]
    (y1_own,) = code(acc, (((10, ((0, 2),)), (11, ((0, 3),))),), (far, y2_own))
    o1 = swap(y1_own, 4, peers)
    (b2_low,) = code(acc, (((4, ((0, 4), (1, 0), (2, 0))),),), (near, y2[0], a3[0], far))
    (b2_high,) = code(acc, (((5, ((0, 5), (1, 0), (2, 0))),),), (near, y2[1], a3[1], b2_low))
    b2 = [swap(b2_low, 8, peers), swap(b2_high, 8, peers)]
    y0_own = code(acc, (((8, ((0, 0), (1, 0))),), ((9, ((0, 1), (1, 1))),)), (far, o1, b2_low))
    y0 = [swap(v, 2, peers) for v in y0_own]
    y0_own = y0_own[0]
    (a1_own,) = code(acc, (((2, ((0, 2),)), (3, ((0, 3),))),), (near, a3_high))
    a1 = swap(a1_own, 4, peers)
    left = lift_matrix(lev_index, lev_frac, b2_high)
    out = finish(0, left, acc, ((0, 0), (1, 0), (2, 0), (3, 0)), (near, y0[0], a1, b2[0]))
    return finish(1, left, acc, ((0, 1), (1, 0), (2, 1), (3, 0)), (near, y0[1], a1, b2[1]), out)


def vertical_matrix(lev_index, lev_frac, levels):
    columns = jnp.arange(levels)[None, :]
    lower = (columns == lev_index[:, None]).astype(jnp.float32)
    upper = (columns == lev_index[:, None] + 1).astype(jnp.float32)
    return (1.0 - lev_frac)[:, None] * lower + lev_frac[:, None] * upper


def slotted(cotangent, weight, target_block, dest, source, count, lev_index, lev_frac):
    peers = lax.axis_size("tile")
    entries, _, cells = weight.shape
    capacity = max(2, 2 * entries // peers)
    slots = peers * capacity
    up, down = ring(peers)
    before = lax.ppermute(cotangent[-1:], "tile", up)
    after = lax.ppermute(cotangent[:1], "tile", down)
    window = jnp.concatenate([before, cotangent, after], axis=0)
    contrib = jnp.einsum(
        "ofp,ops->ofs", window[target_block[0]], weight, preferred_element_type=jnp.float32
    )
    live = jnp.arange(entries) < count[0]
    matches = ((dest[0][:, None] == jnp.arange(peers)[None, :]) & live[:, None]).astype(jnp.int32)
    rank = jnp.sum(matches * jnp.cumsum(matches, axis=0), axis=1) - 1
    slot = jnp.where(live, dest[0] * capacity + rank, slots)
    labels = jnp.full((slots,), SB, jnp.int32).at[slot].set(source[0], mode="drop")
    outgoing = jnp.zeros((slots, ROWS, cells), jnp.float32).at[slot].set(contrib, mode="drop")
    arrived = lax.all_to_all(outgoing, "tile", split_axis=0, concat_axis=0, tiled=True)
    arrived_labels = lax.all_to_all(labels, "tile", split_axis=0, concat_axis=0, tiled=True)
    chooser = (jnp.arange(SB)[:, None] == arrived_labels[None, :]).astype(jnp.float32)
    summed = jnp.einsum("br,rfs->bfs", chooser, arrived, precision=lax.Precision.HIGHEST)
    lifted = jnp.einsum(
        "jl,bvjs->bvls",
        vertical_matrix(lev_index, lev_frac, LEV),
        summed.reshape(SB, VARS, LEVT, cells),
        precision=lax.Precision.HIGHEST,
    )
    return lifted.reshape(SB, VARS * LEV, cells)


def solution(mesh):
    placed = (
        P(("grp", "tile"), None, None),
        P("tile", None, None),
        P("tile", None),
        P("tile", None),
        P("tile", None),
        P("tile"),
        P(),
        P(),
    )
    return jax.shard_map(
        staged if mesh.shape["tile"] == 16 else slotted,
        mesh=mesh,
        in_specs=placed,
        out_specs=P(("grp", "tile"), None, None),
        check_vma=False,
    )
```

```python
import functools

import jax
import jax.numpy as jnp
from jax import lax
from jax.experimental import pallas as pl
from jax.experimental.pallas import tpu as pltpu
from jax.sharding import PartitionSpec as P

VARS = 6
LEV = 20
LEVT = 8
SB = 16
ROWS = VARS * LEVT
HALF = SB // 2
BODY = HALF * ROWS
CODED = BODY + 16
GROUP = 16
MIB = 1 << 20
LITTLE = pl.CostEstimate(flops=1, bytes_accessed=1, transcendentals=0)
MUCH = pl.CostEstimate(flops=1 << 28, bytes_accessed=12 * MIB, transcendentals=0)


def encode(read, write, exps):
    exps[HALF:, :] = jnp.zeros((16 - HALF, exps.shape[1]), jnp.float32)
    for b in range(HALF):
        x = read(b)
        top = jnp.max(jnp.abs(x), axis=0, keepdims=True)
        e = jnp.ceil(jnp.log2(jnp.maximum(top, 1e-30)) + 0.001) - 15.0
        exps[b : b + 1, :] = e
        q = jnp.round(x * jnp.exp2(-e))
        write(b * ROWS, ROWS, q.astype(jnp.int32).astype(jnp.int16))
    write(BODY, 16, exps[...].astype(jnp.int32).astype(jnp.int16))


def scales(ref, i):
    return jnp.exp2(ref[i, BODY:CODED, :].astype(jnp.int32).astype(jnp.float32))


def decode(ref, i, scale, b):
    q = ref[i, b * ROWS : (b + 1) * ROWS, :].astype(jnp.int32).astype(jnp.float32)
    return q * scale[b : b + 1, :]


TRASH = 16 * SB


def add_group(g, count, me, tables, cot, w, acc, ends, add, listing):
    blocks = cot.shape[0]
    n = ends[3, 0] if listing else None
    for i in range(GROUP):
        k = g * GROUP + i
        block = tables[0, k]
        rel = tables[1, k] ^ me
        slot = (rel & 1) * 8 + ((rel >> 1) & 1) * 4 + (rel >> 2)
        live = k < count
        at = jnp.where(live, slot * SB + tables[2, k], TRASH)
        outer = (block == 0) | (block == blocks + 1)
        if listing:
            ends[0, n] = k
            ends[1, n] = at
            ends[2, n] = jnp.where(block == 0, 0, 1)
            n = n + (outer & live).astype(jnp.int32)
        if add:
            at = jnp.where(outer, TRASH, at)
            left = cot[jnp.clip(block - 1, 0, blocks - 1)]
            acc[at] = acc[at] + jnp.dot(left, w[k], preferred_element_type=jnp.float32)
    if listing:
        ends[3, 0] = n


def groups_of(count):
    used = (count + GROUP - 1) // GROUP
    return used, (3 * used + 3) // 4


def load(used, pairs, w_hbm, w, acc, sems, w_sems):
    def w_copy(g):
        part = pl.ds(g * GROUP, GROUP)
        return pltpu.make_async_copy(w_hbm.at[part], w.at[part], w_sems.at[g])

    small = [pltpu.make_async_copy(a, b, sems.at[i]) for i, (a, b) in enumerate(pairs)]
    for copy in small:
        copy.start()
    for g in range(w.shape[0] // GROUP):

        @pl.when(g < used)
        def _():
            w_copy(g).start()

    @pl.loop(0, TRASH, unroll=8)
    def _(b):
        acc[b] = jnp.zeros(acc.shape[1:], jnp.float32)

    acc[TRASH] = jnp.zeros(acc.shape[1:], jnp.float32)
    for copy in small:
        copy.wait()
    return w_copy


def ahead_kernel(
    count_ref, me_ref, tb, dest, src, cot_hbm, w_hbm, low_in, acc, w, cot, low, *scratch
):
    tables, sems, w_sems = scratch
    used, half = groups_of(count_ref[0])
    low[...] = low_in[...]

    @pl.when(me_ref[0] == 0)
    def _():
        pairs = [(cot_hbm, cot)]
        pairs += [(t, tables.at[pl.ds(i, 1)]) for i, t in enumerate((tb, dest, src))]
        w_copy = load(used, pairs, w_hbm, w, acc, sems, w_sems)
        for g in range(w.shape[0] // GROUP):

            @pl.when(g < used)
            def _():
                w_copy(g).wait()

            @pl.when(g < half)
            def _():
                add_group(g, count_ref[0], me_ref[0], tables, cot, w, acc, None, True, False)


def rest_kernel(count_ref, me_ref, tb, dest, src, cot_hbm, w_hbm, acc_in, w_in, cot_in, *refs):
    acc, w, cot, ends, tables, sems, w_sems = refs
    used, half = groups_of(count_ref[0])
    early = me_ref[0] == 0
    done = jnp.where(early, half, 0)
    ends[3, 0] = 0
    three = [(t, tables.at[pl.ds(i, 1)]) for i, t in enumerate((tb, dest, src))]

    @pl.when(early)
    def _():
        small = [pltpu.make_async_copy(a, b, sems.at[i]) for i, (a, b) in enumerate(three)]
        for copy in small:
            copy.start()
        for copy in small:
            copy.wait()

    @pl.when(jnp.logical_not(early))
    def _():
        load(used, three + [(cot_hbm, cot)], w_hbm, w, acc, sems, w_sems)

    @pl.loop(0, done)
    def _(g):
        add_group(g, count_ref[0], me_ref[0], tables, cot, w, acc, ends, False, True)

    for g in range(w.shape[0] // GROUP):

        @pl.when(jnp.logical_not(early) & (g < used))
        def _():
            part = pl.ds(g * GROUP, GROUP)
            pltpu.make_async_copy(w_hbm.at[part], w.at[part], w_sems.at[g]).wait()

        @pl.when((g >= done) & (g < used))
        def _():
            add_group(g, count_ref[0], me_ref[0], tables, cot, w, acc, ends, True, True)

    listed = ends[3, 0]
    for i in range(8):
        ends[0, listed + i] = 0
        ends[1, listed + i] = TRASH
        ends[2, listed + i] = 0


def in_hbm(x):
    return pltpu.with_memory_space_constraint(x, pltpu.HBM)


def products_call(kernel, operands, given, low, cost):
    cotangent, weight = operands[5], operands[6]
    entries, _, cells = weight.shape
    smem = pl.BlockSpec(memory_space=pltpu.SMEM)
    vmem = pl.BlockSpec(memory_space=pltpu.VMEM)
    hbm = pl.BlockSpec(memory_space=pltpu.HBM)
    results = [
        jax.ShapeDtypeStruct((TRASH + 1, ROWS, cells), jnp.float32),
        jax.ShapeDtypeStruct(weight.shape, weight.dtype),
        jax.ShapeDtypeStruct(cotangent.shape, cotangent.dtype),
    ]
    first = not given
    last = low if first else jax.ShapeDtypeStruct((4, entries + 8), jnp.int32)
    results.append(jax.ShapeDtypeStruct(last.shape, last.dtype))
    return pl.pallas_call(
        kernel,
        out_shape=tuple(results),
        in_specs=[smem, smem] + [hbm] * 5 + [vmem] * (1 if first else 3),
        out_specs=(vmem,) * 3 + (vmem if first else smem,),
        scratch_shapes=[
            pltpu.SMEM((3, entries), jnp.int32),
            pltpu.SemaphoreType.DMA((4,)),
            pltpu.SemaphoreType.DMA((entries // GROUP,)),
        ],
        input_output_aliases={} if first else {7: 0, 8: 1, 9: 2},
        compiler_params=pltpu.CompilerParams(vmem_limit_bytes=24 * MIB),
        cost_estimate=cost,
    )(*operands[:2], *[in_hbm(x) for x in operands[2:]], *([low] if first else given))


def code_half(acc, unit, coded, exps, out_ref, at):
    def read(b):
        total = acc[unit * HALF + b]
        for r, i, s in coded:
            total = total + decode(r, i, s, b)
        return total

    def write(row, rows, value):
        out_ref[at, row : row + rows, :] = value

    encode(read, write, exps)


def ends_kernel(ends, before, after, w, acc_in, acc, far_ref, sides, exps):
    sides[0] = before[0]
    sides[1] = after[0]

    @pl.loop(0, (ends[3, 0] + 7) // 8)
    def _(part):
        for i in range(8):
            k = part * 8 + i
            at = ends[1, k]
            left = sides[ends[2, k]]
            acc[at] = acc[at] + jnp.dot(left, w[ends[0, k]], preferred_element_type=jnp.float32)

    @pl.loop(0, 8)
    def _(i):
        code_half(acc, 24 + i, [], exps, far_ref, i)


def add_ends(ends, before, after, w, acc):
    cells = acc.shape[2]
    smem = pl.BlockSpec(memory_space=pltpu.SMEM)
    vmem = pl.BlockSpec(memory_space=pltpu.VMEM)
    return pl.pallas_call(
        ends_kernel,
        out_shape=(
            jax.ShapeDtypeStruct(acc.shape, jnp.float32),
            jax.ShapeDtypeStruct((8, CODED, cells), jnp.int16),
        ),
        in_specs=[smem] + [vmem] * 4,
        out_specs=(vmem, vmem),
        scratch_shapes=[
            pltpu.VMEM((2,) + before.shape[1:], jnp.bfloat16),
            pltpu.VMEM((16, cells), jnp.float32),
        ],
        input_output_aliases={4: 0},
        compiler_params=pltpu.CompilerParams(vmem_limit_bytes=32 * MIB),
        cost_estimate=LITTLE,
    )(ends, before, after, w, acc)


def code_kernel(jobs, acc, *refs):
    arrays, outs, exps = refs[: -1 - len(jobs)], refs[-1 - len(jobs) : -1], refs[-1]
    for parts, out in zip(jobs, outs):
        for at, (unit, takes) in enumerate(parts):
            coded = [(arrays[a], i, scales(arrays[a], i)) for a, i in takes]
            code_half(acc, unit, coded, exps, out, at)


def code(acc, jobs, arrays):
    cells = acc.shape[2]
    vmem = pl.BlockSpec(memory_space=pltpu.VMEM)
    return pl.pallas_call(
        functools.partial(code_kernel, jobs),
        out_shape=tuple(
            jax.ShapeDtypeStruct((len(parts), CODED, cells), jnp.int16) for parts in jobs
        ),
        in_specs=[vmem] * (1 + len(arrays)),
        out_specs=(vmem,) * len(jobs),
        scratch_shapes=[pltpu.VMEM((16, cells), jnp.float32)],
        compiler_params=pltpu.CompilerParams(vmem_limit_bytes=32 * MIB),
        cost_estimate=LITTLE,
    )(acc, *arrays)


def code_near_kernel(acc, near_ref, exps):
    @pl.loop(0, 8)
    def _(i):
        code_half(acc, 16 + i, [], exps, near_ref, i)


def code_near(acc):
    cells = acc.shape[2]
    vmem = pl.BlockSpec(memory_space=pltpu.VMEM)
    return pl.pallas_call(
        code_near_kernel,
        out_shape=jax.ShapeDtypeStruct((8, CODED, cells), jnp.int16),
        in_specs=[vmem],
        out_specs=vmem,
        scratch_shapes=[pltpu.VMEM((16, cells), jnp.float32)],
        compiler_params=pltpu.CompilerParams(vmem_limit_bytes=32 * MIB),
        cost_estimate=LITTLE,
    )(acc)


def lift_kernel(index_ref, frac_ref, after, left):
    high = VARS * LEV
    row = lax.broadcasted_iota(jnp.int32, (high, ROWS), 0)
    col = lax.broadcasted_iota(jnp.int32, (high, ROWS), 1)
    level = row % LEV
    lift = jnp.zeros((high, ROWS), jnp.float32)
    for j in range(LEVT):
        at, frac = index_ref[j], frac_ref[j]
        here = jnp.where(level == at, 1.0 - frac, jnp.where(level == at + 1, frac, 0.0))
        lift = jnp.where(col % LEVT == j, here, lift)
    lift = jnp.where(row // LEV == col // LEVT, lift, 0.0)
    high_part = lift.astype(jnp.bfloat16)
    low_part = (lift - high_part.astype(jnp.float32)).astype(jnp.bfloat16)
    left[...] = jnp.concatenate([high_part, high_part, low_part, low_part], axis=1)


def lift_matrix(lev_index, lev_frac, after):
    smem = pl.BlockSpec(memory_space=pltpu.SMEM)
    vmem = pl.BlockSpec(memory_space=pltpu.VMEM)
    return pl.pallas_call(
        lift_kernel,
        out_shape=jax.ShapeDtypeStruct((VARS * LEV, 4 * ROWS), jnp.bfloat16),
        in_specs=[smem, smem, vmem],
        out_specs=vmem,
        compiler_params=pltpu.CompilerParams(vmem_limit_bytes=4 * MIB),
        cost_estimate=LITTLE,
    )(lev_index, lev_frac, after)


def finish_kernel(half, takes, left, acc, *refs):
    arrays, out_hbm, out, sems = refs[:-3], refs[-3], refs[-2], refs[-1]
    coded = [(arrays[a], i, scales(arrays[a], i)) for a, i in takes]
    copies = []
    for b in range(HALF):
        total = acc[half * HALF + b]
        for r, i, s in coded:
            total = total + decode(r, i, s, b)
        first = total.astype(jnp.bfloat16)
        second = (total - first.astype(jnp.float32)).astype(jnp.bfloat16)
        right = jnp.concatenate([first, second, first, second], axis=0)
        out[b] = jnp.dot(left[...], right, preferred_element_type=jnp.float32)
        if b % 4 == 3:
            copy = pltpu.make_async_copy(
                out.at[pl.ds(b - 3, 4)],
                out_hbm.at[pl.ds(half * HALF + b - 3, 4)],
                sems.at[b // 4],
            )
            copy.start()
            copies.append(copy)
    for copy in copies:
        copy.wait()


def finish(half, left, acc, takes, arrays, begun=None):
    cells = acc.shape[2]
    vmem = pl.BlockSpec(memory_space=pltpu.VMEM)
    hbm = pl.BlockSpec(memory_space=pltpu.HBM)
    extra = () if begun is None else (begun,)
    return pl.pallas_call(
        functools.partial(finish_kernel, half, takes),
        out_shape=jax.ShapeDtypeStruct((SB, VARS * LEV, cells), jnp.float32),
        in_specs=[vmem] * (2 + len(arrays)) + [hbm] * len(extra),
        out_specs=hbm,
        scratch_shapes=[
            pltpu.VMEM((HALF, VARS * LEV, cells), jnp.float32),
            pltpu.SemaphoreType.DMA((HALF // 4,)),
        ],
        input_output_aliases={2 + len(arrays): 0} if extra else {},
        compiler_params=pltpu.CompilerParams(vmem_limit_bytes=32 * MIB),
        cost_estimate=LITTLE,
    )(left, acc, *arrays, *extra)


def ring(peers):
    up = [(i, (i + 1) % peers) for i in range(peers)]
    return up, [(j, i) for i, j in up]


def swap(value, bits, peers):
    return lax.ppermute(value, "tile", [(i, i ^ bits) for i in range(peers)])


def staged(cotangent, weight, target_block, dest, source, count, lev_index, lev_frac):
    peers = 16
    me = lax.axis_index("tile").astype(jnp.int32).reshape(1)
    operands = (count, me, target_block, dest, source, cotangent, weight)
    up, down = ring(peers)
    before = lax.ppermute(cotangent[-1:], "tile", up)
    acc, w, cot, low = products_call(ahead_kernel, operands, (), cotangent[:1], MUCH)
    after = lax.ppermute(low, "tile", down)
    acc, w, cot, ends = products_call(rest_kernel, operands, (acc, w, cot), None, LITTLE)
    acc, far = add_ends(ends, before, after, w, acc)
    far = swap(far, 1, peers)
    near = swap(code_near(acc), 1, peers)
    y3 = code(acc, (((14, ((0, 6),)),), ((15, ((0, 7),)),)), (far,))
    y3_own = y3[0]
    y3 = [swap(v, 2, peers) for v in y3]
    y2 = code(acc, (((12, ((0, 4),)),), ((13, ((0, 5),)),)), (far, y3_own))
    y2_own = y2[0]
    y2 = [swap(v, 2, peers) for v in y2]
    (a3_low,) = code(acc, (((6, ((0, 6), (1, 0))),),), (near, y3[0], far))
    (a3_high,) = code(acc, (((7, ((0, 7), (1, 0))),),), (near, y3[1], a3_low))
    a3 = [swap(a3_low, 4, peers), swap(a3_high, 4, peers)]
    (y1_own,) = code(acc, (((10, ((0, 2),)), (11, ((0, 3),))),), (far, y3_own))
    o1 = swap(y1_own, 4, peers)
    (b2_low,) = code(acc, (((4, ((0, 4), (1, 0), (2, 0))),),), (near, y2[0], a3[0], a3_high))
    (b2_high,) = code(acc, (((5, ((0, 5), (1, 0), (2, 0))),),), (near, y2[1], a3[1], b2_low))
    b2 = [swap(b2_low, 8, peers), swap(b2_high, 8, peers)]
    y0_own = code(acc, (((8, ((0, 0), (1, 0))),), ((9, ((0, 1), (1, 1))),)), (far, o1, a3_high))
    y0 = [swap(v, 2, peers) for v in y0_own]
    y0_own = y0_own[0]
    (a1_own,) = code(acc, (((2, ((0, 2),)), (3, ((0, 3),))),), (near, a3_high))
    a1 = swap(a1_own, 4, peers)
    left = lift_matrix(lev_index, lev_frac, b2_high)
    out = finish(0, left, acc, ((0, 0), (1, 0), (2, 0), (3, 0)), (near, y0[0], a1, b2[0]))
    return finish(1, left, acc, ((0, 1), (1, 0), (2, 1), (3, 0)), (near, y0[1], a1, b2[1]), out)


def vertical_matrix(lev_index, lev_frac, levels):
    columns = jnp.arange(levels)[None, :]
    lower = (columns == lev_index[:, None]).astype(jnp.float32)
    upper = (columns == lev_index[:, None] + 1).astype(jnp.float32)
    return (1.0 - lev_frac)[:, None] * lower + lev_frac[:, None] * upper


def slotted(cotangent, weight, target_block, dest, source, count, lev_index, lev_frac):
    peers = lax.axis_size("tile")
    entries, _, cells = weight.shape
    capacity = max(2, 2 * entries // peers)
    slots = peers * capacity
    up, down = ring(peers)
    before = lax.ppermute(cotangent[-1:], "tile", up)
    after = lax.ppermute(cotangent[:1], "tile", down)
    window = jnp.concatenate([before, cotangent, after], axis=0)
    contrib = jnp.einsum(
        "ofp,ops->ofs", window[target_block[0]], weight, preferred_element_type=jnp.float32
    )
    live = jnp.arange(entries) < count[0]
    matches = ((dest[0][:, None] == jnp.arange(peers)[None, :]) & live[:, None]).astype(jnp.int32)
    rank = jnp.sum(matches * jnp.cumsum(matches, axis=0), axis=1) - 1
    slot = jnp.where(live, dest[0] * capacity + rank, slots)
    labels = jnp.full((slots,), SB, jnp.int32).at[slot].set(source[0], mode="drop")
    outgoing = jnp.zeros((slots, ROWS, cells), jnp.float32).at[slot].set(contrib, mode="drop")
    arrived = lax.all_to_all(outgoing, "tile", split_axis=0, concat_axis=0, tiled=True)
    arrived_labels = lax.all_to_all(labels, "tile", split_axis=0, concat_axis=0, tiled=True)
    chooser = (jnp.arange(SB)[:, None] == arrived_labels[None, :]).astype(jnp.float32)
    summed = jnp.einsum("br,rfs->bfs", chooser, arrived, precision=lax.Precision.HIGHEST)
    lifted = jnp.einsum(
        "jl,bvjs->bvls",
        vertical_matrix(lev_index, lev_frac, LEV),
        summed.reshape(SB, VARS, LEVT, cells),
        precision=lax.Precision.HIGHEST,
    )
    return lifted.reshape(SB, VARS * LEV, cells)


def solution(mesh):
    placed = (
        P(("grp", "tile"), None, None),
        P("tile", None, None),
        P("tile", None),
        P("tile", None),
        P("tile", None),
        P("tile"),
        P(),
        P(),
    )
    return jax.shard_map(
        staged if mesh.shape["tile"] == 16 else slotted,
        mesh=mesh,
        in_specs=placed,
        out_specs=P(("grp", "tile"), None, None),
        check_vma=False,
    )
```
